32 devices in a mesh: dp: 4 (over y, x), enc: 4 (over z), seq: 2 (over core).
Axes of the slice: x: 2, y: 2, z: 4, core: 2. Of those that a mesh axis runs over, the one named last changes fastest.
Arguments:
- queries: bfloat16 [4096, 1280], P(('dp', 'enc', 'seq')), may hold values from -6 to 6
- key_vectors: bfloat16 [4096, 1280], P(('dp', 'enc', 'seq')), may hold values from -6 to 6
- value_vectors: bfloat16 [4096, 1280], P(('dp', 'enc', 'seq')), may hold values from -6 to 6
- residual: bfloat16 [4096, 1280], P(('dp', 'enc', 'seq')), may hold values from -6 to 6
- out_weight: bfloat16 [1280, 1280], replicated, may hold values from -0.15625 to 0.15625
- cotangent: bfloat16 [4096, 1280], P(('dp', 'enc', 'seq')), may hold values from -0.09375 to 0.09375
- send_row: int32 [8192], P(('dp', 'enc', 'seq')), may hold values from 0 to 128, as said below
- image_id: int32 [4096], P(('dp', 'enc', 'seq')), may hold values from 0 to 127, as said below
Outputs:
- layer_out: bfloat16 [4096, 1280], P(('dp', 'enc', 'seq'))
- grad_weight: float32 [1280, 1280], P(('dp', 'seq'), 'enc')
The draws below stay inside these ranges and needn't reach their ends.
Inputs may be any that keep to these rules, and one draw needn't show every extreme that they name: `send_row`: in each device's block of 256 entries every local row 0 .. 127 appears exactly once and every other entry is 128; at most 64 rows go to one encoder device, and in every device's block some encoder device gets exactly 64. Rows with equal image_id lie in one encoder group (equal dp and seq indices) and are all sent to the same encoder device.
All inputs are finite; a program needn't handle non-finite values.
Results may differ from the reference program's by a relative error of at most 0.017.
Values may be sent and summed in bfloat16 or wider, within the bound.
No kernel may reach another device: no remote copies, remote signals or barrier semaphores. Data moves between devices by JAX's collectives and lax.ppermute only.
A program may use at most 64 MiB of HBM per device.

```python
import math
import jax
import jax.numpy as jnp
from jax import lax

D = 1280
HEADS = 16
HEAD_DIM = 80
ROW_DEV = 128
IMAGES_DEV = 4
CAP = 64
SLOTS = 256
ROWS = 4096
N_ENC = 4
N_SEQ = 2
DEVICES = 32


def route_plan(key, device):
    key = jax.random.fold_in(key, device)
    key_slots, key_full, key_rows, key_image, key_other = jax.random.split(key, 5)
    shuffled = jax.random.permutation(key_slots, SLOTS).astype(jnp.int32)
    enc_index = device // N_SEQ % N_ENC
    drawn_target = jax.random.randint(key_full, (), 0, N_ENC)
    full_target = jnp.where(enc_index == 0, N_ENC - 1, jnp.where(enc_index == 1, 0, drawn_target))
    target_of = shuffled // CAP
    ranking = jnp.where(target_of == full_target, shuffled - SLOTS, shuffled)
    ordering = jnp.argsort(ranking, stable=True)
    chosen = shuffled[ordering][:ROW_DEV]
    row_order = jax.random.permutation(key_rows, ROW_DEV).astype(jnp.int32)
    sending = jnp.full((SLOTS,), ROW_DEV, jnp.int32).at[chosen].set(row_order)
    row_target = jnp.zeros((ROW_DEV,), jnp.int32).at[row_order].set(chosen // CAP)
    first_pick = jax.random.randint(key_image, (ROW_DEV,), 0, IMAGES_DEV)
    second_pick = jax.random.randint(key_other, (ROW_DEV,), 0, IMAGES_DEV)
    picked = jnp.minimum(first_pick, second_pick)
    picked = picked.at[row_order[0]].set(IMAGES_DEV - 1)
    picked = picked.at[row_order[1]].set(0)
    group = device // (N_ENC * N_SEQ) * N_SEQ + device % N_SEQ
    images = ((group * N_ENC + row_target) * IMAGES_DEV + picked).astype(jnp.int32)
    return (sending, images)


def all_plans(key):
    devices_range = jnp.arange(DEVICES).astype(jnp.int32)
    return jax.vmap(lambda device: route_plan(key, device))(devices_range)


def draw_send_row(key, part):
    sending, images = all_plans(key)
    return sending.reshape(-1)


def draw_image_id(key, part):
    sending, images = all_plans(key)
    return images.reshape(-1)


def draw_queries(key, part):
    key = jax.random.fold_in(key, 21)
    base = jnp.clip(jax.random.normal(key, (ROWS, D), jnp.float32), -6.0, 6.0)
    return base.astype(jnp.bfloat16)


def draw_key_vectors(key, part):
    key = jax.random.fold_in(key, 22)
    base = jnp.clip(jax.random.normal(key, (ROWS, D), jnp.float32), -6.0, 6.0)
    return base.astype(jnp.bfloat16)


def shard_levels(stream_key, shape, cuts, low, high):
    level = 1.0
    for dim, blocks in cuts:
        draws = jax.random.uniform(jax.random.fold_in(jax.random.fold_in(stream_key, 6), dim), (blocks,), jnp.float32, low / len(cuts), high / len(cuts))
        level = level * jnp.repeat(jnp.exp(draws), shape[dim] // blocks).reshape((-1,) + (1,) * (len(shape) - 1 - dim))
    return level


def bell_draw(own_key, shape, width, limit, cuts=(), kind=jnp.bfloat16):
    level = shard_levels(own_key, shape, cuts, -0.22, 0.18) if cuts else 1.0
    entries = jax.random.normal(own_key, shape, jnp.float32) * width * level
    return jnp.minimum(jnp.maximum(entries, -limit), limit).astype(kind)


def setup_inputs(seed: int = 0) -> dict:
    keys = jax.random.split(jax.random.key(seed), 9)
    queries = draw_queries(jax.random.fold_in(keys[8], 71), 0)
    key_vectors = draw_key_vectors(jax.random.fold_in(keys[8], 71), 0)
    value_vectors = bell_draw(keys[2], (ROWS, D), 1.0, 6.0, ((0, 32),))
    residual = bell_draw(keys[3], (ROWS, D), 1.0, 6.0, ((0, 32),))
    out_weight = bell_draw(keys[4], (D, D), D ** -0.5, 0.15625)
    cotangent = bell_draw(keys[5], (ROWS, D), ROWS ** -0.5, 0.09375, ((0, 32),))
    send_row = draw_send_row(jax.random.fold_in(keys[8], 71), 0)
    image_id = draw_image_id(jax.random.fold_in(keys[8], 71), 0)
    return dict(queries=queries, key_vectors=key_vectors, value_vectors=value_vectors, residual=residual, out_weight=out_weight, cotangent=cotangent, send_row=send_row, image_id=image_id)


def attend_rows(query_rows, key_rows, value_rows, image_ids):
    count = query_rows.shape[0]
    shaped_query = query_rows.astype(jnp.float32).reshape(count, HEADS, HEAD_DIM)
    shaped_key = key_rows.astype(jnp.float32).reshape(count, HEADS, HEAD_DIM)
    shaped_value = value_rows.astype(jnp.float32).reshape(count, HEADS, HEAD_DIM)
    scale = 1.0 / math.sqrt(HEAD_DIM)
    scores = jnp.einsum('qhd,khd->hqk', shaped_query, shaped_key) * scale
    same_image = image_ids[:, None] == image_ids[None, :]
    scores = jnp.where(same_image[None], scores, -1e+30)
    highest = lax.optimization_barrier(jnp.max(scores, axis=-1, keepdims=True))
    weights = jnp.exp(scores - highest)
    probs = (weights / lax.optimization_barrier(jnp.sum(weights, axis=-1, keepdims=True))).astype(jnp.bfloat16)
    mixed = jnp.einsum('hqk,khd->qhd', probs.astype(jnp.float32), shaped_value)
    return mixed.reshape(count, HEADS * HEAD_DIM).astype(jnp.bfloat16)

def reference(queries, key_vectors, value_vectors, residual, out_weight, cotangent, send_row, image_id):
    group_count = DEVICES // N_ENC
    pair_total = group_count * N_ENC

    def one_pair(pair, attended):
        group = pair // N_ENC
        target = pair % N_ENC
        dp_index = group // N_SEQ
        seq_index = group % N_SEQ
        sources = ((dp_index * N_ENC + jnp.arange(N_ENC).astype(jnp.int32)) * N_SEQ + seq_index).astype(jnp.int32)
        slot_index = (sources[:, None] * SLOTS + target * CAP + jnp.arange(CAP).astype(jnp.int32)[None, :]).reshape(-1).astype(jnp.int32)
        local_row = send_row[slot_index]
        is_live = local_row < ROW_DEV
        global_row = (jnp.repeat(sources, CAP) * ROW_DEV + jnp.minimum(local_row, ROW_DEV - 1)).astype(jnp.int32)
        zero = jnp.zeros((), jnp.bfloat16)
        query_rows = jnp.where(is_live[:, None], queries[global_row], zero)
        key_rows = jnp.where(is_live[:, None], key_vectors[global_row], zero)
        value_rows = jnp.where(is_live[:, None], value_vectors[global_row], zero)
        image_ids = jnp.where(is_live, image_id[global_row], -1 - jnp.arange(SLOTS).astype(jnp.int32))
        output = attend_rows(query_rows, key_rows, value_rows, image_ids)
        destination = jnp.where(is_live, global_row, ROWS).astype(jnp.int32)
        return attended.at[destination].set(output, mode='drop')
    attended = lax.fori_loop(0, pair_total, one_pair, jnp.zeros((ROWS, D), jnp.bfloat16))
    projected = jnp.dot(attended, out_weight, preferred_element_type=jnp.float32)
    layer_out = (residual.astype(jnp.float32) + projected).astype(jnp.bfloat16)

    def add_device(device, total):
        block = lax.dynamic_slice_in_dim(attended, device * ROW_DEV, ROW_DEV, 0)
        cot_block = lax.dynamic_slice_in_dim(cotangent, device * ROW_DEV, ROW_DEV, 0)
        term = lax.dot_general(block, cot_block, (((0,), (0,)), ((), ())), preferred_element_type=jnp.float32)
        return total + term.astype(jnp.bfloat16).astype(jnp.float32)
    grad_weight = lax.fori_loop(0, DEVICES, add_device, jnp.zeros((D, D), jnp.float32))
    return (layer_out, grad_weight)
```

```python
import functools
import math

import jax
import jax.numpy as jnp
from jax import lax
from jax.experimental import pallas as pl
from jax.experimental.pallas import tpu as pltpu
from jax.sharding import PartitionSpec as P

HEADS = 16
AXES = ("dp", "enc", "seq")
ID_ROWS = 16
ID_BASE = 64


def call(
    kernel,
    out_shape,
    *args,
    spaces=None,
    out_spaces=None,
    aliases=None,
    scratch=(),
    limit=16,
    flops=0,
    bytes_accessed=0,
):
    def placed(space):
        return pl.BlockSpec(memory_space=space)

    many = isinstance(out_shape, (list, tuple))
    spaces = spaces or [pltpu.VMEM] * len(args)
    args = [
        pltpu.with_memory_space_constraint(arg, pltpu.HBM) if space == pltpu.HBM else arg
        for arg, space in zip(args, spaces)
    ]
    return pl.pallas_call(
        kernel,
        out_shape=out_shape,
        in_specs=[placed(space) for space in spaces],
        out_specs=[placed(space) for space in out_spaces or [pltpu.VMEM] * len(out_shape)]
        if many
        else placed(pltpu.VMEM),
        input_output_aliases=aliases or {},
        scratch_shapes=list(scratch),
        compiler_params=pltpu.CompilerParams(vmem_limit_bytes=limit * 1024 * 1024),
        cost_estimate=pl.CostEstimate(
            flops=flops, bytes_accessed=bytes_accessed, transcendentals=0
        ),
    )(*args)


def pack_kernel(count, half, *refs):
    sources, own, cross = refs[:5], refs[5 : 5 + count], refs[5 + count : 5 + 2 * count]
    ready, held, arrived, ids_held, sems = refs[5 + 2 * count :]
    targets = [ids_held] + [arrived.at[which] for which in range(3)] + [ready]
    copies = [
        pltpu.make_async_copy(source, target, sems.at[which])
        for which, (source, target) in enumerate(zip(sources, targets))
    ]
    for copy in copies:
        copy.start()
    e, s = lax.axis_index("enc"), lax.axis_index("seq")
    copies[0].wait()
    ids = ids_held[...]
    row = lax.broadcasted_iota(jnp.int32, (ID_ROWS, ids.shape[1]), 0)
    digits = jnp.where(row == 0, ids // ID_BASE, jnp.where(row == 1, ids % ID_BASE, 0))
    digits = digits.astype(jnp.float32).astype(jnp.bfloat16)
    for out in own + cross:
        out[3 * half :] = digits
    for which in range(3):
        copies[1 + which].wait()
        held[...] = arrived[which].T
        span = slice(which * half, (which + 1) * half)
        for step in range(count):
            block = (e ^ step) * 2
            own[step][span] = held[pl.ds(pl.multiple_of((block + s) * half, 16), half)]
            cross[step][span] = held[pl.ds(pl.multiple_of((block + 1 - s) * half, 16), half)]
    copies[4].wait()


def attend(slabs, outs, bias, half, head_width, base=0):
    count, rows = len(slabs), slabs[0].shape[1]
    numbers = []
    for slab in slabs:
        digits = slab[3 * half : 3 * half + ID_ROWS].astype(jnp.float32)
        numbers.append(digits[0:1] * ID_BASE + digits[1:2])
    query_ids = jnp.concatenate(numbers, axis=1)
    for index in range(count):
        column = jnp.broadcast_to(numbers[index], (rows, rows)).T
        column = jnp.concatenate([column] * count, axis=1)
        bias[index * rows : (index + 1) * rows] = jnp.where(column == query_ids, 0.0, -1e30)
    factor = math.log2(math.e) / math.sqrt(head_width)
    span = 2 * rows

    def part(which, head):
        begin = which * half + head * head_width
        return jnp.concatenate([slab[begin : begin + head_width] for slab in slabs], axis=1)

    for head in range(half // head_width):
        query, key, value = part(0, head), part(1, head), part(2, head)
        for first in range(0, count * rows, span):
            scores = lax.dot_general(
                key,
                query[:, first : first + span],
                (((0,), (0,)), ((), ())),
                preferred_element_type=jnp.float32,
            )
            scores = scores + bias[:, first : first + span]
            highest = jnp.max(scores, axis=0, keepdims=True)
            weights = jnp.exp2((scores - highest) * factor)
            total = jnp.sum(weights, axis=0, keepdims=True)
            mixed = jnp.dot(
                value, weights.astype(jnp.bfloat16), preferred_element_type=jnp.float32
            )
            mixed = (mixed / total).astype(jnp.bfloat16)
            for index in range(first // rows, (first + span) // rows):
                at = index * rows - first
                outs[index][head * head_width : (head + 1) * head_width, base : base + rows] = mixed[
                    :, at : at + rows
                ]


def attend_own_kernel(count, half, head_width, *refs):
    slabs, beside, outs = refs[:count], refs[count], refs[-3 - count : -3]
    late, bias, sem = refs[-3:]
    copy = pltpu.make_async_copy(beside, late, sem)
    copy.start()
    attend(slabs, outs, bias, half, head_width)
    copy.wait()


def attend_cross_kernel(count, half, head_width, *refs):
    slabs, own, sources = refs[:count], refs[count : 2 * count], refs[2 * count : 3 * count - 1]
    outs, (stacked, bias, sems) = refs[3 * count - 1 : -3], refs[-3:]
    copies = [
        pltpu.make_async_copy(source, stacked.at[index], sems.at[index])
        for index, source in enumerate(sources)
    ]
    for copy in copies:
        copy.start()
    rows = slabs[0].shape[1]
    for mine, out in zip(own, outs):
        out[:, :rows] = mine[...]
    attend(slabs, outs, bias, half, head_width, rows)
    for copy in copies:
        copy.wait()


def order_kernel(count, *refs):
    pieces, outs, (given, held) = refs[:count], refs[count + 2 : 2 * count + 2], refs[-2:]
    d, e = lax.axis_index("dp"), lax.axis_index("enc")
    rows = given.shape[2]
    for step, piece in enumerate(pieces):
        held[step] = piece[...]
        given[step] = piece[:, rows:]
    for step, out in enumerate(outs):
        out[...] = held[d ^ e ^ step]


def project_kernel(count, *refs):
    pieces, (given, residual, weight, out, attended) = refs[:count], refs[count:]
    e, s = lax.axis_index("enc"), lax.axis_index("seq")
    half, rows = given.shape[1:]
    for step, piece in enumerate(pieces):
        for which, source in ((s, piece[:, :rows]), (1 - s, given[step])):
            begin = pl.multiple_of((2 * (e ^ step) + which) * half, 16)
            attended[pl.ds(begin, half)] = source
    projected = lax.dot_general(
        attended[...], weight[...], (((0,), (0,)), ((), ())), preferred_element_type=jnp.float32
    )
    out[...] = (residual[...].astype(jnp.float32) + projected).astype(jnp.bfloat16)


def gradient_kernel(count, *refs):
    pieces, (same, last, others, last_other) = refs[:count], refs[count : count + 4]
    own, *outs = refs[count + 4 :]
    e = lax.axis_index("enc")
    rows = []
    for step in range(count - 1):
        rows += [same[step], others[step]]
    rows += [last[...], last_other[...]]
    total = jnp.dot(
        jnp.concatenate([piece[...] for piece in pieces], axis=1),
        jnp.concatenate(rows, axis=0),
        preferred_element_type=jnp.float32,
    )
    width, short = total.shape[1] // count, total.shape[0] // 2
    for target in range(count):
        block = total[:, target * width : (target + 1) * width]
        folded = jnp.concatenate([block[:short], block[short:]], axis=1).astype(jnp.bfloat16)

        @pl.when(e == target)
        def _():
            own[...] = block

        for index, out in enumerate(outs):

            @pl.when(e ^ target == index + 1)
            def _():
                out[...] = folded


def add_kernel(own, *refs):
    out, width = refs[-1], own.shape[1]
    total = refs[0][...].astype(jnp.float32)
    for ref in refs[1:-1]:
        total = total + ref[...].astype(jnp.float32)
    short = total.shape[0]
    out[:short] = own[:short] + total[:, :width]
    out[short:] = own[short:] + total[:, width:]


def exchange_body(
    sizes, queries, key_vectors, value_vectors, residual, out_weight, cotangent, send_row, image_id
):
    n_dp, n_enc, n_seq = sizes
    rows, width = queries.shape
    block = width // n_enc
    half = block // n_seq
    head_width = width // HEADS
    group = n_enc * rows
    tall = 3 * half + ID_ROWS
    bf16 = functools.partial(jax.ShapeDtypeStruct, dtype=jnp.bfloat16)
    hbm = pltpu.HBM

    hops = range(n_enc - 1, 0, -1)

    def move(data, partner):
        pairs = []
        for d in range(n_dp):
            for e in range(n_enc):
                for s in range(n_seq):
                    to_d, to_e, to_s = partner(d, e, s)
                    pairs.append(
                        ((d * n_enc + e) * n_seq + s, (to_d * n_enc + to_e) * n_seq + to_s)
                    )
        return lax.ppermute(data, AXES, pairs)

    def along_enc(pieces, flip=0):
        moved = {k: move(pieces[k], lambda d, e, s: (d, e ^ k, s ^ flip)) for k in hops}
        if 0 in pieces:
            moved[0] = move(pieces[0], lambda d, e, s: (d, e, s ^ flip)) if flip else pieces[0]
        return [moved[k] for k in sorted(moved)]

    def along_seq(data):
        return move(data, lambda d, e, s: (d, e, s ^ 1))

    with jax.named_scope("pack"):
        outs = call(
            functools.partial(pack_kernel, n_enc, half),
            [bf16((tall, rows))] * (2 * n_enc) + [bf16((rows, width))],
            image_id.reshape(1, rows),
            queries,
            key_vectors,
            value_vectors,
            cotangent,
            spaces=[hbm] * 5,
            scratch=[
                pltpu.VMEM((width, rows), jnp.bfloat16),
                pltpu.VMEM((3, rows, width), jnp.bfloat16),
                pltpu.VMEM((1, rows), jnp.int32),
                pltpu.SemaphoreType.DMA((5,)),
            ],
            bytes_accessed=8 * rows * width * 2,
        )
        own, cross = dict(enumerate(outs[:n_enc])), dict(enumerate(outs[n_enc:-1]))
        cotangent = outs[-1]
    with jax.named_scope("exchange_own"):
        own = along_enc(own)
    with jax.named_scope("exchange_cross"):
        cross = along_enc(cross, 1)
    with jax.named_scope("gather_cotangent"):
        beside = move(cotangent, lambda d, e, s: (d ^ 1, e, s))
        above = move(cotangent, lambda d, e, s: (d ^ 2, e, s))
    cost = dict(flops=4 * group * group * half, bytes_accessed=4 * group * half * 2)
    bias = pltpu.VMEM((group, group), jnp.float32)
    with jax.named_scope("attend_own"):
        *own, late = call(
            functools.partial(attend_own_kernel, n_enc, half, head_width),
            [bf16((half, rows))] * n_enc + [bf16((rows, width))],
            *own,
            beside,
            *cross,
            spaces=[pltpu.VMEM] * (n_enc + 1) + [pl.ANY] * n_enc,
            scratch=[bias, pltpu.SemaphoreType.DMA],
            **cost,
        )
    with jax.named_scope("gather_cotangent"):
        last = move(late, lambda d, e, s: (d ^ 2, e, s))
    with jax.named_scope("attend_cross"):
        *pieces, stacked = call(
            functools.partial(attend_cross_kernel, n_enc, half, head_width),
            [bf16((half, 2 * rows))] * n_enc + [bf16((n_dp - 1, rows, width))],
            *cross,
            *own,
            cotangent,
            beside,
            above,
            scratch=[bias, pltpu.SemaphoreType.DMA((n_dp - 1,))],
            **cost,
        )
    with jax.named_scope("return_heads"):
        pieces = along_enc(dict(enumerate(pieces)))
    with jax.named_scope("exchange_features"):
        *features, stacked, last, given = call(
            functools.partial(order_kernel, n_enc),
            [bf16((half, 2 * rows))] * n_dp
            + [bf16((n_dp - 1, rows, width)), bf16((rows, width)), bf16((n_enc, half, rows))],
            *pieces,
            stacked,
            last,
            spaces=[pltpu.VMEM] * n_enc + [pl.ANY] * 2,
            out_spaces=[pltpu.VMEM] * n_dp + [pl.ANY] * 2 + [pltpu.VMEM],
            aliases={n_enc: n_dp, n_enc + 1: n_dp + 1},
            scratch=[pltpu.VMEM((n_enc, half, 2 * rows), jnp.bfloat16)],
        )
        features = [features[0]] + [
            move(features[k], lambda d, e, s, k=k: (d ^ k, e, s)) for k in range(1, n_dp)
        ]
    with jax.named_scope("gradient"):
        mine, *partial = call(
            functools.partial(gradient_kernel, n_enc),
            [jax.ShapeDtypeStruct((half, block), jnp.float32)]
            + [bf16((half // 2, 2 * block))] * (n_enc - 1),
            *features,
            stacked,
            last,
            along_seq(stacked),
            along_seq(last),
            flops=2 * half * width * rows * n_dp * n_seq,
            bytes_accessed=2 * n_dp * n_seq * rows * width,
        )
    with jax.named_scope("sum_gradient"):
        partial = along_enc({k + 1: part for k, part in enumerate(partial)})
    with jax.named_scope("project"):
        layer_out = call(
            functools.partial(project_kernel, n_enc),
            bf16((rows, width)),
            *pieces,
            along_seq(given),
            residual,
            out_weight,
            scratch=[pltpu.VMEM((width, rows), jnp.bfloat16)],
            flops=2 * rows * width * width,
            bytes_accessed=2 * width * width,
        )
    with jax.named_scope("add_gradient"):
        grad_weight = call(
            add_kernel,
            jax.ShapeDtypeStruct((half, block), jnp.float32),
            mine,
            *partial,
            bytes_accessed=4 * half * block * 4,
        )
    return (layer_out, grad_weight)


def attend_groups(query_group, key_group, value_group, image_ids):
    items, slot_count, group_width = query_group.shape
    group_heads = HEADS // 2
    head_width = group_width // group_heads
    scale = 1.0 / math.sqrt(head_width)
    position = jnp.arange(slot_count)
    image_ids = jnp.where(image_ids < 0, -1 - position[None, :], image_ids)
    shaped_query = query_group.reshape(items, slot_count, group_heads, head_width)
    shaped_key = key_group.reshape(items, slot_count, group_heads, head_width)
    shaped_value = value_group.reshape(items, slot_count, group_heads, head_width)
    scores = (
        jnp.einsum("gqhd,gkhd->ghqk", shaped_query, shaped_key, preferred_element_type=jnp.float32)
        * scale
    )
    same_image = image_ids[:, None, :, None] == image_ids[:, None, None, :]
    scores = jnp.where(same_image, scores, -1e30)
    highest = jnp.max(scores, axis=-1, keepdims=True)
    weights = jnp.exp(scores - highest)
    probs = (weights / jnp.sum(weights, axis=-1, keepdims=True)).astype(jnp.bfloat16)
    mixed = jnp.einsum("ghqk,gkhd->gqhd", probs, shaped_value, preferred_element_type=jnp.float32)
    return mixed.reshape(items, slot_count, group_width).astype(jnp.bfloat16)


def routed_body(
    queries, key_vectors, value_vectors, residual, out_weight, cotangent, send_row, image_id
):
    row_count, full_width = queries.shape
    half_width = full_width // 2
    is_live = send_row < row_count
    source_row = jnp.minimum(send_row, row_count - 1)

    def arrange(data):
        grouped = data.reshape(row_count, 2, half_width).transpose(1, 0, 2)
        return jnp.where(is_live[None, :, None], grouped[:, source_row], jnp.zeros((), data.dtype))

    send_query = arrange(queries)
    send_key = arrange(key_vectors)
    send_value = arrange(value_vectors)
    send_image = jnp.where(is_live, image_id[source_row], -1)
    send_image = jnp.broadcast_to(send_image[None, :], (2, send_row.shape[0]))
    received = (
        lax.all_to_all(send_query, "enc", split_axis=1, concat_axis=1, tiled=True),
        lax.all_to_all(send_key, "enc", split_axis=1, concat_axis=1, tiled=True),
        lax.all_to_all(send_value, "enc", split_axis=1, concat_axis=1, tiled=True),
        lax.all_to_all(send_image, "enc", split_axis=1, concat_axis=1, tiled=True),
    )
    output = attend_groups(received[0], received[1], received[2], received[3])
    returned = lax.all_to_all(output, "enc", split_axis=1, concat_axis=1, tiled=True)
    holder = jnp.zeros((2, row_count + 1, half_width), jnp.bfloat16).at[:, send_row].set(returned)
    attended = holder[:, :row_count].transpose(1, 0, 2).reshape(row_count, full_width)
    projected = jnp.dot(attended, out_weight, preferred_element_type=jnp.float32)
    layer_out = (residual.astype(jnp.float32) + projected).astype(jnp.bfloat16)
    first_sum = lax.psum_scatter(
        lax.dot_general(
            attended, cotangent, (((0,), (0,)), ((), ())), preferred_element_type=jnp.float32
        ).astype(jnp.bfloat16),
        "dp",
        scatter_dimension=0,
        tiled=True,
    )
    second_sum = lax.psum_scatter(first_sum, "seq", scatter_dimension=0, tiled=True).astype(
        jnp.float32
    )
    grad_weight = lax.psum_scatter(second_sum, "enc", scatter_dimension=1, tiled=True)
    return (layer_out, grad_weight)


def solution(mesh):
    sizes = tuple(mesh.shape[name] for name in AXES)
    n_dp, n_enc, n_seq = sizes
    fits = n_seq == 2 and n_dp == n_enc == 4 and HEADS % (2 * n_enc) == 0
    body = functools.partial(exchange_body, sizes) if fits else routed_body
    placed = (
        P(("dp", "enc", "seq"), None),
        P(("dp", "enc", "seq"), None),
        P(("dp", "enc", "seq"), None),
        P(("dp", "enc", "seq"), None),
        P(),
        P(("dp", "enc", "seq"), None),
        P(("dp", "enc", "seq")),
        P(("dp", "enc", "seq")),
    )
    return jax.shard_map(
        body,
        mesh=mesh,
        in_specs=placed,
        out_specs=(P(("dp", "enc", "seq"), None), P(("dp", "seq"), "enc")),
        check_vma=False,
    )
```

```python
import functools
import math

import jax
import jax.numpy as jnp
from jax import lax
from jax.experimental import pallas as pl
from jax.experimental.pallas import tpu as pltpu
from jax.sharding import PartitionSpec as P

HEADS = 16
AXES = ("dp", "enc", "seq")
ID_ROWS = 16
ID_BASE = 64
SENDS = (3, 2, 1, 0)
RETURNS = (3, 2, 1, 0)
SUMS = (3, 2, 1, 0)


def call(
    kernel,
    out_shape,
    *args,
    spaces=None,
    scratch=(),
    limit=16,
    flops=0,
    bytes_accessed=0,
):
    def placed(space):
        return pl.BlockSpec(memory_space=space)

    many = isinstance(out_shape, (list, tuple))
    spaces = spaces or [pltpu.VMEM] * len(args)
    args = [
        pltpu.with_memory_space_constraint(arg, pltpu.HBM) if space == pltpu.HBM else arg
        for arg, space in zip(args, spaces)
    ]
    return pl.pallas_call(
        kernel,
        out_shape=out_shape,
        in_specs=[placed(space) for space in spaces],
        out_specs=[placed(pltpu.VMEM)] * len(out_shape) if many else placed(pltpu.VMEM),
        scratch_shapes=list(scratch),
        compiler_params=pltpu.CompilerParams(vmem_limit_bytes=limit * 1024 * 1024),
        cost_estimate=pl.CostEstimate(
            flops=flops, bytes_accessed=bytes_accessed, transcendentals=0
        ),
    )(*args)


def pack_kernel(block, *refs):
    sources, outs, (ready, held, arrived, ids_held, sems) = refs[:5], refs[5:-5], refs[-5:]
    targets = [ids_held] + [arrived.at[which] for which in range(3)] + [ready]
    copies = [
        pltpu.make_async_copy(source, target, sems.at[which])
        for which, (source, target) in enumerate(zip(sources, targets))
    ]
    for copy in copies:
        copy.start()
    first = lax.axis_index("dp") ^ lax.axis_index("enc")
    copies[0].wait()
    ids = ids_held[...]
    row = lax.broadcasted_iota(jnp.int32, (ID_ROWS, ids.shape[1]), 0)
    digits = jnp.where(row == 0, ids // ID_BASE, jnp.where(row == 1, ids % ID_BASE, 0))
    digits = digits.astype(jnp.float32).astype(jnp.bfloat16)
    for out in outs:
        out[3 * block :] = digits
    for which in range(3):
        copies[1 + which].wait()
        held[...] = arrived[which].T
        for hop, out in zip(SENDS, outs):
            begin = pl.multiple_of((first ^ hop) * block, 16)
            out[which * block : (which + 1) * block] = held[pl.ds(begin, block)]
    copies[4].wait()


def attend_kernel(count, block, head_width, *refs):
    slabs, outs, bias = refs[:count], refs[count : 2 * count], refs[2 * count]
    rows = slabs[0].shape[1]
    numbers = []
    for slab in slabs:
        digits = slab[3 * block : 3 * block + ID_ROWS].astype(jnp.float32)
        numbers.append(digits[0:1] * ID_BASE + digits[1:2])
    query_ids = jnp.concatenate(numbers, axis=1)
    for index in range(count):
        column = jnp.broadcast_to(numbers[index], (rows, rows)).T
        column = jnp.concatenate([column] * count, axis=1)
        bias[index * rows : (index + 1) * rows] = jnp.where(column == query_ids, 0.0, -1e30)
    factor = math.log2(math.e) / math.sqrt(head_width)
    span = 2 * rows

    def part(which, head):
        begin = which * block + head * head_width
        return jnp.concatenate([slab[begin : begin + head_width] for slab in slabs], axis=1)

    for head in range(block // head_width):
        query, key, value = part(0, head), part(1, head), part(2, head)
        for first in range(0, count * rows, span):
            scores = lax.dot_general(
                key,
                query[:, first : first + span],
                (((0,), (0,)), ((), ())),
                preferred_element_type=jnp.float32,
            )
            scores = scores + bias[:, first : first + span]
            highest = jnp.max(scores, axis=0, keepdims=True)
            weights = jnp.exp2((scores - highest) * factor)
            total = jnp.sum(weights, axis=0, keepdims=True)
            mixed = jnp.dot(
                value, weights.astype(jnp.bfloat16), preferred_element_type=jnp.float32
            )
            mixed = (mixed / total).astype(jnp.bfloat16)
            for index in range(first // rows, (first + span) // rows):
                at = index * rows - first
                out = outs[RETURNS.index(SENDS[index])]
                out[head * head_width : (head + 1) * head_width] = mixed[:, at : at + rows]


def stack_kernel(count, *refs):
    sources, out, sems = refs[:count], refs[-2], refs[-1]
    copies = [
        pltpu.make_async_copy(source, out.at[index], sems.at[index])
        for index, source in enumerate(sources)
    ]
    for copy in copies:
        copy.start()
    for copy in copies:
        copy.wait()


def halve_kernel(*refs):
    pieces, (kept, given) = refs[:-2], refs[-2:]
    s = lax.axis_index("seq")
    half = kept.shape[1]
    for hop, piece in zip(RETURNS, pieces):
        kept[hop] = piece[pl.ds(pl.multiple_of(s * half, 16), half)]
        given[hop] = piece[pl.ds(pl.multiple_of((1 - s) * half, 16), half)]


def gradient_kernel(count, *refs):
    kept, given, same, others, *outs = refs
    e = lax.axis_index("enc")
    features, rows = [], []
    for step in range(count):
        features += [kept[step], given[step]]
        rows += [same[step], others[step]]
    total = jnp.dot(
        jnp.concatenate(features, axis=1),
        jnp.concatenate(rows, axis=0),
        preferred_element_type=jnp.float32,
    )
    width, short = total.shape[1] // count, total.shape[0] // 2
    for target in range(count):
        block = total[:, target * width : (target + 1) * width]
        folded = jnp.concatenate([block[:short], block[short:]], axis=1).astype(jnp.bfloat16)

        for index, out in enumerate(outs):

            @pl.when(e ^ target == SUMS[index])
            def _():
                out[...] = folded


def project(pieces, steps, weight, attended):
    first = lax.axis_index("dp") ^ lax.axis_index("enc")
    block = pieces[0].shape[0]
    rows = []
    for index, (step, piece) in enumerate(zip(steps, pieces)):
        attended[index * block : (index + 1) * block] = piece[...]
        rows.append(weight[pl.ds(pl.multiple_of((first ^ step) * block, 16), block)])
    return lax.dot_general(
        attended[...],
        jnp.concatenate(rows, axis=0),
        (((0,), (0,)), ((), ())),
        preferred_element_type=jnp.float32,
    )


def project_kernel(residual, weight, *refs):
    pieces, (out, attended) = refs[:-2], refs[-2:]
    out[...] = residual[...].astype(jnp.float32) + project(
        pieces, range(len(pieces)), weight, attended
    )


def finish_kernel(count, early, *refs):
    partial, pieces = refs[:count], refs[count : 2 * count - early]
    projected, weight, out, grad, attended = refs[2 * count - early :]
    total = partial[0][...].astype(jnp.float32)
    for ref in partial[1:]:
        total = total + ref[...].astype(jnp.float32)
    short, width = total.shape[0], grad.shape[1]
    grad[:short] = total[:, :width]
    grad[short:] = total[:, width:]
    projected = projected[...] + project(pieces, range(early, count), weight, attended)
    out[...] = projected.astype(jnp.bfloat16)


def exchange_body(
    sizes, queries, key_vectors, value_vectors, residual, out_weight, cotangent, send_row, image_id
):
    n_dp, n_enc, n_seq = sizes
    rows, width = queries.shape
    block = width // n_enc
    half = block // n_seq
    head_width = width // HEADS
    group = n_enc * rows
    tall = 3 * block + ID_ROWS
    bf16 = functools.partial(jax.ShapeDtypeStruct, dtype=jnp.bfloat16)
    hbm = pltpu.HBM

    def move(data, partner):
        pairs = []
        for d in range(n_dp):
            for e in range(n_enc):
                for s in range(n_seq):
                    to_d, to_e, to_s = partner(d, e, s)
                    pairs.append(
                        ((d * n_enc + e) * n_seq + s, (to_d * n_enc + to_e) * n_seq + to_s)
                    )
        return lax.ppermute(data, AXES, pairs)

    def along_enc(pieces, hops):
        return [
            move(piece, lambda d, e, s, hop=hop: (d, e ^ hop, s)) if hop else piece
            for hop, piece in zip(hops, pieces)
        ]

    def along_seq(data):
        return move(data, lambda d, e, s: (d, e, s ^ 1))

    with jax.named_scope("pack"):
        outs = call(
            functools.partial(pack_kernel, block),
            [bf16((tall, rows))] * n_enc + [bf16((rows, width))],
            image_id.reshape(1, rows),
            queries,
            key_vectors,
            value_vectors,
            cotangent,
            spaces=[hbm] * 5,
            scratch=[
                pltpu.VMEM((width, rows), jnp.bfloat16),
                pltpu.VMEM((3, rows, width), jnp.bfloat16),
                pltpu.VMEM((1, rows), jnp.int32),
                pltpu.SemaphoreType.DMA((5,)),
            ],
            bytes_accessed=8 * rows * width * 2,
        )
        slabs, cotangent = outs[:-1], outs[-1]
    with jax.named_scope("exchange_heads"):
        slabs = along_enc(slabs, SENDS)
    with jax.named_scope("gather_cotangent"):
        same = [cotangent] + [
            move(cotangent, lambda d, e, s, k=k: (d ^ k, e, s)) for k in range(1, n_dp)
        ]
    with jax.named_scope("attention"):
        pieces = call(
            functools.partial(attend_kernel, n_enc, block, head_width),
            [bf16((block, rows))] * n_enc,
            *slabs,
            scratch=[pltpu.VMEM((group, group), jnp.float32)],
            flops=55 * group * group * block,
            bytes_accessed=8 * group * block,
        )
    with jax.named_scope("send_to_owner"):
        pieces = [
            move(piece, lambda d, e, s, hop=hop: (d ^ hop, e ^ hop, s)) if hop else piece
            for hop, piece in zip(RETURNS, pieces)
        ]
        kept, given = call(
            halve_kernel,
            [bf16((n_dp, half, rows))] * 2,
            *pieces,
            flops=400 * group * group * half,
        )
        given = along_seq(given)
    with jax.named_scope("swap_cotangent"):
        stacked = call(
            functools.partial(stack_kernel, n_dp),
            bf16((n_dp, rows, width)),
            *same,
            spaces=[pltpu.VMEM] * n_dp + [pl.ANY] * 0,
            scratch=[pltpu.SemaphoreType.DMA((n_dp,))],
            bytes_accessed=4 * n_dp * rows * width,
        )
    with jax.named_scope("gradient"):
        partial = call(
            functools.partial(gradient_kernel, n_enc),
            [bf16((half // 2, 2 * block))] * n_enc,
            kept,
            given,
            stacked,
            along_seq(stacked),
            flops=2 * half * width * rows * n_dp * n_seq,
            bytes_accessed=2 * n_dp * n_seq * rows * width,
        )
    with jax.named_scope("sum_gradient"):
        partial = [
            move(part, lambda d, e, s, hop=hop: (d ^ e, e ^ hop, s))
            for hop, part in zip(SUMS, partial)
        ]
    with jax.named_scope("send_home"):
        homes = [pieces[RETURNS.index(k)] for k in range(n_dp)]
        homes[1:] = [
            move(homes[k], lambda d, e, s, k=k: (d ^ k, e, s)) for k in range(1, n_dp)
        ]
    early = 3
    with jax.named_scope("project"):
        projected = call(
            project_kernel,
            jax.ShapeDtypeStruct((rows, width), jnp.float32),
            residual,
            out_weight,
            *homes[:early],
            scratch=[pltpu.VMEM((early * block, rows), jnp.bfloat16)],
            flops=2 * rows * early * block * width,
            bytes_accessed=2 * early * block * width,
        )
    with jax.named_scope("finish"):
        layer_out, grad_weight = call(
            functools.partial(finish_kernel, n_dp, early),
            [bf16((rows, width)), jax.ShapeDtypeStruct((half, block), jnp.float32)],
            *partial,
            *homes[early:],
            projected,
            out_weight,
            scratch=[pltpu.VMEM(((n_dp - early) * block, rows), jnp.bfloat16)],
            flops=2 * rows * (n_dp - early) * block * width,
            bytes_accessed=2 * (n_dp - early) * block * width,
        )
    return (layer_out, grad_weight)


def attend_groups(query_group, key_group, value_group, image_ids):
    items, slot_count, group_width = query_group.shape
    group_heads = HEADS // 2
    head_width = group_width // group_heads
    scale = 1.0 / math.sqrt(head_width)
    position = jnp.arange(slot_count)
    image_ids = jnp.where(image_ids < 0, -1 - position[None, :], image_ids)
    shaped_query = query_group.reshape(items, slot_count, group_heads, head_width)
    shaped_key = key_group.reshape(items, slot_count, group_heads, head_width)
    shaped_value = value_group.reshape(items, slot_count, group_heads, head_width)
    scores = (
        jnp.einsum("gqhd,gkhd->ghqk", shaped_query, shaped_key, preferred_element_type=jnp.float32)
        * scale
    )
    same_image = image_ids[:, None, :, None] == image_ids[:, None, None, :]
    scores = jnp.where(same_image, scores, -1e30)
    highest = jnp.max(scores, axis=-1, keepdims=True)
    weights = jnp.exp(scores - highest)
    probs = (weights / jnp.sum(weights, axis=-1, keepdims=True)).astype(jnp.bfloat16)
    mixed = jnp.einsum("ghqk,gkhd->gqhd", probs, shaped_value, preferred_element_type=jnp.float32)
    return mixed.reshape(items, slot_count, group_width).astype(jnp.bfloat16)


def routed_body(
    queries, key_vectors, value_vectors, residual, out_weight, cotangent, send_row, image_id
):
    row_count, full_width = queries.shape
    half_width = full_width // 2
    is_live = send_row < row_count
    source_row = jnp.minimum(send_row, row_count - 1)

    def arrange(data):
        grouped = data.reshape(row_count, 2, half_width).transpose(1, 0, 2)
        return jnp.where(is_live[None, :, None], grouped[:, source_row], jnp.zeros((), data.dtype))

    send_query = arrange(queries)
    send_key = arrange(key_vectors)
    send_value = arrange(value_vectors)
    send_image = jnp.where(is_live, image_id[source_row], -1)
    send_image = jnp.broadcast_to(send_image[None, :], (2, send_row.shape[0]))
    received = (
        lax.all_to_all(send_query, "enc", split_axis=1, concat_axis=1, tiled=True),
        lax.all_to_all(send_key, "enc", split_axis=1, concat_axis=1, tiled=True),
        lax.all_to_all(send_value, "enc", split_axis=1, concat_axis=1, tiled=True),
        lax.all_to_all(send_image, "enc", split_axis=1, concat_axis=1, tiled=True),
    )
    output = attend_groups(received[0], received[1], received[2], received[3])
    returned = lax.all_to_all(output, "enc", split_axis=1, concat_axis=1, tiled=True)
    holder = jnp.zeros((2, row_count + 1, half_width), jnp.bfloat16).at[:, send_row].set(returned)
    attended = holder[:, :row_count].transpose(1, 0, 2).reshape(row_count, full_width)
    projected = jnp.dot(attended, out_weight, preferred_element_type=jnp.float32)
    layer_out = (residual.astype(jnp.float32) + projected).astype(jnp.bfloat16)
    first_sum = lax.psum_scatter(
        lax.dot_general(
            attended, cotangent, (((0,), (0,)), ((), ())), preferred_element_type=jnp.float32
        ).astype(jnp.bfloat16),
        "dp",
        scatter_dimension=0,
        tiled=True,
    )
    second_sum = lax.psum_scatter(first_sum, "seq", scatter_dimension=0, tiled=True).astype(
        jnp.float32
    )
    grad_weight = lax.psum_scatter(second_sum, "enc", scatter_dimension=1, tiled=True)
    return (layer_out, grad_weight)


def solution(mesh):
    sizes = tuple(mesh.shape[name] for name in AXES)
    n_dp, n_enc, n_seq = sizes
    fits = n_seq == 2 and n_dp == n_enc == 4 and HEADS % (2 * n_enc) == 0
    body = functools.partial(exchange_body, sizes) if fits else routed_body
    placed = (
        P(("dp", "enc", "seq"), None),
        P(("dp", "enc", "seq"), None),
        P(("dp", "enc", "seq"), None),
        P(("dp", "enc", "seq"), None),
        P(),
        P(("dp", "enc", "seq"), None),
        P(("dp", "enc", "seq")),
        P(("dp", "enc", "seq")),
    )
    return jax.shard_map(
        body,
        mesh=mesh,
        in_specs=placed,
        out_specs=(P(("dp", "enc", "seq"), None), P(("dp", "seq"), "enc")),
        check_vma=False,
    )
```

```python
import functools
import math

import jax
import jax.numpy as jnp
from jax import lax
from jax.experimental import pallas as pl
from jax.experimental.pallas import tpu as pltpu
from jax.sharding import PartitionSpec as P

HEADS = 16
AXES = ("dp", "enc", "seq")
ID_ROWS = 16
ID_BASE = 64
SENDS = (0, 3, 1, 2)
RETURNS = (3, 2, 1, 0)
SUMS = (3, 2, 1, 0)


def call(
    kernel,
    out_shape,
    *args,
    spaces=None,
    scratch=(),
    limit=16,
    flops=0,
    bytes_accessed=0,
):
    def placed(space):
        return pl.BlockSpec(memory_space=space)

    many = isinstance(out_shape, (list, tuple))
    spaces = spaces or [pltpu.VMEM] * len(args)
    args = [
        pltpu.with_memory_space_constraint(arg, pltpu.HBM) if space == pltpu.HBM else arg
        for arg, space in zip(args, spaces)
    ]
    return pl.pallas_call(
        kernel,
        out_shape=out_shape,
        in_specs=[placed(space) for space in spaces],
        out_specs=[placed(pltpu.VMEM)] * len(out_shape) if many else placed(pltpu.VMEM),
        scratch_shapes=list(scratch),
        compiler_params=pltpu.CompilerParams(vmem_limit_bytes=limit * 1024 * 1024),
        cost_estimate=pl.CostEstimate(
            flops=flops, bytes_accessed=bytes_accessed, transcendentals=0
        ),
    )(*args)


def pack_kernel(block, *refs):
    sources, outs, (ready, held, arrived, ids_held, sems) = refs[:5], refs[5:-5], refs[-5:]
    targets = [ids_held] + [arrived.at[which] for which in range(3)] + [ready]
    copies = [
        pltpu.make_async_copy(source, target, sems.at[which])
        for which, (source, target) in enumerate(zip(sources, targets))
    ]
    for copy in copies:
        copy.start()
    first = lax.axis_index("dp") ^ lax.axis_index("enc")
    copies[0].wait()
    ids = ids_held[...]
    row = lax.broadcasted_iota(jnp.int32, (ID_ROWS, ids.shape[1]), 0)
    digits = jnp.where(row == 0, ids // ID_BASE, jnp.where(row == 1, ids % ID_BASE, 0))
    digits = digits.astype(jnp.float32).astype(jnp.bfloat16)
    for out in outs:
        out[3 * block :] = digits
    for which in range(3):
        copies[1 + which].wait()
        held[...] = arrived[which].T
        for hop, out in zip(SENDS, outs):
            begin = pl.multiple_of((first ^ hop) * block, 16)
            out[which * block : (which + 1) * block] = held[pl.ds(begin, block)]
    copies[4].wait()


def identifiers(slabs, block):
    numbers = []
    for slab in slabs:
        digits = slab[3 * block : 3 * block + ID_ROWS].astype(jnp.float32)
        numbers.append(digits[0:1] * ID_BASE + digits[1:2])
    return numbers


def set_bias(bias, key_ids, query_ids):
    queries = jnp.concatenate(query_ids, axis=1)
    for index, ids in enumerate(key_ids):
        rows = ids.shape[1]
        column = jnp.broadcast_to(ids, (rows, rows)).T
        column = jnp.concatenate([column] * len(query_ids), axis=1)
        bias[index * rows : (index + 1) * rows] = jnp.where(column == queries, 0.0, -1e30)


def gather(slabs, which, block, head, head_width):
    begin = which * block + head * head_width
    return jnp.concatenate([slab[begin : begin + head_width] for slab in slabs], axis=1)


def weigh(key, query, bias):
    scores = lax.dot_general(
        key, query, (((0,), (0,)), ((), ())), preferred_element_type=jnp.float32
    )
    scores = scores + bias
    return scores, jnp.max(scores, axis=0, keepdims=True)


def attend_first_kernel(block, head_width, *refs):
    slabs, (mixed, highest, total, bias) = refs[:-4], refs[-4:]
    ids = identifiers(slabs, block)
    set_bias(bias, ids, ids)
    factor = math.log2(math.e) / math.sqrt(head_width)
    for head in range(block // head_width):
        query, key, value = (gather(slabs, which, block, head, head_width) for which in range(3))
        scores, top = weigh(key, query, bias[...])
        weights = jnp.exp2((scores - top) * factor)
        highest[head : head + 1] = top
        total[head : head + 1] = jnp.sum(weights, axis=0, keepdims=True)
        mixed[head * head_width : (head + 1) * head_width] = jnp.dot(
            value, weights.astype(jnp.bfloat16), preferred_element_type=jnp.float32
        )


def attend_last_kernel(block, head_width, *refs):
    count = len(SENDS)
    slabs, (mixed, highest, total), outs = refs[:count], refs[count : count + 3], refs[count + 3 : -2]
    old_bias, new_bias = refs[-2:]
    *early, late = slabs
    rows = late.shape[1]
    *early_ids, late_id = identifiers(slabs, block)
    set_bias(old_bias, [late_id], early_ids)
    set_bias(new_bias, early_ids + [late_id], [late_id])
    factor = math.log2(math.e) / math.sqrt(head_width)
    for head in range(block // head_width):
        span = slice(head * head_width, (head + 1) * head_width)
        query, key, value = (gather(early, which, block, head, head_width) for which in range(3))
        new_query, new_key, new_value = (
            gather([late], which, block, head, head_width) for which in range(3)
        )
        scores, top = weigh(new_key, query, old_bias[...])
        before = highest[head : head + 1]
        top = jnp.maximum(top, before)
        weights = jnp.exp2((scores - top) * factor)
        shrink = jnp.exp2((before - top) * factor)
        sums = total[head : head + 1] * shrink + jnp.sum(weights, axis=0, keepdims=True)
        result = mixed[span] * shrink + jnp.dot(
            new_value, weights.astype(jnp.bfloat16), preferred_element_type=jnp.float32
        )
        result = (result / sums).astype(jnp.bfloat16)
        for index in range(count - 1):
            out = outs[RETURNS.index(SENDS[index])]
            out[span] = result[:, index * rows : (index + 1) * rows]
        scores, top = weigh(
            jnp.concatenate([key, new_key], axis=1), new_query, new_bias[...]
        )
        weights = jnp.exp2((scores - top) * factor)
        sums = jnp.sum(weights, axis=0, keepdims=True)
        result = jnp.dot(
            jnp.concatenate([value, new_value], axis=1),
            weights.astype(jnp.bfloat16),
            preferred_element_type=jnp.float32,
        )
        outs[RETURNS.index(SENDS[-1])][span] = (result / sums).astype(jnp.bfloat16)


def stack_kernel(count, *refs):
    sources, out, sems = refs[:count], refs[-2], refs[-1]
    copies = [
        pltpu.make_async_copy(source, out.at[index], sems.at[index])
        for index, source in enumerate(sources)
    ]
    for copy in copies:
        copy.start()
    for copy in copies:
        copy.wait()


def halve_kernel(*refs):
    pieces, (kept, given) = refs[:-2], refs[-2:]
    s = lax.axis_index("seq")
    half = kept.shape[1]
    for hop, piece in zip(RETURNS, pieces):
        kept[hop] = piece[pl.ds(pl.multiple_of(s * half, 16), half)]
        given[hop] = piece[pl.ds(pl.multiple_of((1 - s) * half, 16), half)]


def gradient_kernel(count, *refs):
    kept, given, same, others, *outs = refs
    e = lax.axis_index("enc")
    features, rows = [], []
    for step in range(count):
        features += [kept[step], given[step]]
        rows += [same[step], others[step]]
    total = jnp.dot(
        jnp.concatenate(features, axis=1),
        jnp.concatenate(rows, axis=0),
        preferred_element_type=jnp.float32,
    )
    width, short = total.shape[1] // count, total.shape[0] // 2
    for target in range(count):
        block = total[:, target * width : (target + 1) * width]
        folded = jnp.concatenate([block[:short], block[short:]], axis=1).astype(jnp.bfloat16)

        for index, out in enumerate(outs):

            @pl.when(e ^ target == SUMS[index])
            def _():
                out[...] = folded


def project_kernel(*refs):
    pieces, (residual, weight, out, attended) = refs[:-4], refs[-4:]
    first = lax.axis_index("dp") ^ lax.axis_index("enc")
    block = pieces[0].shape[0]
    for hop, piece in zip(RETURNS, pieces):
        attended[pl.ds(pl.multiple_of((first ^ hop) * block, 16), block)] = piece[...]
    projected = lax.dot_general(
        attended[...], weight[...], (((0,), (0,)), ((), ())), preferred_element_type=jnp.float32
    )
    out[...] = (residual[...].astype(jnp.float32) + projected).astype(jnp.bfloat16)


def add_kernel(*refs):
    partial, out = refs[:-1], refs[-1]
    total = partial[0][...].astype(jnp.float32)
    for ref in partial[1:]:
        total = total + ref[...].astype(jnp.float32)
    short, width = total.shape[0], out.shape[1]
    out[:short] = total[:, :width]
    out[short:] = total[:, width:]


def exchange_body(
    sizes, queries, key_vectors, value_vectors, residual, out_weight, cotangent, send_row, image_id
):
    n_dp, n_enc, n_seq = sizes
    rows, width = queries.shape
    block = width // n_enc
    half = block // n_seq
    head_width = width // HEADS
    group = n_enc * rows
    tall = 3 * block + ID_ROWS
    bf16 = functools.partial(jax.ShapeDtypeStruct, dtype=jnp.bfloat16)
    hbm = pltpu.HBM

    def move(data, partner):
        pairs = []
        for d in range(n_dp):
            for e in range(n_enc):
                for s in range(n_seq):
                    to_d, to_e, to_s = partner(d, e, s)
                    pairs.append(
                        ((d * n_enc + e) * n_seq + s, (to_d * n_enc + to_e) * n_seq + to_s)
                    )
        return lax.ppermute(data, AXES, pairs)

    def along_enc(pieces, hops):
        return [
            move(piece, lambda d, e, s, hop=hop: (d, e ^ hop, s)) if hop else piece
            for hop, piece in zip(hops, pieces)
        ]

    def along_seq(data):
        return move(data, lambda d, e, s: (d, e, s ^ 1))

    with jax.named_scope("pack"):
        outs = call(
            functools.partial(pack_kernel, block),
            [bf16((tall, rows))] * n_enc + [bf16((rows, width))],
            image_id.reshape(1, rows),
            queries,
            key_vectors,
            value_vectors,
            cotangent,
            spaces=[hbm] * 5,
            scratch=[
                pltpu.VMEM((width, rows), jnp.bfloat16),
                pltpu.VMEM((3, rows, width), jnp.bfloat16),
                pltpu.VMEM((1, rows), jnp.int32),
                pltpu.SemaphoreType.DMA((5,)),
            ],
            bytes_accessed=8 * rows * width * 2,
        )
        slabs, cotangent = outs[:-1], outs[-1]
    with jax.named_scope("exchange_heads"):
        slabs = along_enc(slabs, SENDS)
    with jax.named_scope("gather_cotangent"):
        same = [cotangent] + [
            move(cotangent, lambda d, e, s, k=k: (d ^ k, e, s)) for k in range(1, n_dp)
        ]
    with jax.named_scope("attention"):
        known = group - rows
        f32 = functools.partial(jax.ShapeDtypeStruct, dtype=jnp.float32)
        state = call(
            functools.partial(attend_first_kernel, block, head_width),
            [f32((block, known)), f32((8, known)), f32((8, known))],
            *slabs[:-1],
            scratch=[pltpu.VMEM((known, known), jnp.float32)],
            flops=55 * known * known * block,
            bytes_accessed=8 * group * block,
        )
        pieces = call(
            functools.partial(attend_last_kernel, block, head_width),
            [bf16((block, rows))] * n_enc,
            *slabs,
            *state,
            scratch=[pltpu.VMEM((rows, known), jnp.float32), pltpu.VMEM((group, rows), jnp.float32)],
            flops=55 * (group * group - known * known) * block,
            bytes_accessed=8 * group * block,
        )
    with jax.named_scope("send_to_owner"):
        pieces = [
            move(piece, lambda d, e, s, hop=hop: (d ^ hop, e ^ hop, s)) if hop else piece
            for hop, piece in zip(RETURNS, pieces)
        ]
        kept, given = call(
            halve_kernel,
            [bf16((n_dp, half, rows))] * 2,
            *pieces,
            flops=400 * group * group * half,
        )
        given = along_seq(given)
    with jax.named_scope("swap_cotangent"):
        stacked = call(
            functools.partial(stack_kernel, n_dp),
            bf16((n_dp, rows, width)),
            *same,
            spaces=[pltpu.VMEM] * n_dp + [pl.ANY] * 0,
            scratch=[pltpu.SemaphoreType.DMA((n_dp,))],
            bytes_accessed=4 * n_dp * rows * width,
        )
    with jax.named_scope("gradient"):
        partial = call(
            functools.partial(gradient_kernel, n_enc),
            [bf16((half // 2, 2 * block))] * n_enc,
            kept,
            given,
            stacked,
            along_seq(stacked),
            flops=2 * half * width * rows * n_dp * n_seq,
            bytes_accessed=2 * n_dp * n_seq * rows * width,
        )
    with jax.named_scope("sum_gradient"):
        partial = [
            move(part, lambda d, e, s, hop=hop: (d ^ e, e ^ hop, s))
            for hop, part in zip(SUMS, partial)
        ]
    with jax.named_scope("send_home"):
        homes = [
            move(piece, lambda d, e, s, hop=hop: (d ^ hop, e, s)) if hop else piece
            for hop, piece in zip(RETURNS, pieces)
        ]
    with jax.named_scope("project"):
        layer_out = call(
            project_kernel,
            bf16((rows, width)),
            *homes,
            residual,
            out_weight,
            scratch=[pltpu.VMEM((width, rows), jnp.bfloat16)],
            flops=rows * width * width,
            bytes_accessed=2 * width * width,
        )
    with jax.named_scope("add_gradient"):
        grad_weight = call(
            add_kernel,
            jax.ShapeDtypeStruct((half, block), jnp.float32),
            *partial,
            bytes_accessed=4 * half * block * 4,
        )
    return (layer_out, grad_weight)


def attend_groups(query_group, key_group, value_group, image_ids):
    items, slot_count, group_width = query_group.shape
    group_heads = HEADS // 2
    head_width = group_width // group_heads
    scale = 1.0 / math.sqrt(head_width)
    position = jnp.arange(slot_count)
    image_ids = jnp.where(image_ids < 0, -1 - position[None, :], image_ids)
    shaped_query = query_group.reshape(items, slot_count, group_heads, head_width)
    shaped_key = key_group.reshape(items, slot_count, group_heads, head_width)
    shaped_value = value_group.reshape(items, slot_count, group_heads, head_width)
    scores = (
        jnp.einsum("gqhd,gkhd->ghqk", shaped_query, shaped_key, preferred_element_type=jnp.float32)
        * scale
    )
    same_image = image_ids[:, None, :, None] == image_ids[:, None, None, :]
    scores = jnp.where(same_image, scores, -1e30)
    highest = jnp.max(scores, axis=-1, keepdims=True)
    weights = jnp.exp(scores - highest)
    probs = (weights / jnp.sum(weights, axis=-1, keepdims=True)).astype(jnp.bfloat16)
    mixed = jnp.einsum("ghqk,gkhd->gqhd", probs, shaped_value, preferred_element_type=jnp.float32)
    return mixed.reshape(items, slot_count, group_width).astype(jnp.bfloat16)


def routed_body(
    queries, key_vectors, value_vectors, residual, out_weight, cotangent, send_row, image_id
):
    row_count, full_width = queries.shape
    half_width = full_width // 2
    is_live = send_row < row_count
    source_row = jnp.minimum(send_row, row_count - 1)

    def arrange(data):
        grouped = data.reshape(row_count, 2, half_width).transpose(1, 0, 2)
        return jnp.where(is_live[None, :, None], grouped[:, source_row], jnp.zeros((), data.dtype))

    send_query = arrange(queries)
    send_key = arrange(key_vectors)
    send_value = arrange(value_vectors)
    send_image = jnp.where(is_live, image_id[source_row], -1)
    send_image = jnp.broadcast_to(send_image[None, :], (2, send_row.shape[0]))
    received = (
        lax.all_to_all(send_query, "enc", split_axis=1, concat_axis=1, tiled=True),
        lax.all_to_all(send_key, "enc", split_axis=1, concat_axis=1, tiled=True),
        lax.all_to_all(send_value, "enc", split_axis=1, concat_axis=1, tiled=True),
        lax.all_to_all(send_image, "enc", split_axis=1, concat_axis=1, tiled=True),
    )
    output = attend_groups(received[0], received[1], received[2], received[3])
    returned = lax.all_to_all(output, "enc", split_axis=1, concat_axis=1, tiled=True)
    holder = jnp.zeros((2, row_count + 1, half_width), jnp.bfloat16).at[:, send_row].set(returned)
    attended = holder[:, :row_count].transpose(1, 0, 2).reshape(row_count, full_width)
    projected = jnp.dot(attended, out_weight, preferred_element_type=jnp.float32)
    layer_out = (residual.astype(jnp.float32) + projected).astype(jnp.bfloat16)
    first_sum = lax.psum_scatter(
        lax.dot_general(
            attended, cotangent, (((0,), (0,)), ((), ())), preferred_element_type=jnp.float32
        ).astype(jnp.bfloat16),
        "dp",
        scatter_dimension=0,
        tiled=True,
    )
    second_sum = lax.psum_scatter(first_sum, "seq", scatter_dimension=0, tiled=True).astype(
        jnp.float32
    )
    grad_weight = lax.psum_scatter(second_sum, "enc", scatter_dimension=1, tiled=True)
    return (layer_out, grad_weight)


def solution(mesh):
    sizes = tuple(mesh.shape[name] for name in AXES)
    n_dp, n_enc, n_seq = sizes
    fits = n_seq == 2 and n_dp == n_enc == 4 and HEADS % (2 * n_enc) == 0
    body = functools.partial(exchange_body, sizes) if fits else routed_body
    placed = (
        P(("dp", "enc", "seq"), None),
        P(("dp", "enc", "seq"), None),
        P(("dp", "enc", "seq"), None),
        P(("dp", "enc", "seq"), None),
        P(),
        P(("dp", "enc", "seq"), None),
        P(("dp", "enc", "seq")),
        P(("dp", "enc", "seq")),
    )
    return jax.shard_map(
        body,
        mesh=mesh,
        in_specs=placed,
        out_specs=(P(("dp", "enc", "seq"), None), P(("dp", "seq"), "enc")),
        check_vma=False,
    )
```

```python
import functools
import math

import jax
import jax.numpy as jnp
from jax import lax
from jax.experimental import pallas as pl
from jax.experimental.pallas import tpu as pltpu
from jax.sharding import PartitionSpec as P

HEADS = 16
AXES = ("dp", "enc", "seq")
ID_ROWS = 16
ID_BASE = 64
SENDS = (0, 3, 1, 2)
RETURNS = (1, 3, 2, 0)
SUMS = (1, 3, 2, 0)


def call(
    kernel,
    out_shape,
    *args,
    spaces=None,
    scratch=(),
    limit=16,
    flops=0,
    bytes_accessed=0,
):
    def placed(space):
        return pl.BlockSpec(memory_space=space)

    many = isinstance(out_shape, (list, tuple))
    spaces = spaces or [pltpu.VMEM] * len(args)
    args = [
        pltpu.with_memory_space_constraint(arg, pltpu.HBM) if space == pltpu.HBM else arg
        for arg, space in zip(args, spaces)
    ]
    return pl.pallas_call(
        kernel,
        out_shape=out_shape,
        in_specs=[placed(space) for space in spaces],
        out_specs=[placed(pltpu.VMEM)] * len(out_shape) if many else placed(pltpu.VMEM),
        scratch_shapes=list(scratch),
        compiler_params=pltpu.CompilerParams(vmem_limit_bytes=limit * 1024 * 1024),
        cost_estimate=pl.CostEstimate(
            flops=flops, bytes_accessed=bytes_accessed, transcendentals=0
        ),
    )(*args)


def pack_kernel(block, *refs):
    sources, outs, (ready, held, arrived, ids_held, sems) = refs[:5], refs[5:-5], refs[-5:]
    targets = [ids_held] + [arrived.at[which] for which in range(3)] + [ready]
    copies = [
        pltpu.make_async_copy(source, target, sems.at[which])
        for which, (source, target) in enumerate(zip(sources, targets))
    ]
    for copy in copies:
        copy.start()
    first = lax.axis_index("dp") ^ lax.axis_index("enc")
    copies[0].wait()
    ids = ids_held[...]
    row = lax.broadcasted_iota(jnp.int32, (ID_ROWS, ids.shape[1]), 0)
    digits = jnp.where(row == 0, ids // ID_BASE, jnp.where(row == 1, ids % ID_BASE, 0))
    digits = digits.astype(jnp.float32).astype(jnp.bfloat16)
    for out in outs:
        out[3 * block :] = digits
    for which in range(3):
        copies[1 + which].wait()
        held[...] = arrived[which].T
        for hop, out in zip(SENDS, outs):
            begin = pl.multiple_of((first ^ hop) * block, 16)
            out[which * block : (which + 1) * block] = held[pl.ds(begin, block)]
    copies[4].wait()


def identifiers(slabs, block):
    numbers = []
    for slab in slabs:
        digits = slab[3 * block : 3 * block + ID_ROWS].astype(jnp.float32)
        numbers.append(digits[0:1] * ID_BASE + digits[1:2])
    return numbers


def set_bias(bias, key_ids, query_ids):
    queries = jnp.concatenate(query_ids, axis=1)
    for index, ids in enumerate(key_ids):
        rows = ids.shape[1]
        column = jnp.broadcast_to(ids, (rows, rows)).T
        column = jnp.concatenate([column] * len(query_ids), axis=1)
        bias[index * rows : (index + 1) * rows] = jnp.where(column == queries, 0.0, -1e30)


def gather(slabs, which, block, head, head_width):
    begin = which * block + head * head_width
    return jnp.concatenate([slab[begin : begin + head_width] for slab in slabs], axis=1)


def weigh(key, query, bias):
    scores = lax.dot_general(
        key, query, (((0,), (0,)), ((), ())), preferred_element_type=jnp.float32
    )
    scores = scores + bias
    return scores, jnp.max(scores, axis=0, keepdims=True)


def attend_first_kernel(block, head_width, *refs):
    slabs, (mixed, highest, total, bias) = refs[:-4], refs[-4:]
    ids = identifiers(slabs, block)
    set_bias(bias, ids, ids)
    factor = math.log2(math.e) / math.sqrt(head_width)
    for head in range(block // head_width):
        query, key, value = (gather(slabs, which, block, head, head_width) for which in range(3))
        scores, top = weigh(key, query, bias[...])
        weights = jnp.exp2((scores - top) * factor)
        highest[head : head + 1] = top
        total[head : head + 1] = jnp.sum(weights, axis=0, keepdims=True)
        mixed[head * head_width : (head + 1) * head_width] = jnp.dot(
            value, weights.astype(jnp.bfloat16), preferred_element_type=jnp.float32
        )


def attend_last_kernel(block, head_width, *refs):
    count = len(SENDS)
    slabs, (mixed, highest, total), outs = refs[:count], refs[count : count + 3], refs[count + 3 : -2]
    old_bias, new_bias = refs[-2:]
    *early, late = slabs
    rows = late.shape[1]
    *early_ids, late_id = identifiers(slabs, block)
    set_bias(old_bias, [late_id], early_ids)
    set_bias(new_bias, early_ids + [late_id], [late_id])
    factor = math.log2(math.e) / math.sqrt(head_width)
    for head in range(block // head_width):
        span = slice(head * head_width, (head + 1) * head_width)
        query, key, value = (gather(early, which, block, head, head_width) for which in range(3))
        new_query, new_key, new_value = (
            gather([late], which, block, head, head_width) for which in range(3)
        )
        scores, top = weigh(new_key, query, old_bias[...])
        before = highest[head : head + 1]
        top = jnp.maximum(top, before)
        weights = jnp.exp2((scores - top) * factor)
        shrink = jnp.exp2((before - top) * factor)
        sums = total[head : head + 1] * shrink + jnp.sum(weights, axis=0, keepdims=True)
        result = mixed[span] * shrink + jnp.dot(
            new_value, weights.astype(jnp.bfloat16), preferred_element_type=jnp.float32
        )
        result = (result / sums).astype(jnp.bfloat16)
        for index in range(count - 1):
            out = outs[RETURNS.index(SENDS[index])]
            out[span] = result[:, index * rows : (index + 1) * rows]
        scores, top = weigh(
            jnp.concatenate([key, new_key], axis=1), new_query, new_bias[...]
        )
        weights = jnp.exp2((scores - top) * factor)
        sums = jnp.sum(weights, axis=0, keepdims=True)
        result = jnp.dot(
            jnp.concatenate([value, new_value], axis=1),
            weights.astype(jnp.bfloat16),
            preferred_element_type=jnp.float32,
        )
        outs[RETURNS.index(SENDS[-1])][span] = (result / sums).astype(jnp.bfloat16)


def stack_kernel(count, *refs):
    sources, out, sems = refs[:count], refs[-2], refs[-1]
    copies = [
        pltpu.make_async_copy(source, out.at[index], sems.at[index])
        for index, source in enumerate(sources)
    ]
    for copy in copies:
        copy.start()
    for copy in copies:
        copy.wait()


def halve_kernel(*refs):
    pieces, (kept, given) = refs[:-2], refs[-2:]
    s = lax.axis_index("seq")
    half = kept.shape[1]
    for hop, piece in zip(RETURNS, pieces):
        kept[hop] = piece[pl.ds(pl.multiple_of(s * half, 16), half)]
        given[hop] = piece[pl.ds(pl.multiple_of((1 - s) * half, 16), half)]


def gradient_kernel(count, *refs):
    kept, given, same, others, *outs = refs
    e = lax.axis_index("enc")
    features, rows = [], []
    for step in range(count):
        features += [kept[step], given[step]]
        rows += [same[step], others[step]]
    total = jnp.dot(
        jnp.concatenate(features, axis=1),
        jnp.concatenate(rows, axis=0),
        preferred_element_type=jnp.float32,
    )
    width, short = total.shape[1] // count, total.shape[0] // 2
    for target in range(count):
        block = total[:, target * width : (target + 1) * width]
        folded = jnp.concatenate([block[:short], block[short:]], axis=1).astype(jnp.bfloat16)

        for index, out in enumerate(outs):

            @pl.when(e ^ target == SUMS[index])
            def _():
                out[...] = folded


def project_kernel(*refs):
    pieces, (residual, weight, out, attended) = refs[:-4], refs[-4:]
    first = lax.axis_index("dp") ^ lax.axis_index("enc")
    block = pieces[0].shape[0]
    for hop, piece in zip(RETURNS, pieces):
        attended[pl.ds(pl.multiple_of((first ^ hop) * block, 16), block)] = piece[...]
    projected = lax.dot_general(
        attended[...], weight[...], (((0,), (0,)), ((), ())), preferred_element_type=jnp.float32
    )
    out[...] = (residual[...].astype(jnp.float32) + projected).astype(jnp.bfloat16)


def add_kernel(*refs):
    partial, out = refs[:-1], refs[-1]
    total = partial[0][...].astype(jnp.float32)
    for ref in partial[1:]:
        total = total + ref[...].astype(jnp.float32)
    short, width = total.shape[0], out.shape[1]
    out[:short] = total[:, :width]
    out[short:] = total[:, width:]


def exchange_body(
    sizes, queries, key_vectors, value_vectors, residual, out_weight, cotangent, send_row, image_id
):
    n_dp, n_enc, n_seq = sizes
    rows, width = queries.shape
    block = width // n_enc
    half = block // n_seq
    head_width = width // HEADS
    group = n_enc * rows
    tall = 3 * block + ID_ROWS
    bf16 = functools.partial(jax.ShapeDtypeStruct, dtype=jnp.bfloat16)
    hbm = pltpu.HBM

    def move(data, partner):
        pairs = []
        for d in range(n_dp):
            for e in range(n_enc):
                for s in range(n_seq):
                    to_d, to_e, to_s = partner(d, e, s)
                    pairs.append(
                        ((d * n_enc + e) * n_seq + s, (to_d * n_enc + to_e) * n_seq + to_s)
                    )
        return lax.ppermute(data, AXES, pairs)

    def along_enc(pieces, hops):
        return [
            move(piece, lambda d, e, s, hop=hop: (d, e ^ hop, s)) if hop else piece
            for hop, piece in zip(hops, pieces)
        ]

    def along_seq(data):
        return move(data, lambda d, e, s: (d, e, s ^ 1))

    with jax.named_scope("pack"):
        outs = call(
            functools.partial(pack_kernel, block),
            [bf16((tall, rows))] * n_enc + [bf16((rows, width))],
            image_id.reshape(1, rows),
            queries,
            key_vectors,
            value_vectors,
            cotangent,
            spaces=[hbm] * 5,
            scratch=[
                pltpu.VMEM((width, rows), jnp.bfloat16),
                pltpu.VMEM((3, rows, width), jnp.bfloat16),
                pltpu.VMEM((1, rows), jnp.int32),
                pltpu.SemaphoreType.DMA((5,)),
            ],
            bytes_accessed=8 * rows * width * 2,
        )
        slabs, cotangent = outs[:-1], outs[-1]
    with jax.named_scope("exchange_heads"):
        slabs = along_enc(slabs, SENDS)
    with jax.named_scope("gather_cotangent"):
        same = [cotangent] + [
            move(cotangent, lambda d, e, s, k=k: (d ^ k, e, s)) for k in range(1, n_dp)
        ]
    with jax.named_scope("attention"):
        known = group - rows
        f32 = functools.partial(jax.ShapeDtypeStruct, dtype=jnp.float32)
        state = call(
            functools.partial(attend_first_kernel, block, head_width),
            [f32((block, known)), f32((8, known)), f32((8, known))],
            *slabs[:-1],
            scratch=[pltpu.VMEM((known, known), jnp.float32)],
            flops=55 * known * known * block,
            bytes_accessed=8 * group * block,
        )
        pieces = call(
            functools.partial(attend_last_kernel, block, head_width),
            [bf16((block, rows))] * n_enc,
            *slabs,
            *state,
            scratch=[pltpu.VMEM((rows, known), jnp.float32), pltpu.VMEM((group, rows), jnp.float32)],
            flops=55 * (group * group - known * known) * block,
            bytes_accessed=8 * group * block,
        )
    with jax.named_scope("send_to_owner"):
        pieces = [
            move(piece, lambda d, e, s, hop=hop: (d ^ hop, e ^ hop, s)) if hop else piece
            for hop, piece in zip(RETURNS, pieces)
        ]
        kept, given = call(
            halve_kernel,
            [bf16((n_dp, half, rows))] * 2,
            *pieces,
            flops=400 * group * group * half,
        )
        given = along_seq(given)
    with jax.named_scope("swap_cotangent"):
        stacked = call(
            functools.partial(stack_kernel, n_dp),
            bf16((n_dp, rows, width)),
            *same,
            spaces=[pltpu.VMEM] * n_dp + [pl.ANY] * 0,
            scratch=[pltpu.SemaphoreType.DMA((n_dp,))],
            bytes_accessed=4 * n_dp * rows * width,
        )
    with jax.named_scope("gradient"):
        partial = call(
            functools.partial(gradient_kernel, n_enc),
            [bf16((half // 2, 2 * block))] * n_enc,
            kept,
            given,
            stacked,
            along_seq(stacked),
            flops=2 * half * width * rows * n_dp * n_seq,
            bytes_accessed=2 * n_dp * n_seq * rows * width,
        )
    with jax.named_scope("sum_gradient"):
        partial = [
            move(part, lambda d, e, s, hop=hop: (d ^ e, e ^ hop, s))
            for hop, part in zip(SUMS, partial)
        ]
    with jax.named_scope("send_home"):
        homes = [
            move(piece, lambda d, e, s, hop=hop: (d ^ hop, e, s)) if hop else piece
            for hop, piece in zip(RETURNS, pieces)
        ]
    with jax.named_scope("project"):
        layer_out = call(
            project_kernel,
            bf16((rows, width)),
            *homes,
            residual,
            out_weight,
            scratch=[pltpu.VMEM((width, rows), jnp.bfloat16)],
            flops=2 * rows * width * width,
            bytes_accessed=2 * width * width,
        )
    with jax.named_scope("add_gradient"):
        grad_weight = call(
            add_kernel,
            jax.ShapeDtypeStruct((half, block), jnp.float32),
            *partial,
            bytes_accessed=4 * half * block * 4,
        )
    return (layer_out, grad_weight)


def attend_groups(query_group, key_group, value_group, image_ids):
    items, slot_count, group_width = query_group.shape
    group_heads = HEADS // 2
    head_width = group_width // group_heads
    scale = 1.0 / math.sqrt(head_width)
    position = jnp.arange(slot_count)
    image_ids = jnp.where(image_ids < 0, -1 - position[None, :], image_ids)
    shaped_query = query_group.reshape(items, slot_count, group_heads, head_width)
    shaped_key = key_group.reshape(items, slot_count, group_heads, head_width)
    shaped_value = value_group.reshape(items, slot_count, group_heads, head_width)
    scores = (
        jnp.einsum("gqhd,gkhd->ghqk", shaped_query, shaped_key, preferred_element_type=jnp.float32)
        * scale
    )
    same_image = image_ids[:, None, :, None] == image_ids[:, None, None, :]
    scores = jnp.where(same_image, scores, -1e30)
    highest = jnp.max(scores, axis=-1, keepdims=True)
    weights = jnp.exp(scores - highest)
    probs = (weights / jnp.sum(weights, axis=-1, keepdims=True)).astype(jnp.bfloat16)
    mixed = jnp.einsum("ghqk,gkhd->gqhd", probs, shaped_value, preferred_element_type=jnp.float32)
    return mixed.reshape(items, slot_count, group_width).astype(jnp.bfloat16)


def routed_body(
    queries, key_vectors, value_vectors, residual, out_weight, cotangent, send_row, image_id
):
    row_count, full_width = queries.shape
    half_width = full_width // 2
    is_live = send_row < row_count
    source_row = jnp.minimum(send_row, row_count - 1)

    def arrange(data):
        grouped = data.reshape(row_count, 2, half_width).transpose(1, 0, 2)
        return jnp.where(is_live[None, :, None], grouped[:, source_row], jnp.zeros((), data.dtype))

    send_query = arrange(queries)
    send_key = arrange(key_vectors)
    send_value = arrange(value_vectors)
    send_image = jnp.where(is_live, image_id[source_row], -1)
    send_image = jnp.broadcast_to(send_image[None, :], (2, send_row.shape[0]))
    received = (
        lax.all_to_all(send_query, "enc", split_axis=1, concat_axis=1, tiled=True),
        lax.all_to_all(send_key, "enc", split_axis=1, concat_axis=1, tiled=True),
        lax.all_to_all(send_value, "enc", split_axis=1, concat_axis=1, tiled=True),
        lax.all_to_all(send_image, "enc", split_axis=1, concat_axis=1, tiled=True),
    )
    output = attend_groups(received[0], received[1], received[2], received[3])
    returned = lax.all_to_all(output, "enc", split_axis=1, concat_axis=1, tiled=True)
    holder = jnp.zeros((2, row_count + 1, half_width), jnp.bfloat16).at[:, send_row].set(returned)
    attended = holder[:, :row_count].transpose(1, 0, 2).reshape(row_count, full_width)
    projected = jnp.dot(attended, out_weight, preferred_element_type=jnp.float32)
    layer_out = (residual.astype(jnp.float32) + projected).astype(jnp.bfloat16)
    first_sum = lax.psum_scatter(
        lax.dot_general(
            attended, cotangent, (((0,), (0,)), ((), ())), preferred_element_type=jnp.float32
        ).astype(jnp.bfloat16),
        "dp",
        scatter_dimension=0,
        tiled=True,
    )
    second_sum = lax.psum_scatter(first_sum, "seq", scatter_dimension=0, tiled=True).astype(
        jnp.float32
    )
    grad_weight = lax.psum_scatter(second_sum, "enc", scatter_dimension=1, tiled=True)
    return (layer_out, grad_weight)


def solution(mesh):
    sizes = tuple(mesh.shape[name] for name in AXES)
    n_dp, n_enc, n_seq = sizes
    fits = n_seq == 2 and n_dp == n_enc == 4 and HEADS % (2 * n_enc) == 0
    body = functools.partial(exchange_body, sizes) if fits else routed_body
    placed = (
        P(("dp", "enc", "seq"), None),
        P(("dp", "enc", "seq"), None),
        P(("dp", "enc", "seq"), None),
        P(("dp", "enc", "seq"), None),
        P(),
        P(("dp", "enc", "seq"), None),
        P(("dp", "enc", "seq")),
        P(("dp", "enc", "seq")),
    )
    return jax.shard_map(
        body,
        mesh=mesh,
        in_specs=placed,
        out_specs=(P(("dp", "enc", "seq"), None), P(("dp", "seq"), "enc")),
        check_vma=False,
    )
```

```python
import functools
import math

import jax
import jax.numpy as jnp
from jax import lax
from jax.experimental import pallas as pl
from jax.experimental.pallas import tpu as pltpu
from jax.sharding import PartitionSpec as P

HEADS = 16
AXES = ("dp", "enc", "seq")
ID_ROWS = 16
ID_BASE = 64
SENDS = (0, 3, 1, 2)
RETURNS = (2, 3, 1, 0)
SUMS = (2, 3, 1, 0)


def call(
    kernel,
    out_shape,
    *args,
    spaces=None,
    scratch=(),
    limit=16,
    flops=0,
    bytes_accessed=0,
):
    def placed(space):
        return pl.BlockSpec(memory_space=space)

    many = isinstance(out_shape, (list, tuple))
    spaces = spaces or [pltpu.VMEM] * len(args)
    args = [
        pltpu.with_memory_space_constraint(arg, pltpu.HBM) if space == pltpu.HBM else arg
        for arg, space in zip(args, spaces)
    ]
    return pl.pallas_call(
        kernel,
        out_shape=out_shape,
        in_specs=[placed(space) for space in spaces],
        out_specs=[placed(pltpu.VMEM)] * len(out_shape) if many else placed(pltpu.VMEM),
        scratch_shapes=list(scratch),
        compiler_params=pltpu.CompilerParams(vmem_limit_bytes=limit * 1024 * 1024),
        cost_estimate=pl.CostEstimate(
            flops=flops, bytes_accessed=bytes_accessed, transcendentals=0
        ),
    )(*args)


def pack_kernel(block, *refs):
    sources, outs, (ready, held, arrived, ids_held, sems) = refs[:5], refs[5:-5], refs[-5:]
    targets = [ids_held] + [arrived.at[which] for which in range(3)] + [ready]
    copies = [
        pltpu.make_async_copy(source, target, sems.at[which])
        for which, (source, target) in enumerate(zip(sources, targets))
    ]
    for copy in copies:
        copy.start()
    first = lax.axis_index("dp") ^ lax.axis_index("enc")
    copies[0].wait()
    ids = ids_held[...]
    row = lax.broadcasted_iota(jnp.int32, (ID_ROWS, ids.shape[1]), 0)
    digits = jnp.where(row == 0, ids // ID_BASE, jnp.where(row == 1, ids % ID_BASE, 0))
    digits = digits.astype(jnp.float32).astype(jnp.bfloat16)
    for out in outs:
        out[3 * block :] = digits
    for which in range(3):
        copies[1 + which].wait()
        held[...] = arrived[which].T
        for hop, out in zip(SENDS, outs):
            begin = pl.multiple_of((first ^ hop) * block, 16)
            out[which * block : (which + 1) * block] = held[pl.ds(begin, block)]
    copies[4].wait()


def identifiers(slabs, block):
    numbers = []
    for slab in slabs:
        digits = slab[3 * block : 3 * block + ID_ROWS].astype(jnp.float32)
        numbers.append(digits[0:1] * ID_BASE + digits[1:2])
    return numbers


def set_bias(bias, key_ids, query_ids):
    queries = jnp.concatenate(query_ids, axis=1)
    for index, ids in enumerate(key_ids):
        rows = ids.shape[1]
        column = jnp.broadcast_to(ids, (rows, rows)).T
        column = jnp.concatenate([column] * len(query_ids), axis=1)
        bias[index * rows : (index + 1) * rows] = jnp.where(column == queries, 0.0, -1e30)


def gather(slabs, which, block, head, head_width):
    begin = which * block + head * head_width
    return jnp.concatenate([slab[begin : begin + head_width] for slab in slabs], axis=1)


def weigh(key, query, bias):
    scores = jnp.dot(key, query, preferred_element_type=jnp.float32) + bias
    return scores, jnp.max(scores, axis=0, keepdims=True)


def attend_first_kernel(block, head_width, *refs):
    slabs, (mixed, highest, total, turned, bias) = refs[:-5], refs[-5:]
    ids = identifiers(slabs, block)
    set_bias(bias, ids, ids)
    factor = math.log2(math.e) / math.sqrt(head_width)
    for head in range(block // head_width):
        query, key, value = (gather(slabs, which, block, head, head_width) for which in range(3))
        key = key.T
        turned[head] = key
        scores, top = weigh(key, query, bias[...])
        weights = jnp.exp2((scores - top) * factor)
        highest[head : head + 1] = top
        total[head : head + 1] = jnp.sum(weights, axis=0, keepdims=True)
        mixed[head * head_width : (head + 1) * head_width] = jnp.dot(
            value, weights.astype(jnp.bfloat16), preferred_element_type=jnp.float32
        )


def attend_last_kernel(block, head_width, *refs):
    count = len(SENDS)
    slabs, (mixed, highest, total, turned) = refs[:count], refs[count : count + 4]
    outs = refs[count + 4 : -2]
    old_bias, new_bias = refs[-2:]
    *early, late = slabs
    rows = late.shape[1]
    *early_ids, late_id = identifiers(slabs, block)
    set_bias(old_bias, [late_id], early_ids)
    set_bias(new_bias, early_ids + [late_id], [late_id])
    factor = math.log2(math.e) / math.sqrt(head_width)
    for head in range(block // head_width):
        span = slice(head * head_width, (head + 1) * head_width)
        query, value = (gather(early, which, block, head, head_width) for which in (0, 2))
        new_query, new_key, new_value = (
            gather([late], which, block, head, head_width) for which in range(3)
        )
        new_key = new_key.T
        scores, top = weigh(new_key, query, old_bias[...])
        before = highest[head : head + 1]
        top = jnp.maximum(top, before)
        weights = jnp.exp2((scores - top) * factor)
        shrink = jnp.exp2((before - top) * factor)
        sums = total[head : head + 1] * shrink + jnp.sum(weights, axis=0, keepdims=True)
        result = mixed[span] * shrink + jnp.dot(
            new_value, weights.astype(jnp.bfloat16), preferred_element_type=jnp.float32
        )
        result = (result / sums).astype(jnp.bfloat16)
        for index in range(count - 1):
            out = outs[RETURNS.index(SENDS[index])]
            out[span] = result[:, index * rows : (index + 1) * rows]
        scores, top = weigh(
            jnp.concatenate([turned[head], new_key], axis=0), new_query, new_bias[...]
        )
        weights = jnp.exp2((scores - top) * factor)
        sums = jnp.sum(weights, axis=0, keepdims=True)
        result = jnp.dot(
            jnp.concatenate([value, new_value], axis=1),
            weights.astype(jnp.bfloat16),
            preferred_element_type=jnp.float32,
        )
        outs[RETURNS.index(SENDS[-1])][span] = (result / sums).astype(jnp.bfloat16)


def stack_kernel(count, *refs):
    sources, out, sems = refs[:count], refs[-2], refs[-1]
    copies = [
        pltpu.make_async_copy(source, out.at[index], sems.at[index])
        for index, source in enumerate(sources)
    ]
    for copy in copies:
        copy.start()
    for copy in copies:
        copy.wait()


def halve_kernel(*refs):
    pieces, (kept, given) = refs[:-2], refs[-2:]
    s = lax.axis_index("seq")
    half = kept.shape[1]
    for hop, piece in zip(RETURNS, pieces):
        kept[hop] = piece[pl.ds(pl.multiple_of(s * half, 16), half)]
        given[hop] = piece[pl.ds(pl.multiple_of((1 - s) * half, 16), half)]


def gradient_kernel(count, *refs):
    kept, given, same, others, *outs = refs
    e = lax.axis_index("enc")
    features, rows = [], []
    for step in range(count):
        features += [kept[step], given[step]]
        rows += [same[step], others[step]]
    total = jnp.dot(
        jnp.concatenate(features, axis=1),
        jnp.concatenate(rows, axis=0),
        preferred_element_type=jnp.float32,
    )
    width, short = total.shape[1] // count, total.shape[0] // 2
    for target in range(count):
        block = total[:, target * width : (target + 1) * width]
        folded = jnp.concatenate([block[:short], block[short:]], axis=1).astype(jnp.bfloat16)

        for index, out in enumerate(outs):

            @pl.when(e ^ target == SUMS[index])
            def _():
                out[...] = folded


def project_kernel(*refs):
    pieces, (residual, weight, out, attended) = refs[:-4], refs[-4:]
    first = lax.axis_index("dp") ^ lax.axis_index("enc")
    block = pieces[0].shape[0]
    for hop, piece in zip(RETURNS, pieces):
        attended[pl.ds(pl.multiple_of((first ^ hop) * block, 16), block)] = piece[...]
    projected = lax.dot_general(
        attended[...], weight[...], (((0,), (0,)), ((), ())), preferred_element_type=jnp.float32
    )
    out[...] = (residual[...].astype(jnp.float32) + projected).astype(jnp.bfloat16)


def add_kernel(*refs):
    partial, out = refs[:-1], refs[-1]
    total = partial[0][...].astype(jnp.float32)
    for ref in partial[1:]:
        total = total + ref[...].astype(jnp.float32)
    short, width = total.shape[0], out.shape[1]
    out[:short] = total[:, :width]
    out[short:] = total[:, width:]


def exchange_body(
    sizes, queries, key_vectors, value_vectors, residual, out_weight, cotangent, send_row, image_id
):
    n_dp, n_enc, n_seq = sizes
    rows, width = queries.shape
    block = width // n_enc
    half = block // n_seq
    head_width = width // HEADS
    group = n_enc * rows
    tall = 3 * block + ID_ROWS
    bf16 = functools.partial(jax.ShapeDtypeStruct, dtype=jnp.bfloat16)
    hbm = pltpu.HBM

    def move(data, partner):
        pairs = []
        for d in range(n_dp):
            for e in range(n_enc):
                for s in range(n_seq):
                    to_d, to_e, to_s = partner(d, e, s)
                    pairs.append(
                        ((d * n_enc + e) * n_seq + s, (to_d * n_enc + to_e) * n_seq + to_s)
                    )
        return lax.ppermute(data, AXES, pairs)

    def along_enc(pieces, hops):
        return [
            move(piece, lambda d, e, s, hop=hop: (d, e ^ hop, s)) if hop else piece
            for hop, piece in zip(hops, pieces)
        ]

    def along_seq(data):
        return move(data, lambda d, e, s: (d, e, s ^ 1))

    with jax.named_scope("pack"):
        outs = call(
            functools.partial(pack_kernel, block),
            [bf16((tall, rows))] * n_enc + [bf16((rows, width))],
            image_id.reshape(1, rows),
            queries,
            key_vectors,
            value_vectors,
            cotangent,
            spaces=[hbm] * 5,
            scratch=[
                pltpu.VMEM((width, rows), jnp.bfloat16),
                pltpu.VMEM((3, rows, width), jnp.bfloat16),
                pltpu.VMEM((1, rows), jnp.int32),
                pltpu.SemaphoreType.DMA((5,)),
            ],
            bytes_accessed=8 * rows * width * 2,
        )
        slabs, cotangent = outs[:-1], outs[-1]
    with jax.named_scope("exchange_heads"):
        slabs = along_enc(slabs, SENDS)
    with jax.named_scope("gather_cotangent"):
        same = [cotangent] + [
            move(cotangent, lambda d, e, s, k=k: (d ^ k, e, s)) for k in range(1, n_dp)
        ]
    with jax.named_scope("attention"):
        known = group - rows
        f32 = functools.partial(jax.ShapeDtypeStruct, dtype=jnp.float32)
        state = call(
            functools.partial(attend_first_kernel, block, head_width),
            [
                f32((block, known)),
                f32((8, known)),
                f32((8, known)),
                bf16((block // head_width, known, head_width)),
            ],
            *slabs[:-1],
            scratch=[pltpu.VMEM((known, known), jnp.float32)],
            flops=55 * known * known * block,
            bytes_accessed=8 * group * block,
        )
        pieces = call(
            functools.partial(attend_last_kernel, block, head_width),
            [bf16((block, rows))] * n_enc,
            *slabs,
            *state,
            scratch=[pltpu.VMEM((rows, known), jnp.float32), pltpu.VMEM((group, rows), jnp.float32)],
            flops=55 * (group * group - known * known) * block,
            bytes_accessed=8 * group * block,
        )
    with jax.named_scope("send_to_owner"):
        pieces = [
            move(piece, lambda d, e, s, hop=hop: (d ^ hop, e ^ hop, s)) if hop else piece
            for hop, piece in zip(RETURNS, pieces)
        ]
        kept, given = call(
            halve_kernel,
            [bf16((n_dp, half, rows))] * 2,
            *pieces,
            flops=400 * group * group * half,
        )
        given = along_seq(given)
    with jax.named_scope("swap_cotangent"):
        stacked = call(
            functools.partial(stack_kernel, n_dp),
            bf16((n_dp, rows, width)),
            *same,
            spaces=[pltpu.VMEM] * n_dp + [pl.ANY] * 0,
            scratch=[pltpu.SemaphoreType.DMA((n_dp,))],
            bytes_accessed=4 * n_dp * rows * width,
        )
    with jax.named_scope("gradient"):
        partial = call(
            functools.partial(gradient_kernel, n_enc),
            [bf16((half // 2, 2 * block))] * n_enc,
            kept,
            given,
            stacked,
            along_seq(stacked),
            flops=2 * half * width * rows * n_dp * n_seq,
            bytes_accessed=2 * n_dp * n_seq * rows * width,
        )
    with jax.named_scope("sum_gradient"):
        partial = [
            move(part, lambda d, e, s, hop=hop: (d ^ e, e ^ hop, s))
            for hop, part in zip(SUMS, partial)
        ]
    with jax.named_scope("send_home"):
        homes = [
            move(piece, lambda d, e, s, hop=hop: (d ^ hop, e, s)) if hop else piece
            for hop, piece in zip(RETURNS, pieces)
        ]
    with jax.named_scope("project"):
        layer_out = call(
            project_kernel,
            bf16((rows, width)),
            *homes,
            residual,
            out_weight,
            scratch=[pltpu.VMEM((width, rows), jnp.bfloat16)],
            flops=2 * rows * width * width,
            bytes_accessed=2 * width * width,
        )
    with jax.named_scope("add_gradient"):
        grad_weight = call(
            add_kernel,
            jax.ShapeDtypeStruct((half, block), jnp.float32),
            *partial,
            bytes_accessed=4 * half * block * 4,
        )
    return (layer_out, grad_weight)


def attend_groups(query_group, key_group, value_group, image_ids):
    items, slot_count, group_width = query_group.shape
    group_heads = HEADS // 2
    head_width = group_width // group_heads
    scale = 1.0 / math.sqrt(head_width)
    position = jnp.arange(slot_count)
    image_ids = jnp.where(image_ids < 0, -1 - position[None, :], image_ids)
    shaped_query = query_group.reshape(items, slot_count, group_heads, head_width)
    shaped_key = key_group.reshape(items, slot_count, group_heads, head_width)
    shaped_value = value_group.reshape(items, slot_count, group_heads, head_width)
    scores = (
        jnp.einsum("gqhd,gkhd->ghqk", shaped_query, shaped_key, preferred_element_type=jnp.float32)
        * scale
    )
    same_image = image_ids[:, None, :, None] == image_ids[:, None, None, :]
    scores = jnp.where(same_image, scores, -1e30)
    highest = jnp.max(scores, axis=-1, keepdims=True)
    weights = jnp.exp(scores - highest)
    probs = (weights / jnp.sum(weights, axis=-1, keepdims=True)).astype(jnp.bfloat16)
    mixed = jnp.einsum("ghqk,gkhd->gqhd", probs, shaped_value, preferred_element_type=jnp.float32)
    return mixed.reshape(items, slot_count, group_width).astype(jnp.bfloat16)


def routed_body(
    queries, key_vectors, value_vectors, residual, out_weight, cotangent, send_row, image_id
):
    row_count, full_width = queries.shape
    half_width = full_width // 2
    is_live = send_row < row_count
    source_row = jnp.minimum(send_row, row_count - 1)

    def arrange(data):
        grouped = data.reshape(row_count, 2, half_width).transpose(1, 0, 2)
        return jnp.where(is_live[None, :, None], grouped[:, source_row], jnp.zeros((), data.dtype))

    send_query = arrange(queries)
    send_key = arrange(key_vectors)
    send_value = arrange(value_vectors)
    send_image = jnp.where(is_live, image_id[source_row], -1)
    send_image = jnp.broadcast_to(send_image[None, :], (2, send_row.shape[0]))
    received = (
        lax.all_to_all(send_query, "enc", split_axis=1, concat_axis=1, tiled=True),
        lax.all_to_all(send_key, "enc", split_axis=1, concat_axis=1, tiled=True),
        lax.all_to_all(send_value, "enc", split_axis=1, concat_axis=1, tiled=True),
        lax.all_to_all(send_image, "enc", split_axis=1, concat_axis=1, tiled=True),
    )
    output = attend_groups(received[0], received[1], received[2], received[3])
    returned = lax.all_to_all(output, "enc", split_axis=1, concat_axis=1, tiled=True)
    holder = jnp.zeros((2, row_count + 1, half_width), jnp.bfloat16).at[:, send_row].set(returned)
    attended = holder[:, :row_count].transpose(1, 0, 2).reshape(row_count, full_width)
    projected = jnp.dot(attended, out_weight, preferred_element_type=jnp.float32)
    layer_out = (residual.astype(jnp.float32) + projected).astype(jnp.bfloat16)
    first_sum = lax.psum_scatter(
        lax.dot_general(
            attended, cotangent, (((0,), (0,)), ((), ())), preferred_element_type=jnp.float32
        ).astype(jnp.bfloat16),
        "dp",
        scatter_dimension=0,
        tiled=True,
    )
    second_sum = lax.psum_scatter(first_sum, "seq", scatter_dimension=0, tiled=True).astype(
        jnp.float32
    )
    grad_weight = lax.psum_scatter(second_sum, "enc", scatter_dimension=1, tiled=True)
    return (layer_out, grad_weight)


def solution(mesh):
    sizes = tuple(mesh.shape[name] for name in AXES)
    n_dp, n_enc, n_seq = sizes
    fits = n_seq == 2 and n_dp == n_enc == 4 and HEADS % (2 * n_enc) == 0
    body = functools.partial(exchange_body, sizes) if fits else routed_body
    placed = (
        P(("dp", "enc", "seq"), None),
        P(("dp", "enc", "seq"), None),
        P(("dp", "enc", "seq"), None),
        P(("dp", "enc", "seq"), None),
        P(),
        P(("dp", "enc", "seq"), None),
        P(("dp", "enc", "seq")),
        P(("dp", "enc", "seq")),
    )
    return jax.shard_map(
        body,
        mesh=mesh,
        in_specs=placed,
        out_specs=(P(("dp", "enc", "seq"), None), P(("dp", "seq"), "enc")),
        check_vma=False,
    )
```

```python
import functools
import math

import jax
import jax.numpy as jnp
from jax import lax
from jax.experimental import pallas as pl
from jax.experimental.pallas import tpu as pltpu
from jax.sharding import PartitionSpec as P

HEADS = 16
AXES = ("dp", "enc", "seq")
ID_ROWS = 16
ID_BASE = 64
SENDS = (3, 0, 1, 2)
RETURNS = (2, 3, 1, 0)
SUMS = (2, 3, 1, 0)


def call(
    kernel,
    out_shape,
    *args,
    spaces=None,
    scratch=(),
    limit=16,
    flops=0,
    bytes_accessed=0,
):
    def placed(space):
        return pl.BlockSpec(memory_space=space)

    many = isinstance(out_shape, (list, tuple))
    spaces = spaces or [pltpu.VMEM] * len(args)
    args = [
        pltpu.with_memory_space_constraint(arg, pltpu.HBM) if space == pltpu.HBM else arg
        for arg, space in zip(args, spaces)
    ]
    return pl.pallas_call(
        kernel,
        out_shape=out_shape,
        in_specs=[placed(space) for space in spaces],
        out_specs=[placed(pltpu.VMEM)] * len(out_shape) if many else placed(pltpu.VMEM),
        scratch_shapes=list(scratch),
        compiler_params=pltpu.CompilerParams(vmem_limit_bytes=limit * 1024 * 1024),
        cost_estimate=pl.CostEstimate(
            flops=flops, bytes_accessed=bytes_accessed, transcendentals=0
        ),
    )(*args)


def pack_kernel(block, *refs):
    sources, outs, (ready, held, arrived, ids_held, sems) = refs[:5], refs[5:-5], refs[-5:]
    targets = [ids_held] + [arrived.at[which] for which in range(3)] + [ready]
    copies = [
        pltpu.make_async_copy(source, target, sems.at[which])
        for which, (source, target) in enumerate(zip(sources, targets))
    ]
    for copy in copies:
        copy.start()
    first = lax.axis_index("dp") ^ lax.axis_index("enc")
    copies[0].wait()
    ids = ids_held[...]
    row = lax.broadcasted_iota(jnp.int32, (ID_ROWS, ids.shape[1]), 0)
    digits = jnp.where(row == 0, ids // ID_BASE, jnp.where(row == 1, ids % ID_BASE, 0))
    digits = digits.astype(jnp.float32).astype(jnp.bfloat16)
    for out in outs:
        out[3 * block :] = digits
    for which in range(3):
        copies[1 + which].wait()
        held[...] = arrived[which].T
        for hop, out in zip(SENDS, outs):
            begin = pl.multiple_of((first ^ hop) * block, 16)
            out[which * block : (which + 1) * block] = held[pl.ds(begin, block)]
    copies[4].wait()


def identifiers(slabs, block):
    numbers = []
    for slab in slabs:
        digits = slab[3 * block : 3 * block + ID_ROWS].astype(jnp.float32)
        numbers.append(digits[0:1] * ID_BASE + digits[1:2])
    return numbers


def set_bias(bias, key_ids, query_ids):
    queries = jnp.concatenate(query_ids, axis=1)
    for index, ids in enumerate(key_ids):
        rows = ids.shape[1]
        column = jnp.broadcast_to(ids, (rows, rows)).T
        column = jnp.concatenate([column] * len(query_ids), axis=1)
        bias[index * rows : (index + 1) * rows] = jnp.where(column == queries, 0.0, -1e30)


def gather(slabs, which, block, head, head_width):
    begin = which * block + head * head_width
    return jnp.concatenate([slab[begin : begin + head_width] for slab in slabs], axis=1)


def weigh(key, query, bias):
    scores = lax.dot_general(
        key, query, (((0,), (0,)), ((), ())), preferred_element_type=jnp.float32
    )
    scores = scores + bias
    return scores, jnp.max(scores, axis=0, keepdims=True)


def attend_first_kernel(block, head_width, *refs):
    slabs, (mixed, highest, total, bias) = refs[:-4], refs[-4:]
    ids = identifiers(slabs, block)
    set_bias(bias, ids, ids)
    factor = math.log2(math.e) / math.sqrt(head_width)
    for head in range(block // head_width):
        query, key, value = (gather(slabs, which, block, head, head_width) for which in range(3))
        scores, top = weigh(key, query, bias[...])
        weights = jnp.exp2((scores - top) * factor)
        highest[head : head + 1] = top
        total[head : head + 1] = jnp.sum(weights, axis=0, keepdims=True)
        mixed[head * head_width : (head + 1) * head_width] = jnp.dot(
            value, weights.astype(jnp.bfloat16), preferred_element_type=jnp.float32
        )


def attend_more(early, late, state, bias, outs, first, head_width):
    mixed, highest, total = state
    block, rows = outs[0].shape
    columns = slice(first, first + len(early) * rows)
    set_bias(bias, identifiers([late], block), identifiers(early, block))
    factor = math.log2(math.e) / math.sqrt(head_width)
    for head in range(block // head_width):
        span = slice(head * head_width, (head + 1) * head_width)
        query = gather(early, 0, block, head, head_width)
        key, value = (gather([late], which, block, head, head_width) for which in (1, 2))
        scores, top = weigh(key, query, bias[...])
        before = highest[head : head + 1, columns]
        top = jnp.maximum(top, before)
        weights = jnp.exp2((scores - top) * factor)
        shrink = jnp.exp2((before - top) * factor)
        sums = total[head : head + 1, columns] * shrink
        sums = sums + jnp.sum(weights, axis=0, keepdims=True)
        result = mixed[span, columns] * shrink + jnp.dot(
            value, weights.astype(jnp.bfloat16), preferred_element_type=jnp.float32
        )
        result = (result / sums).astype(jnp.bfloat16)
        for index, out in enumerate(outs):
            out[span] = result[:, index * rows : (index + 1) * rows]


def attend_across_kernel(head_width, *refs):
    count = len(SENDS)
    slabs, state, (first, last, old_bias, bias) = refs[:count], refs[count:-4], refs[-4:]
    block = last.shape[0]
    ids = identifiers(slabs, block)
    set_bias(bias, ids, ids[-1:])
    factor = math.log2(math.e) / math.sqrt(head_width)
    for head in range(block // head_width):
        span = slice(head * head_width, (head + 1) * head_width)
        query = gather(slabs[-1:], 0, block, head, head_width)
        key, value = (gather(slabs, which, block, head, head_width) for which in (1, 2))
        scores, top = weigh(key, query, bias[...])
        weights = jnp.exp2((scores - top) * factor)
        sums = jnp.sum(weights, axis=0, keepdims=True)
        result = jnp.dot(value, weights.astype(jnp.bfloat16), preferred_element_type=jnp.float32)
        last[span] = (result / sums).astype(jnp.bfloat16)
    attend_more(slabs[:1], slabs[-1], state, old_bias, [first], 0, head_width)


def attend_rest_kernel(head_width, *refs):
    early, late, state, outs, bias = refs[:2], refs[2], refs[3:6], refs[6:8], refs[8]
    attend_more(early, late, state, bias, outs, late.shape[1], head_width)


def stack_kernel(count, *refs):
    sources, out, sems = refs[:count], refs[-2], refs[-1]
    copies = [
        pltpu.make_async_copy(source, out.at[index], sems.at[index])
        for index, source in enumerate(sources)
    ]
    for copy in copies:
        copy.start()
    for copy in copies:
        copy.wait()


def halve_kernel(*refs):
    pieces, (kept, given) = refs[:-2], refs[-2:]
    s = lax.axis_index("seq")
    half = kept.shape[1]
    for hop, piece in zip(RETURNS, pieces):
        kept[hop] = piece[pl.ds(pl.multiple_of(s * half, 16), half)]
        given[hop] = piece[pl.ds(pl.multiple_of((1 - s) * half, 16), half)]


def gradient_kernel(count, *refs):
    kept, given, same, others, *outs = refs
    e = lax.axis_index("enc")
    features, rows = [], []
    for step in range(count):
        features += [kept[step], given[step]]
        rows += [same[step], others[step]]
    total = jnp.dot(
        jnp.concatenate(features, axis=1),
        jnp.concatenate(rows, axis=0),
        preferred_element_type=jnp.float32,
    )
    width, short = total.shape[1] // count, total.shape[0] // 2
    for target in range(count):
        block = total[:, target * width : (target + 1) * width]
        folded = jnp.concatenate([block[:short], block[short:]], axis=1).astype(jnp.bfloat16)

        for index, out in enumerate(outs):

            @pl.when(e ^ target == SUMS[index])
            def _():
                out[...] = folded


def project_kernel(*refs):
    pieces, (residual, weight, out, attended) = refs[:-4], refs[-4:]
    first = lax.axis_index("dp") ^ lax.axis_index("enc")
    block = pieces[0].shape[0]
    for hop, piece in zip(RETURNS, pieces):
        attended[pl.ds(pl.multiple_of((first ^ hop) * block, 16), block)] = piece[...]
    projected = lax.dot_general(
        attended[...], weight[...], (((0,), (0,)), ((), ())), preferred_element_type=jnp.float32
    )
    out[...] = (residual[...].astype(jnp.float32) + projected).astype(jnp.bfloat16)


def add_kernel(*refs):
    partial, out = refs[:-1], refs[-1]
    total = partial[0][...].astype(jnp.float32)
    for ref in partial[1:]:
        total = total + ref[...].astype(jnp.float32)
    short, width = total.shape[0], out.shape[1]
    out[:short] = total[:, :width]
    out[short:] = total[:, width:]


def exchange_body(
    sizes, queries, key_vectors, value_vectors, residual, out_weight, cotangent, send_row, image_id
):
    n_dp, n_enc, n_seq = sizes
    rows, width = queries.shape
    block = width // n_enc
    half = block // n_seq
    head_width = width // HEADS
    group = n_enc * rows
    tall = 3 * block + ID_ROWS
    bf16 = functools.partial(jax.ShapeDtypeStruct, dtype=jnp.bfloat16)
    hbm = pltpu.HBM

    def move(data, partner):
        pairs = []
        for d in range(n_dp):
            for e in range(n_enc):
                for s in range(n_seq):
                    to_d, to_e, to_s = partner(d, e, s)
                    pairs.append(
                        ((d * n_enc + e) * n_seq + s, (to_d * n_enc + to_e) * n_seq + to_s)
                    )
        return lax.ppermute(data, AXES, pairs)

    def along_enc(pieces, hops):
        return [
            move(piece, lambda d, e, s, hop=hop: (d, e ^ hop, s)) if hop else piece
            for hop, piece in zip(hops, pieces)
        ]

    def along_seq(data):
        return move(data, lambda d, e, s: (d, e, s ^ 1))

    with jax.named_scope("pack"):
        outs = call(
            functools.partial(pack_kernel, block),
            [bf16((tall, rows))] * n_enc + [bf16((rows, width))],
            image_id.reshape(1, rows),
            queries,
            key_vectors,
            value_vectors,
            cotangent,
            spaces=[hbm] * 5,
            scratch=[
                pltpu.VMEM((width, rows), jnp.bfloat16),
                pltpu.VMEM((3, rows, width), jnp.bfloat16),
                pltpu.VMEM((1, rows), jnp.int32),
                pltpu.SemaphoreType.DMA((5,)),
            ],
            bytes_accessed=8 * rows * width * 2,
        )
        slabs, cotangent = outs[:-1], outs[-1]
    with jax.named_scope("exchange_heads"):
        slabs = along_enc(slabs, SENDS)
    with jax.named_scope("gather_cotangent"):
        same = [cotangent] + [
            move(cotangent, lambda d, e, s, k=k: (d ^ k, e, s)) for k in range(1, n_dp)
        ]
    with jax.named_scope("attention"):
        known = group - rows
        f32 = functools.partial(jax.ShapeDtypeStruct, dtype=jnp.float32)
        state = call(
            functools.partial(attend_first_kernel, block, head_width),
            [f32((block, known)), f32((8, known)), f32((8, known))],
            *slabs[:-1],
            scratch=[pltpu.VMEM((known, known), jnp.float32)],
            flops=55 * known * known * block,
            bytes_accessed=8 * group * block,
        )
        across = call(
            functools.partial(attend_across_kernel, head_width),
            [bf16((block, rows))] * 2,
            *slabs,
            *state,
            scratch=[pltpu.VMEM((rows, rows), jnp.float32), pltpu.VMEM((group, rows), jnp.float32)],
            flops=55 * rows * (rows + group) * block,
            bytes_accessed=8 * group * block,
        )
        rest = call(
            functools.partial(attend_rest_kernel, head_width),
            [bf16((block, rows))] * 2,
            *slabs[1:],
            *state,
            scratch=[pltpu.VMEM((rows, 2 * rows), jnp.float32)],
            flops=55 * rows * 2 * rows * block,
            bytes_accessed=8 * group * block,
        )
        pieces = dict(zip(SENDS, [across[0], *rest, across[1]]))
        pieces = [pieces[hop] for hop in RETURNS]
    with jax.named_scope("send_to_owner"):
        pieces = [
            move(piece, lambda d, e, s, hop=hop: (d ^ hop, e ^ hop, s)) if hop else piece
            for hop, piece in zip(RETURNS, pieces)
        ]
        kept, given = call(
            halve_kernel,
            [bf16((n_dp, half, rows))] * 2,
            *pieces,
            flops=400 * group * group * half,
        )
        given = along_seq(given)
    with jax.named_scope("swap_cotangent"):
        stacked = call(
            functools.partial(stack_kernel, n_dp),
            bf16((n_dp, rows, width)),
            *same,
            spaces=[pltpu.VMEM] * n_dp + [pl.ANY] * 0,
            scratch=[pltpu.SemaphoreType.DMA((n_dp,))],
            bytes_accessed=4 * n_dp * rows * width,
        )
    with jax.named_scope("gradient"):
        partial = call(
            functools.partial(gradient_kernel, n_enc),
            [bf16((half // 2, 2 * block))] * n_enc,
            kept,
            given,
            stacked,
            along_seq(stacked),
            flops=2 * half * width * rows * n_dp * n_seq,
            bytes_accessed=2 * n_dp * n_seq * rows * width,
        )
    with jax.named_scope("sum_gradient"):
        partial = [
            move(part, lambda d, e, s, hop=hop: (d ^ e, e ^ hop, s))
            for hop, part in zip(SUMS, partial)
        ]
    with jax.named_scope("send_home"):
        homes = [
            move(piece, lambda d, e, s, hop=hop: (d ^ hop, e, s)) if hop else piece
            for hop, piece in zip(RETURNS, pieces)
        ]
    with jax.named_scope("project"):
        layer_out = call(
            project_kernel,
            bf16((rows, width)),
            *homes,
            residual,
            out_weight,
            scratch=[pltpu.VMEM((width, rows), jnp.bfloat16)],
            flops=2 * rows * width * width,
            bytes_accessed=2 * width * width,
        )
    with jax.named_scope("add_gradient"):
        grad_weight = call(
            add_kernel,
            jax.ShapeDtypeStruct((half, block), jnp.float32),
            *partial,
            bytes_accessed=4 * half * block * 4,
        )
    return (layer_out, grad_weight)


def attend_groups(query_group, key_group, value_group, image_ids):
    items, slot_count, group_width = query_group.shape
    group_heads = HEADS // 2
    head_width = group_width // group_heads
    scale = 1.0 / math.sqrt(head_width)
    position = jnp.arange(slot_count)
    image_ids = jnp.where(image_ids < 0, -1 - position[None, :], image_ids)
    shaped_query = query_group.reshape(items, slot_count, group_heads, head_width)
    shaped_key = key_group.reshape(items, slot_count, group_heads, head_width)
    shaped_value = value_group.reshape(items, slot_count, group_heads, head_width)
    scores = (
        jnp.einsum("gqhd,gkhd->ghqk", shaped_query, shaped_key, preferred_element_type=jnp.float32)
        * scale
    )
    same_image = image_ids[:, None, :, None] == image_ids[:, None, None, :]
    scores = jnp.where(same_image, scores, -1e30)
    highest = jnp.max(scores, axis=-1, keepdims=True)
    weights = jnp.exp(scores - highest)
    probs = (weights / jnp.sum(weights, axis=-1, keepdims=True)).astype(jnp.bfloat16)
    mixed = jnp.einsum("ghqk,gkhd->gqhd", probs, shaped_value, preferred_element_type=jnp.float32)
    return mixed.reshape(items, slot_count, group_width).astype(jnp.bfloat16)


def routed_body(
    queries, key_vectors, value_vectors, residual, out_weight, cotangent, send_row, image_id
):
    row_count, full_width = queries.shape
    half_width = full_width // 2
    is_live = send_row < row_count
    source_row = jnp.minimum(send_row, row_count - 1)

    def arrange(data):
        grouped = data.reshape(row_count, 2, half_width).transpose(1, 0, 2)
        return jnp.where(is_live[None, :, None], grouped[:, source_row], jnp.zeros((), data.dtype))

    send_query = arrange(queries)
    send_key = arrange(key_vectors)
    send_value = arrange(value_vectors)
    send_image = jnp.where(is_live, image_id[source_row], -1)
    send_image = jnp.broadcast_to(send_image[None, :], (2, send_row.shape[0]))
    received = (
        lax.all_to_all(send_query, "enc", split_axis=1, concat_axis=1, tiled=True),
        lax.all_to_all(send_key, "enc", split_axis=1, concat_axis=1, tiled=True),
        lax.all_to_all(send_value, "enc", split_axis=1, concat_axis=1, tiled=True),
        lax.all_to_all(send_image, "enc", split_axis=1, concat_axis=1, tiled=True),
    )
    output = attend_groups(received[0], received[1], received[2], received[3])
    returned = lax.all_to_all(output, "enc", split_axis=1, concat_axis=1, tiled=True)
    holder = jnp.zeros((2, row_count + 1, half_width), jnp.bfloat16).at[:, send_row].set(returned)
    attended = holder[:, :row_count].transpose(1, 0, 2).reshape(row_count, full_width)
    projected = jnp.dot(attended, out_weight, preferred_element_type=jnp.float32)
    layer_out = (residual.astype(jnp.float32) + projected).astype(jnp.bfloat16)
    first_sum = lax.psum_scatter(
        lax.dot_general(
            attended, cotangent, (((0,), (0,)), ((), ())), preferred_element_type=jnp.float32
        ).astype(jnp.bfloat16),
        "dp",
        scatter_dimension=0,
        tiled=True,
    )
    second_sum = lax.psum_scatter(first_sum, "seq", scatter_dimension=0, tiled=True).astype(
        jnp.float32
    )
    grad_weight = lax.psum_scatter(second_sum, "enc", scatter_dimension=1, tiled=True)
    return (layer_out, grad_weight)


def solution(mesh):
    sizes = tuple(mesh.shape[name] for name in AXES)
    n_dp, n_enc, n_seq = sizes
    fits = n_seq == 2 and n_dp == n_enc == 4 and HEADS % (2 * n_enc) == 0
    body = functools.partial(exchange_body, sizes) if fits else routed_body
    placed = (
        P(("dp", "enc", "seq"), None),
        P(("dp", "enc", "seq"), None),
        P(("dp", "enc", "seq"), None),
        P(("dp", "enc", "seq"), None),
        P(),
        P(("dp", "enc", "seq"), None),
        P(("dp", "enc", "seq")),
        P(("dp", "enc", "seq")),
    )
    return jax.shard_map(
        body,
        mesh=mesh,
        in_specs=placed,
        out_specs=(P(("dp", "enc", "seq"), None), P(("dp", "seq"), "enc")),
        check_vma=False,
    )
```

```python
import functools
import math

import jax
import jax.numpy as jnp
from jax import lax
from jax.experimental import pallas as pl
from jax.experimental.pallas import tpu as pltpu
from jax.sharding import PartitionSpec as P

HEADS = 16
AXES = ("dp", "enc", "seq")
ID_ROWS = 16
ID_BASE = 64
SENDS = (3, 0, 1, 2)
RETURNS = (2, 3, 1, 0)
SUMS = (2, 3, 1, 0)
TURN = (0, 3, 2, 1)


def call(
    kernel,
    out_shape,
    *args,
    spaces=None,
    scratch=(),
    limit=16,
    flops=0,
    bytes_accessed=0,
):
    def placed(space):
        return pl.BlockSpec(memory_space=space)

    many = isinstance(out_shape, (list, tuple))
    spaces = spaces or [pltpu.VMEM] * len(args)
    args = [
        pltpu.with_memory_space_constraint(arg, pltpu.HBM) if space == pltpu.HBM else arg
        for arg, space in zip(args, spaces)
    ]
    return pl.pallas_call(
        kernel,
        out_shape=out_shape,
        in_specs=[placed(space) for space in spaces],
        out_specs=[placed(pltpu.VMEM)] * len(out_shape) if many else placed(pltpu.VMEM),
        scratch_shapes=list(scratch),
        compiler_params=pltpu.CompilerParams(vmem_limit_bytes=limit * 1024 * 1024),
        cost_estimate=pl.CostEstimate(
            flops=flops, bytes_accessed=bytes_accessed, transcendentals=0
        ),
    )(*args)


def pack_kernel(block, *refs):
    sources, outs, (ready, held, arrived, ids_held, sems) = refs[:5], refs[5:-5], refs[-5:]
    targets = [ids_held] + [arrived.at[which] for which in range(3)] + [ready]
    copies = [
        pltpu.make_async_copy(source, target, sems.at[which])
        for which, (source, target) in enumerate(zip(sources, targets))
    ]
    for copy in copies:
        copy.start()
    first = lax.axis_index("dp") ^ ((4 - lax.axis_index("enc")) & 3)
    copies[0].wait()
    ids = ids_held[...]
    row = lax.broadcasted_iota(jnp.int32, (ID_ROWS, ids.shape[1]), 0)
    digits = jnp.where(row == 0, ids // ID_BASE, jnp.where(row == 1, ids % ID_BASE, 0))
    digits = digits.astype(jnp.float32).astype(jnp.bfloat16)
    for out in outs:
        out[3 * block :] = digits
    for which in range(3):
        copies[1 + which].wait()
        held[...] = arrived[which].T
        for hop, out in zip(SENDS, outs):
            begin = pl.multiple_of((first ^ TURN[hop]) * block, 16)
            out[which * block : (which + 1) * block] = held[pl.ds(begin, block)]
    copies[4].wait()


def identifiers(slabs, block):
    numbers = []
    for slab in slabs:
        digits = slab[3 * block : 3 * block + ID_ROWS].astype(jnp.float32)
        numbers.append(digits[0:1] * ID_BASE + digits[1:2])
    return numbers


def set_bias(bias, key_ids, query_ids):
    queries = jnp.concatenate(query_ids, axis=1)
    for index, ids in enumerate(key_ids):
        rows = ids.shape[1]
        column = jnp.broadcast_to(ids, (rows, rows)).T
        column = jnp.concatenate([column] * len(query_ids), axis=1)
        bias[index * rows : (index + 1) * rows] = jnp.where(column == queries, 0.0, -1e30)


def gather(slabs, which, block, head, head_width):
    begin = which * block + head * head_width
    return jnp.concatenate([slab[begin : begin + head_width] for slab in slabs], axis=1)


def weigh(key, query, bias):
    scores = lax.dot_general(
        key, query, (((0,), (0,)), ((), ())), preferred_element_type=jnp.float32
    )
    scores = scores + bias
    return scores, jnp.max(scores, axis=0, keepdims=True)


def attend_first_kernel(block, head_width, *refs):
    slabs, (mixed, highest, total, bias) = refs[:-4], refs[-4:]
    ids = identifiers(slabs, block)
    set_bias(bias, ids, ids)
    factor = math.log2(math.e) / math.sqrt(head_width)
    for head in range(block // head_width):
        query, key, value = (gather(slabs, which, block, head, head_width) for which in range(3))
        scores, top = weigh(key, query, bias[...])
        weights = jnp.exp2((scores - top) * factor)
        highest[head : head + 1] = top
        total[head : head + 1] = jnp.sum(weights, axis=0, keepdims=True)
        mixed[head * head_width : (head + 1) * head_width] = jnp.dot(
            value, weights.astype(jnp.bfloat16), preferred_element_type=jnp.float32
        )


def attend_more(early, late, state, bias, outs, first, head_width):
    mixed, highest, total = state
    block, rows = outs[0].shape
    columns = slice(first, first + len(early) * rows)
    set_bias(bias, identifiers([late], block), identifiers(early, block))
    factor = math.log2(math.e) / math.sqrt(head_width)
    for head in range(block // head_width):
        span = slice(head * head_width, (head + 1) * head_width)
        query = gather(early, 0, block, head, head_width)
        key, value = (gather([late], which, block, head, head_width) for which in (1, 2))
        scores, top = weigh(key, query, bias[...])
        before = highest[head : head + 1, columns]
        top = jnp.maximum(top, before)
        weights = jnp.exp2((scores - top) * factor)
        shrink = jnp.exp2((before - top) * factor)
        sums = total[head : head + 1, columns] * shrink
        sums = sums + jnp.sum(weights, axis=0, keepdims=True)
        result = mixed[span, columns] * shrink + jnp.dot(
            value, weights.astype(jnp.bfloat16), preferred_element_type=jnp.float32
        )
        result = (result / sums).astype(jnp.bfloat16)
        for index, out in enumerate(outs):
            out[span] = result[:, index * rows : (index + 1) * rows]


def attend_across_kernel(head_width, *refs):
    count = len(SENDS)
    slabs, state, (first, last, old_bias, bias) = refs[:count], refs[count:-4], refs[-4:]
    block = last.shape[0]
    ids = identifiers(slabs, block)
    set_bias(bias, ids, ids[-1:])
    factor = math.log2(math.e) / math.sqrt(head_width)
    for head in range(block // head_width):
        span = slice(head * head_width, (head + 1) * head_width)
        query = gather(slabs[-1:], 0, block, head, head_width)
        key, value = (gather(slabs, which, block, head, head_width) for which in (1, 2))
        scores, top = weigh(key, query, bias[...])
        weights = jnp.exp2((scores - top) * factor)
        sums = jnp.sum(weights, axis=0, keepdims=True)
        result = jnp.dot(value, weights.astype(jnp.bfloat16), preferred_element_type=jnp.float32)
        last[span] = (result / sums).astype(jnp.bfloat16)
    attend_more(slabs[:1], slabs[-1], state, old_bias, [first], 0, head_width)


def attend_one_kernel(head_width, first, early, late, *refs):
    state, (out, bias) = refs[:3], refs[3:]
    attend_more([early], late, state, bias, [out], first, head_width)


def stack_kernel(count, *refs):
    sources, out, sems = refs[:count], refs[-2], refs[-1]
    copies = [
        pltpu.make_async_copy(source, out.at[index], sems.at[index])
        for index, source in enumerate(sources)
    ]
    for copy in copies:
        copy.start()
    for copy in copies:
        copy.wait()


def halve_kernel(*refs):
    pieces, (kept, given) = refs[:-2], refs[-2:]
    s = lax.axis_index("seq")
    half = kept.shape[1]
    for hop, piece in zip(RETURNS, pieces):
        kept[TURN[hop]] = piece[pl.ds(pl.multiple_of(s * half, 16), half)]
        given[TURN[hop]] = piece[pl.ds(pl.multiple_of((1 - s) * half, 16), half)]


def gradient_kernel(count, *refs):
    kept, given, same, others, *outs = refs
    e = lax.axis_index("enc")
    features, rows = [], []
    for step in range(count):
        features += [kept[step], given[step]]
        rows += [same[step], others[step]]
    total = jnp.dot(
        jnp.concatenate(features, axis=1),
        jnp.concatenate(rows, axis=0),
        preferred_element_type=jnp.float32,
    )
    width, short = total.shape[1] // count, total.shape[0] // 2
    for target in range(count):
        block = total[:, target * width : (target + 1) * width]
        folded = jnp.concatenate([block[:short], block[short:]], axis=1).astype(jnp.bfloat16)

        for index, out in enumerate(outs):

            @pl.when(e ^ target == SUMS[index])
            def _():
                out[...] = folded


def project_kernel(*refs):
    pieces, (residual, weight, out, attended) = refs[:-4], refs[-4:]
    first = lax.axis_index("dp") ^ ((4 - lax.axis_index("enc")) & 3)
    block = pieces[0].shape[0]
    for hop, piece in zip(RETURNS, pieces):
        attended[pl.ds(pl.multiple_of((first ^ TURN[hop]) * block, 16), block)] = piece[...]
    projected = lax.dot_general(
        attended[...], weight[...], (((0,), (0,)), ((), ())), preferred_element_type=jnp.float32
    )
    out[...] = (residual[...].astype(jnp.float32) + projected).astype(jnp.bfloat16)


def add_kernel(*refs):
    partial, out = refs[:-1], refs[-1]
    total = partial[0][...].astype(jnp.float32)
    for ref in partial[1:]:
        total = total + ref[...].astype(jnp.float32)
    short, width = total.shape[0], out.shape[1]
    out[:short] = total[:, :width]
    out[short:] = total[:, width:]


def exchange_body(
    sizes, queries, key_vectors, value_vectors, residual, out_weight, cotangent, send_row, image_id
):
    n_dp, n_enc, n_seq = sizes
    rows, width = queries.shape
    block = width // n_enc
    half = block // n_seq
    head_width = width // HEADS
    group = n_enc * rows
    tall = 3 * block + ID_ROWS
    bf16 = functools.partial(jax.ShapeDtypeStruct, dtype=jnp.bfloat16)
    hbm = pltpu.HBM

    def move(data, partner):
        pairs = []
        for d in range(n_dp):
            for e in range(n_enc):
                for s in range(n_seq):
                    to_d, to_e, to_s = partner(d, e, s)
                    pairs.append(
                        ((d * n_enc + e) * n_seq + s, (to_d * n_enc + to_e) * n_seq + to_s)
                    )
        return lax.ppermute(data, AXES, pairs)

    def along_enc(pieces, hops):
        return [
            move(piece, lambda d, e, s, hop=hop: (d, e ^ hop, s)) if hop else piece
            for hop, piece in zip(hops, pieces)
        ]

    def along_seq(data):
        return move(data, lambda d, e, s: (d, e, s ^ 1))

    with jax.named_scope("pack"):
        outs = call(
            functools.partial(pack_kernel, block),
            [bf16((tall, rows))] * n_enc + [bf16((rows, width))],
            image_id.reshape(1, rows),
            queries,
            key_vectors,
            value_vectors,
            cotangent,
            spaces=[hbm] * 5,
            scratch=[
                pltpu.VMEM((width, rows), jnp.bfloat16),
                pltpu.VMEM((3, rows, width), jnp.bfloat16),
                pltpu.VMEM((1, rows), jnp.int32),
                pltpu.SemaphoreType.DMA((5,)),
            ],
            bytes_accessed=8 * rows * width * 2,
        )
        slabs, cotangent = outs[:-1], outs[-1]
    with jax.named_scope("exchange_heads"):
        slabs = along_enc(slabs, SENDS)
    with jax.named_scope("gather_cotangent"):
        same = [cotangent] + [
            move(cotangent, lambda d, e, s, k=k: (d ^ k, e, s)) for k in range(1, n_dp)
        ]
    with jax.named_scope("attention"):
        known = group - rows
        f32 = functools.partial(jax.ShapeDtypeStruct, dtype=jnp.float32)
        state = call(
            functools.partial(attend_first_kernel, block, head_width),
            [f32((block, known)), f32((8, known)), f32((8, known))],
            *slabs[:-1],
            scratch=[pltpu.VMEM((known, known), jnp.float32)],
            flops=55 * known * known * block,
            bytes_accessed=8 * group * block,
        )
        across = call(
            functools.partial(attend_across_kernel, head_width),
            [bf16((block, rows))] * 2,
            *slabs,
            *state,
            scratch=[pltpu.VMEM((rows, rows), jnp.float32), pltpu.VMEM((group, rows), jnp.float32)],
            flops=55 * rows * (rows + group) * block,
            bytes_accessed=8 * group * block,
        )
        rest = [
            call(
                functools.partial(attend_one_kernel, head_width, index * rows),
                bf16((block, rows)),
                slabs[index],
                slabs[-1],
                *state,
                scratch=[pltpu.VMEM((rows, rows), jnp.float32)],
                flops=55 * rows * rows * block,
                bytes_accessed=8 * rows * block,
            )
            for index in (1, 2)
        ]
        pieces = dict(zip(SENDS, [across[0], *rest, across[1]]))
        pieces = [pieces[hop] for hop in RETURNS]
    with jax.named_scope("send_to_owner"):
        pieces = [
            move(piece, lambda d, e, s, hop=hop: (d ^ TURN[hop], e ^ hop, s)) if hop else piece
            for hop, piece in zip(RETURNS, pieces)
        ]
        kept, given = call(
            halve_kernel,
            [bf16((n_dp, half, rows))] * 2,
            *pieces,
            flops=400 * group * group * half,
        )
        given = along_seq(given)
    with jax.named_scope("swap_cotangent"):
        stacked = call(
            functools.partial(stack_kernel, n_dp),
            bf16((n_dp, rows, width)),
            *same,
            spaces=[pltpu.VMEM] * n_dp + [pl.ANY] * 0,
            scratch=[pltpu.SemaphoreType.DMA((n_dp,))],
            bytes_accessed=4 * n_dp * rows * width,
        )
    with jax.named_scope("gradient"):
        partial = call(
            functools.partial(gradient_kernel, n_enc),
            [bf16((half // 2, 2 * block))] * n_enc,
            kept,
            given,
            stacked,
            along_seq(stacked),
            flops=2 * half * width * rows * n_dp * n_seq,
            bytes_accessed=2 * n_dp * n_seq * rows * width,
        )
    with jax.named_scope("sum_gradient"):
        partial = [
            move(part, lambda d, e, s, hop=hop: (d ^ TURN[e], e ^ hop, s))
            for hop, part in zip(SUMS, partial)
        ]
    with jax.named_scope("send_home"):
        homes = [
            move(piece, lambda d, e, s, hop=hop: (d ^ TURN[hop], e, s)) if hop else piece
            for hop, piece in zip(RETURNS, pieces)
        ]
    with jax.named_scope("project"):
        layer_out = call(
            project_kernel,
            bf16((rows, width)),
            *homes,
            residual,
            out_weight,
            scratch=[pltpu.VMEM((width, rows), jnp.bfloat16)],
            flops=2 * rows * width * width,
            bytes_accessed=2 * width * width,
        )
    with jax.named_scope("add_gradient"):
        grad_weight = call(
            add_kernel,
            jax.ShapeDtypeStruct((half, block), jnp.float32),
            *partial,
            bytes_accessed=4 * half * block * 4,
        )
    return (layer_out, grad_weight)


def attend_groups(query_group, key_group, value_group, image_ids):
    items, slot_count, group_width = query_group.shape
    group_heads = HEADS // 2
    head_width = group_width // group_heads
    scale = 1.0 / math.sqrt(head_width)
    position = jnp.arange(slot_count)
    image_ids = jnp.where(image_ids < 0, -1 - position[None, :], image_ids)
    shaped_query = query_group.reshape(items, slot_count, group_heads, head_width)
    shaped_key = key_group.reshape(items, slot_count, group_heads, head_width)
    shaped_value = value_group.reshape(items, slot_count, group_heads, head_width)
    scores = (
        jnp.einsum("gqhd,gkhd->ghqk", shaped_query, shaped_key, preferred_element_type=jnp.float32)
        * scale
    )
    same_image = image_ids[:, None, :, None] == image_ids[:, None, None, :]
    scores = jnp.where(same_image, scores, -1e30)
    highest = jnp.max(scores, axis=-1, keepdims=True)
    weights = jnp.exp(scores - highest)
    probs = (weights / jnp.sum(weights, axis=-1, keepdims=True)).astype(jnp.bfloat16)
    mixed = jnp.einsum("ghqk,gkhd->gqhd", probs, shaped_value, preferred_element_type=jnp.float32)
    return mixed.reshape(items, slot_count, group_width).astype(jnp.bfloat16)


def routed_body(
    queries, key_vectors, value_vectors, residual, out_weight, cotangent, send_row, image_id
):
    row_count, full_width = queries.shape
    half_width = full_width // 2
    is_live = send_row < row_count
    source_row = jnp.minimum(send_row, row_count - 1)

    def arrange(data):
        grouped = data.reshape(row_count, 2, half_width).transpose(1, 0, 2)
        return jnp.where(is_live[None, :, None], grouped[:, source_row], jnp.zeros((), data.dtype))

    send_query = arrange(queries)
    send_key = arrange(key_vectors)
    send_value = arrange(value_vectors)
    send_image = jnp.where(is_live, image_id[source_row], -1)
    send_image = jnp.broadcast_to(send_image[None, :], (2, send_row.shape[0]))
    received = (
        lax.all_to_all(send_query, "enc", split_axis=1, concat_axis=1, tiled=True),
        lax.all_to_all(send_key, "enc", split_axis=1, concat_axis=1, tiled=True),
        lax.all_to_all(send_value, "enc", split_axis=1, concat_axis=1, tiled=True),
        lax.all_to_all(send_image, "enc", split_axis=1, concat_axis=1, tiled=True),
    )
    output = attend_groups(received[0], received[1], received[2], received[3])
    returned = lax.all_to_all(output, "enc", split_axis=1, concat_axis=1, tiled=True)
    holder = jnp.zeros((2, row_count + 1, half_width), jnp.bfloat16).at[:, send_row].set(returned)
    attended = holder[:, :row_count].transpose(1, 0, 2).reshape(row_count, full_width)
    projected = jnp.dot(attended, out_weight, preferred_element_type=jnp.float32)
    layer_out = (residual.astype(jnp.float32) + projected).astype(jnp.bfloat16)
    first_sum = lax.psum_scatter(
        lax.dot_general(
            attended, cotangent, (((0,), (0,)), ((), ())), preferred_element_type=jnp.float32
        ).astype(jnp.bfloat16),
        "dp",
        scatter_dimension=0,
        tiled=True,
    )
    second_sum = lax.psum_scatter(first_sum, "seq", scatter_dimension=0, tiled=True).astype(
        jnp.float32
    )
    grad_weight = lax.psum_scatter(second_sum, "enc", scatter_dimension=1, tiled=True)
    return (layer_out, grad_weight)


def solution(mesh):
    sizes = tuple(mesh.shape[name] for name in AXES)
    n_dp, n_enc, n_seq = sizes
    fits = n_seq == 2 and n_dp == n_enc == 4 and HEADS % (2 * n_enc) == 0
    body = functools.partial(exchange_body, sizes) if fits else routed_body
    placed = (
        P(("dp", "enc", "seq"), None),
        P(("dp", "enc", "seq"), None),
        P(("dp", "enc", "seq"), None),
        P(("dp", "enc", "seq"), None),
        P(),
        P(("dp", "enc", "seq"), None),
        P(("dp", "enc", "seq")),
        P(("dp", "enc", "seq")),
    )
    return jax.shard_map(
        body,
        mesh=mesh,
        in_specs=placed,
        out_specs=(P(("dp", "enc", "seq"), None), P(("dp", "seq"), "enc")),
        check_vma=False,
    )
```

```python
import functools
import math

import jax
import jax.numpy as jnp
from jax import lax
from jax.experimental import pallas as pl
from jax.experimental.pallas import tpu as pltpu
from jax.sharding import PartitionSpec as P

HEADS = 16
AXES = ("dp", "enc", "seq")
ID_ROWS = 16
ID_BASE = 64
SENDS = (3, 0, 1, 2)
RETURNS = (2, 3, 1, 0)
SUMS = (2, 3, 1, 0)


def call(
    kernel,
    out_shape,
    *args,
    spaces=None,
    scratch=(),
    limit=16,
    flops=0,
    bytes_accessed=0,
):
    def placed(space):
        return pl.BlockSpec(memory_space=space)

    many = isinstance(out_shape, (list, tuple))
    spaces = spaces or [pltpu.VMEM] * len(args)
    args = [
        pltpu.with_memory_space_constraint(arg, pltpu.HBM) if space == pltpu.HBM else arg
        for arg, space in zip(args, spaces)
    ]
    return pl.pallas_call(
        kernel,
        out_shape=out_shape,
        in_specs=[placed(space) for space in spaces],
        out_specs=[placed(pltpu.VMEM)] * len(out_shape) if many else placed(pltpu.VMEM),
        scratch_shapes=list(scratch),
        compiler_params=pltpu.CompilerParams(vmem_limit_bytes=limit * 1024 * 1024),
        cost_estimate=pl.CostEstimate(
            flops=flops, bytes_accessed=bytes_accessed, transcendentals=0
        ),
    )(*args)


def pack_kernel(block, *refs):
    sources, outs, (ready, held, arrived, ids_held, sems) = refs[:5], refs[5:-5], refs[-5:]
    targets = [ids_held] + [arrived.at[which] for which in range(3)] + [ready]
    copies = [
        pltpu.make_async_copy(source, target, sems.at[which])
        for which, (source, target) in enumerate(zip(sources, targets))
    ]
    for copy in copies:
        copy.start()
    first = lax.axis_index("dp") ^ lax.axis_index("enc")
    copies[0].wait()
    ids = ids_held[...]
    row = lax.broadcasted_iota(jnp.int32, (ID_ROWS, ids.shape[1]), 0)
    digits = jnp.where(row == 0, ids // ID_BASE, jnp.where(row == 1, ids % ID_BASE, 0))
    digits = digits.astype(jnp.float32).astype(jnp.bfloat16)
    for out in outs:
        out[3 * block :] = digits
    for which in range(3):
        copies[1 + which].wait()
        held[...] = arrived[which].T
        for hop, out in zip(SENDS, outs):
            begin = pl.multiple_of((first ^ hop) * block, 16)
            out[which * block : (which + 1) * block] = held[pl.ds(begin, block)]
    copies[4].wait()


def identifiers(slabs, block):
    numbers = []
    for slab in slabs:
        digits = slab[3 * block : 3 * block + ID_ROWS].astype(jnp.float32)
        numbers.append(digits[0:1] * ID_BASE + digits[1:2])
    return numbers


def set_bias(bias, key_ids, query_ids):
    queries = jnp.concatenate(query_ids, axis=1)
    for index, ids in enumerate(key_ids):
        rows = ids.shape[1]
        column = jnp.broadcast_to(ids, (rows, rows)).T
        column = jnp.concatenate([column] * len(query_ids), axis=1)
        bias[index * rows : (index + 1) * rows] = jnp.where(column == queries, 0.0, -1e30)


def gather(slabs, which, block, head, head_width):
    begin = which * block + head * head_width
    return jnp.concatenate([slab[begin : begin + head_width] for slab in slabs], axis=1)


def weigh(key, query, bias):
    scores = lax.dot_general(
        key, query, (((0,), (0,)), ((), ())), preferred_element_type=jnp.float32
    )
    scores = scores + bias
    return scores, jnp.max(scores, axis=0, keepdims=True)


def attend_first_kernel(block, head_width, *refs):
    slabs, (mixed, highest, total, bias) = refs[:-4], refs[-4:]
    ids = identifiers(slabs, block)
    set_bias(bias, ids, ids)
    factor = math.log2(math.e) / math.sqrt(head_width)
    for head in range(block // head_width):
        query, key, value = (gather(slabs, which, block, head, head_width) for which in range(3))
        scores, top = weigh(key, query, bias[...])
        weights = jnp.exp2((scores - top) * factor)
        highest[head : head + 1] = top
        total[head : head + 1] = jnp.sum(weights, axis=0, keepdims=True)
        mixed[head * head_width : (head + 1) * head_width] = jnp.dot(
            value, weights.astype(jnp.bfloat16), preferred_element_type=jnp.float32
        )


def attend_more(early, late, state, bias, outs, first, head_width):
    mixed, highest, total = state
    block, rows = outs[0].shape
    columns = slice(first, first + len(early) * rows)
    set_bias(bias, identifiers([late], block), identifiers(early, block))
    factor = math.log2(math.e) / math.sqrt(head_width)
    for head in range(block // head_width):
        span = slice(head * head_width, (head + 1) * head_width)
        query = gather(early, 0, block, head, head_width)
        key, value = (gather([late], which, block, head, head_width) for which in (1, 2))
        scores, top = weigh(key, query, bias[...])
        before = highest[head : head + 1, columns]
        top = jnp.maximum(top, before)
        weights = jnp.exp2((scores - top) * factor)
        shrink = jnp.exp2((before - top) * factor)
        sums = total[head : head + 1, columns] * shrink
        sums = sums + jnp.sum(weights, axis=0, keepdims=True)
        result = mixed[span, columns] * shrink + jnp.dot(
            value, weights.astype(jnp.bfloat16), preferred_element_type=jnp.float32
        )
        result = (result / sums).astype(jnp.bfloat16)
        for index, out in enumerate(outs):
            out[span] = result[:, index * rows : (index + 1) * rows]


def attend_across_kernel(head_width, *refs):
    count = len(SENDS)
    slabs, state, (first, last, old_bias, bias) = refs[:count], refs[count:-4], refs[-4:]
    block = last.shape[0]
    ids = identifiers(slabs, block)
    set_bias(bias, ids, ids[-1:])
    factor = math.log2(math.e) / math.sqrt(head_width)
    for head in range(block // head_width):
        span = slice(head * head_width, (head + 1) * head_width)
        query = gather(slabs[-1:], 0, block, head, head_width)
        key, value = (gather(slabs, which, block, head, head_width) for which in (1, 2))
        scores, top = weigh(key, query, bias[...])
        weights = jnp.exp2((scores - top) * factor)
        sums = jnp.sum(weights, axis=0, keepdims=True)
        result = jnp.dot(value, weights.astype(jnp.bfloat16), preferred_element_type=jnp.float32)
        last[span] = (result / sums).astype(jnp.bfloat16)
    attend_more(slabs[:1], slabs[-1], state, old_bias, [first], 0, head_width)


def attend_one_kernel(head_width, first, early, late, *refs):
    state, (out, bias) = refs[:3], refs[3:]
    attend_more([early], late, state, bias, [out], first, head_width)


def stack_kernel(count, *refs):
    sources, out, sems = refs[:count], refs[-2], refs[-1]
    copies = [
        pltpu.make_async_copy(source, out.at[index], sems.at[index])
        for index, source in enumerate(sources)
    ]
    for copy in copies:
        copy.start()
    for copy in copies:
        copy.wait()


def halve_kernel(*refs):
    pieces, (kept, given) = refs[:-2], refs[-2:]
    s = lax.axis_index("seq")
    half = kept.shape[1]
    for hop, piece in zip(RETURNS, pieces):
        kept[hop] = piece[pl.ds(pl.multiple_of(s * half, 16), half)]
        given[hop] = piece[pl.ds(pl.multiple_of((1 - s) * half, 16), half)]


def gradient_kernel(count, *refs):
    kept, given, same, others, *outs = refs
    e = lax.axis_index("enc")
    features, rows = [], []
    for step in range(count):
        features += [kept[step], given[step]]
        rows += [same[step], others[step]]
    total = jnp.dot(
        jnp.concatenate(features, axis=1),
        jnp.concatenate(rows, axis=0),
        preferred_element_type=jnp.float32,
    )
    width, short = total.shape[1] // count, total.shape[0] // 2
    for target in range(count):
        block = total[:, target * width : (target + 1) * width]
        folded = jnp.concatenate([block[:short], block[short:]], axis=1).astype(jnp.bfloat16)

        for index, out in enumerate(outs):

            @pl.when(e ^ target == SUMS[index])
            def _():
                out[...] = folded


def project_kernel(*refs):
    pieces, (residual, weight, out, attended) = refs[:-4], refs[-4:]
    first = lax.axis_index("dp") ^ lax.axis_index("enc")
    block = pieces[0].shape[0]
    for hop, piece in zip(RETURNS, pieces):
        attended[pl.ds(pl.multiple_of((first ^ hop) * block, 16), block)] = piece[...]
    projected = lax.dot_general(
        attended[...], weight[...], (((0,), (0,)), ((), ())), preferred_element_type=jnp.float32
    )
    out[...] = (residual[...].astype(jnp.float32) + projected).astype(jnp.bfloat16)


def add_kernel(*refs):
    partial, out = refs[:-1], refs[-1]
    total = partial[0][...].astype(jnp.float32)
    for ref in partial[1:]:
        total = total + ref[...].astype(jnp.float32)
    short, width = total.shape[0], out.shape[1]
    out[:short] = total[:, :width]
    out[short:] = total[:, width:]


def exchange_body(
    sizes, queries, key_vectors, value_vectors, residual, out_weight, cotangent, send_row, image_id
):
    n_dp, n_enc, n_seq = sizes
    rows, width = queries.shape
    block = width // n_enc
    half = block // n_seq
    head_width = width // HEADS
    group = n_enc * rows
    tall = 3 * block + ID_ROWS
    bf16 = functools.partial(jax.ShapeDtypeStruct, dtype=jnp.bfloat16)
    hbm = pltpu.HBM

    def move(data, partner):
        pairs = []
        for d in range(n_dp):
            for e in range(n_enc):
                for s in range(n_seq):
                    to_d, to_e, to_s = partner(d, e, s)
                    pairs.append(
                        ((d * n_enc + e) * n_seq + s, (to_d * n_enc + to_e) * n_seq + to_s)
                    )
        return lax.ppermute(data, AXES, pairs)

    def along_enc(pieces, hops):
        return [
            move(piece, lambda d, e, s, hop=hop: (d, e ^ hop, s)) if hop else piece
            for hop, piece in zip(hops, pieces)
        ]

    def along_seq(data):
        return move(data, lambda d, e, s: (d, e, s ^ 1))

    with jax.named_scope("pack"):
        outs = call(
            functools.partial(pack_kernel, block),
            [bf16((tall, rows))] * n_enc + [bf16((rows, width))],
            image_id.reshape(1, rows),
            queries,
            key_vectors,
            value_vectors,
            cotangent,
            spaces=[hbm] * 5,
            scratch=[
                pltpu.VMEM((width, rows), jnp.bfloat16),
                pltpu.VMEM((3, rows, width), jnp.bfloat16),
                pltpu.VMEM((1, rows), jnp.int32),
                pltpu.SemaphoreType.DMA((5,)),
            ],
            bytes_accessed=8 * rows * width * 2,
        )
        slabs, cotangent = outs[:-1], outs[-1]
    with jax.named_scope("exchange_heads"):
        slabs = along_enc(slabs, SENDS)
    with jax.named_scope("gather_cotangent"):
        same = [cotangent] + [
            move(cotangent, lambda d, e, s, k=k: (d ^ k, e, s)) for k in range(1, n_dp)
        ]
    with jax.named_scope("attention"):
        known = group - rows
        f32 = functools.partial(jax.ShapeDtypeStruct, dtype=jnp.float32)
        state = call(
            functools.partial(attend_first_kernel, block, head_width),
            [f32((block, known)), f32((8, known)), f32((8, known))],
            *slabs[:-1],
            scratch=[pltpu.VMEM((known, known), jnp.float32)],
            flops=55 * known * known * block,
            bytes_accessed=8 * group * block,
        )
        across = call(
            functools.partial(attend_across_kernel, head_width),
            [bf16((block, rows))] * 2,
            *slabs,
            *state,
            scratch=[pltpu.VMEM((rows, rows), jnp.float32), pltpu.VMEM((group, rows), jnp.float32)],
            flops=55 * rows * (rows + group) * block,
            bytes_accessed=8 * group * block,
        )
        rest = [
            call(
                functools.partial(attend_one_kernel, head_width, index * rows),
                bf16((block, rows)),
                slabs[index],
                slabs[-1],
                *state,
                scratch=[pltpu.VMEM((rows, rows), jnp.float32)],
                flops=55 * rows * rows * block,
                bytes_accessed=8 * rows * block,
            )
            for index in (1, 2)
        ]
        pieces = dict(zip(SENDS, [across[0], *rest, across[1]]))
        pieces = [pieces[hop] for hop in RETURNS]
    with jax.named_scope("send_to_owner"):
        pieces = [
            move(piece, lambda d, e, s, hop=hop: (d ^ hop, e ^ hop, s)) if hop else piece
            for hop, piece in zip(RETURNS, pieces)
        ]
        kept, given = call(
            halve_kernel,
            [bf16((n_dp, half, rows))] * 2,
            *pieces,
            flops=400 * group * group * half,
        )
        given = along_seq(given)
    with jax.named_scope("swap_cotangent"):
        stacked = call(
            functools.partial(stack_kernel, n_dp),
            bf16((n_dp, rows, width)),
            *same,
            spaces=[pltpu.VMEM] * n_dp + [pl.ANY] * 0,
            scratch=[pltpu.SemaphoreType.DMA((n_dp,))],
            bytes_accessed=4 * n_dp * rows * width,
        )
    with jax.named_scope("gradient"):
        partial = call(
            functools.partial(gradient_kernel, n_enc),
            [bf16((half // 2, 2 * block))] * n_enc,
            kept,
            given,
            stacked,
            along_seq(stacked),
            flops=2 * half * width * rows * n_dp * n_seq,
            bytes_accessed=2 * n_dp * n_seq * rows * width,
        )
    with jax.named_scope("sum_gradient"):
        partial = [
            move(part, lambda d, e, s, hop=hop: (d ^ e, e ^ hop, s))
            for hop, part in zip(SUMS, partial)
        ]
    with jax.named_scope("send_home"):
        homes = [
            move(piece, lambda d, e, s, hop=hop: (d ^ hop, e, s)) if hop else piece
            for hop, piece in zip(RETURNS, pieces)
        ]
    with jax.named_scope("project"):
        layer_out = call(
            project_kernel,
            bf16((rows, width)),
            *homes,
            residual,
            out_weight,
            scratch=[pltpu.VMEM((width, rows), jnp.bfloat16)],
            flops=2 * rows * width * width,
            bytes_accessed=2 * width * width,
        )
    with jax.named_scope("add_gradient"):
        grad_weight = call(
            add_kernel,
            jax.ShapeDtypeStruct((half, block), jnp.float32),
            *partial,
            bytes_accessed=4 * half * block * 4,
        )
    return (layer_out, grad_weight)


def attend_groups(query_group, key_group, value_group, image_ids):
    items, slot_count, group_width = query_group.shape
    group_heads = HEADS // 2
    head_width = group_width // group_heads
    scale = 1.0 / math.sqrt(head_width)
    position = jnp.arange(slot_count)
    image_ids = jnp.where(image_ids < 0, -1 - position[None, :], image_ids)
    shaped_query = query_group.reshape(items, slot_count, group_heads, head_width)
    shaped_key = key_group.reshape(items, slot_count, group_heads, head_width)
    shaped_value = value_group.reshape(items, slot_count, group_heads, head_width)
    scores = (
        jnp.einsum("gqhd,gkhd->ghqk", shaped_query, shaped_key, preferred_element_type=jnp.float32)
        * scale
    )
    same_image = image_ids[:, None, :, None] == image_ids[:, None, None, :]
    scores = jnp.where(same_image, scores, -1e30)
    highest = jnp.max(scores, axis=-1, keepdims=True)
    weights = jnp.exp(scores - highest)
    probs = (weights / jnp.sum(weights, axis=-1, keepdims=True)).astype(jnp.bfloat16)
    mixed = jnp.einsum("ghqk,gkhd->gqhd", probs, shaped_value, preferred_element_type=jnp.float32)
    return mixed.reshape(items, slot_count, group_width).astype(jnp.bfloat16)


def routed_body(
    queries, key_vectors, value_vectors, residual, out_weight, cotangent, send_row, image_id
):
    row_count, full_width = queries.shape
    half_width = full_width // 2
    is_live = send_row < row_count
    source_row = jnp.minimum(send_row, row_count - 1)

    def arrange(data):
        grouped = data.reshape(row_count, 2, half_width).transpose(1, 0, 2)
        return jnp.where(is_live[None, :, None], grouped[:, source_row], jnp.zeros((), data.dtype))

    send_query = arrange(queries)
    send_key = arrange(key_vectors)
    send_value = arrange(value_vectors)
    send_image = jnp.where(is_live, image_id[source_row], -1)
    send_image = jnp.broadcast_to(send_image[None, :], (2, send_row.shape[0]))
    received = (
        lax.all_to_all(send_query, "enc", split_axis=1, concat_axis=1, tiled=True),
        lax.all_to_all(send_key, "enc", split_axis=1, concat_axis=1, tiled=True),
        lax.all_to_all(send_value, "enc", split_axis=1, concat_axis=1, tiled=True),
        lax.all_to_all(send_image, "enc", split_axis=1, concat_axis=1, tiled=True),
    )
    output = attend_groups(received[0], received[1], received[2], received[3])
    returned = lax.all_to_all(output, "enc", split_axis=1, concat_axis=1, tiled=True)
    holder = jnp.zeros((2, row_count + 1, half_width), jnp.bfloat16).at[:, send_row].set(returned)
    attended = holder[:, :row_count].transpose(1, 0, 2).reshape(row_count, full_width)
    projected = jnp.dot(attended, out_weight, preferred_element_type=jnp.float32)
    layer_out = (residual.astype(jnp.float32) + projected).astype(jnp.bfloat16)
    first_sum = lax.psum_scatter(
        lax.dot_general(
            attended, cotangent, (((0,), (0,)), ((), ())), preferred_element_type=jnp.float32
        ).astype(jnp.bfloat16),
        "dp",
        scatter_dimension=0,
        tiled=True,
    )
    second_sum = lax.psum_scatter(first_sum, "seq", scatter_dimension=0, tiled=True).astype(
        jnp.float32
    )
    grad_weight = lax.psum_scatter(second_sum, "enc", scatter_dimension=1, tiled=True)
    return (layer_out, grad_weight)


def solution(mesh):
    sizes = tuple(mesh.shape[name] for name in AXES)
    n_dp, n_enc, n_seq = sizes
    fits = n_seq == 2 and n_dp == n_enc == 4 and HEADS % (2 * n_enc) == 0
    body = functools.partial(exchange_body, sizes) if fits else routed_body
    placed = (
        P(("dp", "enc", "seq"), None),
        P(("dp", "enc", "seq"), None),
        P(("dp", "enc", "seq"), None),
        P(("dp", "enc", "seq"), None),
        P(),
        P(("dp", "enc", "seq"), None),
        P(("dp", "enc", "seq")),
        P(("dp", "enc", "seq")),
    )
    return jax.shard_map(
        body,
        mesh=mesh,
        in_specs=placed,
        out_specs=(P(("dp", "enc", "seq"), None), P(("dp", "seq"), "enc")),
        check_vma=False,
    )
```

```python
import functools
import math

import jax
import jax.numpy as jnp
from jax import lax
from jax.experimental import pallas as pl
from jax.experimental.pallas import tpu as pltpu
from jax.sharding import PartitionSpec as P

HEADS = 16
AXES = ("dp", "enc", "seq")
ID_ROWS = 16
ID_BASE = 64
SENDS = (3, 0, 1, 2)
RETURNS = (2, 3, 0, 1)
SUMS = (2, 3, 1)


def call(
    kernel,
    out_shape,
    *args,
    spaces=None,
    scratch=(),
    limit=16,
    flops=0,
    bytes_accessed=0,
):
    def placed(space):
        return pl.BlockSpec(memory_space=space)

    many = isinstance(out_shape, (list, tuple))
    spaces = spaces or [pltpu.VMEM] * len(args)
    args = [
        pltpu.with_memory_space_constraint(arg, pltpu.HBM) if space == pltpu.HBM else arg
        for arg, space in zip(args, spaces)
    ]
    return pl.pallas_call(
        kernel,
        out_shape=out_shape,
        in_specs=[placed(space) for space in spaces],
        out_specs=[placed(pltpu.VMEM)] * len(out_shape) if many else placed(pltpu.VMEM),
        scratch_shapes=list(scratch),
        compiler_params=pltpu.CompilerParams(vmem_limit_bytes=limit * 1024 * 1024),
        cost_estimate=pl.CostEstimate(
            flops=flops, bytes_accessed=bytes_accessed, transcendentals=0
        ),
    )(*args)


def pack_kernel(block, *refs):
    sources, outs, (ready, held, arrived, ids_held, sems) = refs[:5], refs[5:-5], refs[-5:]
    targets = [ids_held] + [arrived.at[which] for which in range(3)] + [ready]
    copies = [
        pltpu.make_async_copy(source, target, sems.at[which])
        for which, (source, target) in enumerate(zip(sources, targets))
    ]
    for copy in copies:
        copy.start()
    first = lax.axis_index("dp") ^ lax.axis_index("enc")
    copies[0].wait()
    ids = ids_held[...]
    row = lax.broadcasted_iota(jnp.int32, (ID_ROWS, ids.shape[1]), 0)
    digits = jnp.where(row == 0, ids // ID_BASE, jnp.where(row == 1, ids % ID_BASE, 0))
    digits = digits.astype(jnp.float32).astype(jnp.bfloat16)
    for out in outs:
        out[3 * block :] = digits
    for which in range(3):
        copies[1 + which].wait()
        held[...] = arrived[which].T
        for hop, out in zip(SENDS, outs):
            begin = pl.multiple_of((first ^ hop) * block, 16)
            out[which * block : (which + 1) * block] = held[pl.ds(begin, block)]
    copies[4].wait()


def identifiers(slabs, block):
    numbers = []
    for slab in slabs:
        digits = slab[3 * block : 3 * block + ID_ROWS].astype(jnp.float32)
        numbers.append(digits[0:1] * ID_BASE + digits[1:2])
    return numbers


def set_bias(bias, key_ids, query_ids):
    queries = jnp.concatenate(query_ids, axis=1)
    for index, ids in enumerate(key_ids):
        rows = ids.shape[1]
        column = jnp.broadcast_to(ids, (rows, rows)).T
        column = jnp.concatenate([column] * len(query_ids), axis=1)
        bias[index * rows : (index + 1) * rows] = jnp.where(column == queries, 0.0, -1e30)


def gather(slabs, which, block, head, head_width):
    begin = which * block + head * head_width
    return jnp.concatenate([slab[begin : begin + head_width] for slab in slabs], axis=1)


def weigh(key, query, bias):
    scores = lax.dot_general(
        key, query, (((0,), (0,)), ((), ())), preferred_element_type=jnp.float32
    )
    scores = scores + bias
    return scores, jnp.max(scores, axis=0, keepdims=True)


def attend_first_kernel(block, head_width, *refs):
    slabs, (mixed, highest, total, bias) = refs[:-4], refs[-4:]
    ids = identifiers(slabs, block)
    set_bias(bias, ids, ids)
    factor = math.log2(math.e) / math.sqrt(head_width)
    for head in range(block // head_width):
        query, key, value = (gather(slabs, which, block, head, head_width) for which in range(3))
        scores, top = weigh(key, query, bias[...])
        weights = jnp.exp2((scores - top) * factor)
        highest[head : head + 1] = top
        total[head : head + 1] = jnp.sum(weights, axis=0, keepdims=True)
        mixed[head * head_width : (head + 1) * head_width] = jnp.dot(
            value, weights.astype(jnp.bfloat16), preferred_element_type=jnp.float32
        )


def attend_more(early, late, state, bias, outs, first, head_width):
    mixed, highest, total = state
    block, rows = outs[0].shape
    columns = slice(first, first + len(early) * rows)
    set_bias(bias, identifiers([late], block), identifiers(early, block))
    factor = math.log2(math.e) / math.sqrt(head_width)
    for head in range(block // head_width):
        span = slice(head * head_width, (head + 1) * head_width)
        query = gather(early, 0, block, head, head_width)
        key, value = (gather([late], which, block, head, head_width) for which in (1, 2))
        scores, top = weigh(key, query, bias[...])
        before = highest[head : head + 1, columns]
        top = jnp.maximum(top, before)
        weights = jnp.exp2((scores - top) * factor)
        shrink = jnp.exp2((before - top) * factor)
        sums = total[head : head + 1, columns] * shrink
        sums = sums + jnp.sum(weights, axis=0, keepdims=True)
        result = mixed[span, columns] * shrink + jnp.dot(
            value, weights.astype(jnp.bfloat16), preferred_element_type=jnp.float32
        )
        result = (result / sums).astype(jnp.bfloat16)
        for index, out in enumerate(outs):
            out[span] = result[:, index * rows : (index + 1) * rows]


def attend_across_kernel(head_width, *refs):
    count = len(SENDS)
    slabs, state, (first, last, old_bias, bias) = refs[:count], refs[count:-4], refs[-4:]
    block = last.shape[0]
    ids = identifiers(slabs, block)
    set_bias(bias, ids, ids[-1:])
    factor = math.log2(math.e) / math.sqrt(head_width)
    for head in range(block // head_width):
        span = slice(head * head_width, (head + 1) * head_width)
        query = gather(slabs[-1:], 0, block, head, head_width)
        key, value = (gather(slabs, which, block, head, head_width) for which in (1, 2))
        scores, top = weigh(key, query, bias[...])
        weights = jnp.exp2((scores - top) * factor)
        sums = jnp.sum(weights, axis=0, keepdims=True)
        result = jnp.dot(value, weights.astype(jnp.bfloat16), preferred_element_type=jnp.float32)
        last[span] = (result / sums).astype(jnp.bfloat16)
    attend_more(slabs[:1], slabs[-1], state, old_bias, [first], 0, head_width)


def attend_rest_kernel(head_width, *refs):
    early, late, state, outs, bias = refs[:2], refs[2], refs[3:6], refs[6:8], refs[8]
    attend_more(early, late, state, bias, outs, late.shape[1], head_width)


def stack_kernel(count, *refs):
    sources, out, sems = refs[:count], refs[-2], refs[-1]
    copies = [
        pltpu.make_async_copy(source, out.at[index], sems.at[index])
        for index, source in enumerate(sources)
    ]
    for copy in copies:
        copy.start()
    for copy in copies:
        copy.wait()


def halve_kernel(*refs):
    count = len(RETURNS)
    pieces, homes, (kept, given) = refs[:count], refs[count : 2 * count], refs[2 * count :]
    e, s = lax.axis_index("enc"), lax.axis_index("seq")
    half = kept.shape[1]
    for hop, piece in zip(RETURNS, pieces):
        kept[e ^ hop] = piece[pl.ds(pl.multiple_of(s * half, 16), half)]
        given[e ^ hop] = piece[pl.ds(pl.multiple_of((1 - s) * half, 16), half)]
    for hop, piece in zip(RETURNS, pieces):
        for step, home in enumerate(homes):

            @pl.when(e ^ hop == step)
            def _():
                home[...] = piece[...]


def gradient_kernel(count, *refs):
    kept, given, same, others, own, *outs = refs
    e = lax.axis_index("enc")
    features, rows = [], []
    for step in range(count):
        features += [kept[step], given[step]]
        rows += [same[step], others[step]]
    total = jnp.dot(
        jnp.concatenate(features, axis=1),
        jnp.concatenate(rows, axis=0),
        preferred_element_type=jnp.float32,
    )
    width, short = total.shape[1] // count, total.shape[0] // 2
    for target in range(count):
        block = total[:, target * width : (target + 1) * width]
        folded = jnp.concatenate([block[:short], block[short:]], axis=1).astype(jnp.bfloat16)

        @pl.when(e == target)
        def _():
            own[...] = block

        for index, out in enumerate(outs):

            @pl.when(e ^ target == SUMS[index])
            def _():
                out[...] = folded


def project_kernel(*refs):
    pieces, (residual, weight, out, attended) = refs[:-4], refs[-4:]
    d = lax.axis_index("dp")
    block = pieces[0].shape[0]
    for step, piece in enumerate(pieces):
        attended[pl.ds(pl.multiple_of((d ^ step) * block, 16), block)] = piece[...]
    projected = lax.dot_general(
        attended[...], weight[...], (((0,), (0,)), ((), ())), preferred_element_type=jnp.float32
    )
    out[...] = (residual[...].astype(jnp.float32) + projected).astype(jnp.bfloat16)


def add_kernel(own, *refs):
    out, width = refs[-1], own.shape[1]
    total = refs[0][...].astype(jnp.float32)
    for ref in refs[1:-1]:
        total = total + ref[...].astype(jnp.float32)
    short = total.shape[0]
    out[:short] = own[:short] + total[:, :width]
    out[short:] = own[short:] + total[:, width:]


def exchange_body(
    sizes, queries, key_vectors, value_vectors, residual, out_weight, cotangent, send_row, image_id
):
    n_dp, n_enc, n_seq = sizes
    rows, width = queries.shape
    block = width // n_enc
    half = block // n_seq
    head_width = width // HEADS
    group = n_enc * rows
    tall = 3 * block + ID_ROWS
    bf16 = functools.partial(jax.ShapeDtypeStruct, dtype=jnp.bfloat16)
    hbm = pltpu.HBM

    def move(data, partner):
        pairs = []
        for d in range(n_dp):
            for e in range(n_enc):
                for s in range(n_seq):
                    to_d, to_e, to_s = partner(d, e, s)
                    pairs.append(
                        ((d * n_enc + e) * n_seq + s, (to_d * n_enc + to_e) * n_seq + to_s)
                    )
        return lax.ppermute(data, AXES, pairs)

    def along_enc(pieces, hops):
        return [
            move(piece, lambda d, e, s, hop=hop: (d, e ^ hop, s)) if hop else piece
            for hop, piece in zip(hops, pieces)
        ]

    def along_seq(data):
        return move(data, lambda d, e, s: (d, e, s ^ 1))

    with jax.named_scope("pack"):
        outs = call(
            functools.partial(pack_kernel, block),
            [bf16((tall, rows))] * n_enc + [bf16((rows, width))],
            image_id.reshape(1, rows),
            queries,
            key_vectors,
            value_vectors,
            cotangent,
            spaces=[hbm] * 5,
            scratch=[
                pltpu.VMEM((width, rows), jnp.bfloat16),
                pltpu.VMEM((3, rows, width), jnp.bfloat16),
                pltpu.VMEM((1, rows), jnp.int32),
                pltpu.SemaphoreType.DMA((5,)),
            ],
            bytes_accessed=8 * rows * width * 2,
        )
        slabs, cotangent = outs[:-1], outs[-1]
    with jax.named_scope("exchange_heads"):
        slabs = along_enc(slabs, SENDS)
    with jax.named_scope("gather_cotangent"):
        same = [cotangent] + [
            move(cotangent, lambda d, e, s, k=k: (d ^ k, e, s)) for k in range(1, n_dp)
        ]
    with jax.named_scope("attention"):
        known = group - rows
        f32 = functools.partial(jax.ShapeDtypeStruct, dtype=jnp.float32)
        state = call(
            functools.partial(attend_first_kernel, block, head_width),
            [f32((block, known)), f32((8, known)), f32((8, known))],
            *slabs[:-1],
            scratch=[pltpu.VMEM((known, known), jnp.float32)],
            flops=55 * known * known * block,
            bytes_accessed=8 * group * block,
        )
        across = call(
            functools.partial(attend_across_kernel, head_width),
            [bf16((block, rows))] * 2,
            *slabs,
            *state,
            scratch=[pltpu.VMEM((rows, rows), jnp.float32), pltpu.VMEM((group, rows), jnp.float32)],
            flops=55 * rows * (rows + group) * block,
            bytes_accessed=8 * group * block,
        )
        rest = call(
            functools.partial(attend_rest_kernel, head_width),
            [bf16((block, rows))] * 2,
            *slabs[1:],
            *state,
            scratch=[pltpu.VMEM((rows, 2 * rows), jnp.float32)],
            flops=55 * rows * 2 * rows * block,
            bytes_accessed=8 * group * block,
        )
        pieces = dict(zip(SENDS, [across[0], *rest, across[1]]))
        pieces = [pieces[hop] for hop in RETURNS]
    with jax.named_scope("send_to_owner"):
        pieces = [
            move(piece, lambda d, e, s, hop=hop: (d ^ e, e ^ hop, s))
            for hop, piece in zip(RETURNS, pieces)
        ]
        *homes, kept, given = call(
            halve_kernel,
            [bf16((block, rows))] * n_dp + [bf16((n_dp, half, rows))] * 2,
            *pieces,
            flops=400 * group * group * half,
        )
        given = along_seq(given)
    with jax.named_scope("swap_cotangent"):
        stacked = call(
            functools.partial(stack_kernel, n_dp),
            bf16((n_dp, rows, width)),
            *same,
            spaces=[pltpu.VMEM] * n_dp + [pl.ANY] * 0,
            scratch=[pltpu.SemaphoreType.DMA((n_dp,))],
            bytes_accessed=4 * n_dp * rows * width,
        )
    with jax.named_scope("gradient"):
        mine, *partial = call(
            functools.partial(gradient_kernel, n_enc),
            [jax.ShapeDtypeStruct((half, block), jnp.float32)]
            + [bf16((half // 2, 2 * block))] * (n_enc - 1),
            kept,
            given,
            stacked,
            along_seq(stacked),
            flops=2 * half * width * rows * n_dp * n_seq,
            bytes_accessed=2 * n_dp * n_seq * rows * width,
        )
    with jax.named_scope("sum_gradient"):
        partial = along_enc(partial, SUMS)
    with jax.named_scope("send_home"):
        homes[1:] = [
            move(homes[k], lambda d, e, s, k=k: (d ^ k, e, s)) for k in range(1, n_dp)
        ]
    with jax.named_scope("project"):
        layer_out = call(
            project_kernel,
            bf16((rows, width)),
            *homes,
            residual,
            out_weight,
            scratch=[pltpu.VMEM((width, rows), jnp.bfloat16)],
            flops=1 * rows * width * width,
            bytes_accessed=2 * width * width,
        )
    with jax.named_scope("add_gradient"):
        grad_weight = call(
            add_kernel,
            jax.ShapeDtypeStruct((half, block), jnp.float32),
            mine,
            *partial,
            bytes_accessed=4 * half * block * 4,
        )
    return (layer_out, grad_weight)


def attend_groups(query_group, key_group, value_group, image_ids):
    items, slot_count, group_width = query_group.shape
    group_heads = HEADS // 2
    head_width = group_width // group_heads
    scale = 1.0 / math.sqrt(head_width)
    position = jnp.arange(slot_count)
    image_ids = jnp.where(image_ids < 0, -1 - position[None, :], image_ids)
    shaped_query = query_group.reshape(items, slot_count, group_heads, head_width)
    shaped_key = key_group.reshape(items, slot_count, group_heads, head_width)
    shaped_value = value_group.reshape(items, slot_count, group_heads, head_width)
    scores = (
        jnp.einsum("gqhd,gkhd->ghqk", shaped_query, shaped_key, preferred_element_type=jnp.float32)
        * scale
    )
    same_image = image_ids[:, None, :, None] == image_ids[:, None, None, :]
    scores = jnp.where(same_image, scores, -1e30)
    highest = jnp.max(scores, axis=-1, keepdims=True)
    weights = jnp.exp(scores - highest)
    probs = (weights / jnp.sum(weights, axis=-1, keepdims=True)).astype(jnp.bfloat16)
    mixed = jnp.einsum("ghqk,gkhd->gqhd", probs, shaped_value, preferred_element_type=jnp.float32)
    return mixed.reshape(items, slot_count, group_width).astype(jnp.bfloat16)


def routed_body(
    queries, key_vectors, value_vectors, residual, out_weight, cotangent, send_row, image_id
):
    row_count, full_width = queries.shape
    half_width = full_width // 2
    is_live = send_row < row_count
    source_row = jnp.minimum(send_row, row_count - 1)

    def arrange(data):
        grouped = data.reshape(row_count, 2, half_width).transpose(1, 0, 2)
        return jnp.where(is_live[None, :, None], grouped[:, source_row], jnp.zeros((), data.dtype))

    send_query = arrange(queries)
    send_key = arrange(key_vectors)
    send_value = arrange(value_vectors)
    send_image = jnp.where(is_live, image_id[source_row], -1)
    send_image = jnp.broadcast_to(send_image[None, :], (2, send_row.shape[0]))
    received = (
        lax.all_to_all(send_query, "enc", split_axis=1, concat_axis=1, tiled=True),
        lax.all_to_all(send_key, "enc", split_axis=1, concat_axis=1, tiled=True),
        lax.all_to_all(send_value, "enc", split_axis=1, concat_axis=1, tiled=True),
        lax.all_to_all(send_image, "enc", split_axis=1, concat_axis=1, tiled=True),
    )
    output = attend_groups(received[0], received[1], received[2], received[3])
    returned = lax.all_to_all(output, "enc", split_axis=1, concat_axis=1, tiled=True)
    holder = jnp.zeros((2, row_count + 1, half_width), jnp.bfloat16).at[:, send_row].set(returned)
    attended = holder[:, :row_count].transpose(1, 0, 2).reshape(row_count, full_width)
    projected = jnp.dot(attended, out_weight, preferred_element_type=jnp.float32)
    layer_out = (residual.astype(jnp.float32) + projected).astype(jnp.bfloat16)
    first_sum = lax.psum_scatter(
        lax.dot_general(
            attended, cotangent, (((0,), (0,)), ((), ())), preferred_element_type=jnp.float32
        ).astype(jnp.bfloat16),
        "dp",
        scatter_dimension=0,
        tiled=True,
    )
    second_sum = lax.psum_scatter(first_sum, "seq", scatter_dimension=0, tiled=True).astype(
        jnp.float32
    )
    grad_weight = lax.psum_scatter(second_sum, "enc", scatter_dimension=1, tiled=True)
    return (layer_out, grad_weight)


def solution(mesh):
    sizes = tuple(mesh.shape[name] for name in AXES)
    n_dp, n_enc, n_seq = sizes
    fits = n_seq == 2 and n_dp == n_enc == 4 and HEADS % (2 * n_enc) == 0
    body = functools.partial(exchange_body, sizes) if fits else routed_body
    placed = (
        P(("dp", "enc", "seq"), None),
        P(("dp", "enc", "seq"), None),
        P(("dp", "enc", "seq"), None),
        P(("dp", "enc", "seq"), None),
        P(),
        P(("dp", "enc", "seq"), None),
        P(("dp", "enc", "seq")),
        P(("dp", "enc", "seq")),
    )
    return jax.shard_map(
        body,
        mesh=mesh,
        in_specs=placed,
        out_specs=(P(("dp", "enc", "seq"), None), P(("dp", "seq"), "enc")),
        check_vma=False,
    )
```

```python
import functools
import math

import jax
import jax.numpy as jnp
from jax import lax
from jax.experimental import pallas as pl
from jax.experimental.pallas import tpu as pltpu
from jax.sharding import PartitionSpec as P

HEADS = 16
AXES = ("dp", "enc", "seq")
ID_ROWS = 16
ID_BASE = 64
SENDS = (3, 0, 1, 2)
RETURNS = (2, 3, 1, 0)
SUMS = (2, 3, 1, 0)


def call(
    kernel,
    out_shape,
    *args,
    spaces=None,
    scratch=(),
    limit=16,
    flops=0,
    bytes_accessed=0,
):
    def placed(space):
        return pl.BlockSpec(memory_space=space)

    many = isinstance(out_shape, (list, tuple))
    spaces = spaces or [pltpu.VMEM] * len(args)
    args = [
        pltpu.with_memory_space_constraint(arg, pltpu.HBM) if space == pltpu.HBM else arg
        for arg, space in zip(args, spaces)
    ]
    return pl.pallas_call(
        kernel,
        out_shape=out_shape,
        in_specs=[placed(space) for space in spaces],
        out_specs=[placed(pltpu.VMEM)] * len(out_shape) if many else placed(pltpu.VMEM),
        scratch_shapes=list(scratch),
        compiler_params=pltpu.CompilerParams(vmem_limit_bytes=limit * 1024 * 1024),
        cost_estimate=pl.CostEstimate(
            flops=flops, bytes_accessed=bytes_accessed, transcendentals=0
        ),
    )(*args)


def pack_kernel(block, *refs):
    sources, outs, (ready, held, arrived, ids_held, sems) = refs[:5], refs[5:-5], refs[-5:]
    targets = [ids_held] + [arrived.at[which] for which in range(3)] + [ready]
    copies = [
        pltpu.make_async_copy(source, target, sems.at[which])
        for which, (source, target) in enumerate(zip(sources, targets))
    ]
    for copy in copies:
        copy.start()
    first = lax.axis_index("dp") ^ lax.axis_index("enc")
    copies[0].wait()
    ids = ids_held[...]
    row = lax.broadcasted_iota(jnp.int32, (ID_ROWS, ids.shape[1]), 0)
    digits = jnp.where(row == 0, ids // ID_BASE, jnp.where(row == 1, ids % ID_BASE, 0))
    digits = digits.astype(jnp.float32).astype(jnp.bfloat16)
    for out in outs:
        out[3 * block :] = digits
    for which in range(3):
        copies[1 + which].wait()
        held[...] = arrived[which].T
        for hop, out in zip(SENDS, outs):
            begin = pl.multiple_of((first ^ hop) * block, 16)
            out[which * block : (which + 1) * block] = held[pl.ds(begin, block)]
    copies[4].wait()


def identifiers(slabs, block):
    numbers = []
    for slab in slabs:
        digits = slab[3 * block : 3 * block + ID_ROWS].astype(jnp.float32)
        numbers.append(digits[0:1] * ID_BASE + digits[1:2])
    return numbers


def set_bias(bias, key_ids, query_ids):
    queries = jnp.concatenate(query_ids, axis=1)
    for index, ids in enumerate(key_ids):
        rows = ids.shape[1]
        column = jnp.broadcast_to(ids, (rows, rows)).T
        column = jnp.concatenate([column] * len(query_ids), axis=1)
        bias[index * rows : (index + 1) * rows] = jnp.where(column == queries, 0.0, -1e30)


def gather(slabs, which, block, head, head_width):
    begin = which * block + head * head_width
    return jnp.concatenate([slab[begin : begin + head_width] for slab in slabs], axis=1)


def weigh(key, query, bias):
    scores = lax.dot_general(
        key, query, (((0,), (0,)), ((), ())), preferred_element_type=jnp.float32
    )
    scores = scores + bias
    return scores, jnp.max(scores, axis=0, keepdims=True)


def attend_first_kernel(block, head_width, *refs):
    slabs, (mixed, highest, total, bias) = refs[:-4], refs[-4:]
    ids = identifiers(slabs, block)
    set_bias(bias, ids, ids)
    factor = math.log2(math.e) / math.sqrt(head_width)
    for head in range(block // head_width):
        query, key, value = (gather(slabs, which, block, head, head_width) for which in range(3))
        scores, top = weigh(key, query, bias[...])
        weights = jnp.exp2((scores - top) * factor)
        highest[head : head + 1] = top
        total[head : head + 1] = jnp.sum(weights, axis=0, keepdims=True)
        mixed[head * head_width : (head + 1) * head_width] = jnp.dot(
            value, weights.astype(jnp.bfloat16), preferred_element_type=jnp.float32
        )


def attend_more(early, late, state, bias, outs, first, head_width):
    mixed, highest, total = state
    block, rows = outs[0].shape
    columns = slice(first, first + len(early) * rows)
    set_bias(bias, identifiers([late], block), identifiers(early, block))
    factor = math.log2(math.e) / math.sqrt(head_width)
    for head in range(block // head_width):
        span = slice(head * head_width, (head + 1) * head_width)
        query = gather(early, 0, block, head, head_width)
        key, value = (gather([late], which, block, head, head_width) for which in (1, 2))
        scores, top = weigh(key, query, bias[...])
        before = highest[head : head + 1, columns]
        top = jnp.maximum(top, before)
        weights = jnp.exp2((scores - top) * factor)
        shrink = jnp.exp2((before - top) * factor)
        sums = total[head : head + 1, columns] * shrink
        sums = sums + jnp.sum(weights, axis=0, keepdims=True)
        result = mixed[span, columns] * shrink + jnp.dot(
            value, weights.astype(jnp.bfloat16), preferred_element_type=jnp.float32
        )
        result = (result / sums).astype(jnp.bfloat16)
        for index, out in enumerate(outs):
            out[span] = result[:, index * rows : (index + 1) * rows]


def attend_across_kernel(head_width, *refs):
    count = len(SENDS)
    slabs, state, (first, last, old_bias, bias) = refs[:count], refs[count:-4], refs[-4:]
    block = last.shape[0]
    ids = identifiers(slabs, block)
    set_bias(bias, ids, ids[-1:])
    factor = math.log2(math.e) / math.sqrt(head_width)
    for head in range(block // head_width):
        span = slice(head * head_width, (head + 1) * head_width)
        query = gather(slabs[-1:], 0, block, head, head_width)
        key, value = (gather(slabs, which, block, head, head_width) for which in (1, 2))
        scores, top = weigh(key, query, bias[...])
        weights = jnp.exp2((scores - top) * factor)
        sums = jnp.sum(weights, axis=0, keepdims=True)
        result = jnp.dot(value, weights.astype(jnp.bfloat16), preferred_element_type=jnp.float32)
        last[span] = (result / sums).astype(jnp.bfloat16)
    attend_more(slabs[:1], slabs[-1], state, old_bias, [first], 0, head_width)


def attend_rest_kernel(head_width, *refs):
    early, late, state, outs, bias = refs[:2], refs[2], refs[3:6], refs[6:8], refs[8]
    attend_more(early, late, state, bias, outs, late.shape[1], head_width)


def stack_kernel(count, *refs):
    sources, out, sems = refs[:count], refs[-2], refs[-1]
    copies = [
        pltpu.make_async_copy(source, out.at[index], sems.at[index])
        for index, source in enumerate(sources)
    ]
    for copy in copies:
        copy.start()
    for copy in copies:
        copy.wait()


def halve_kernel(*refs):
    pieces, (kept, given) = refs[:-2], refs[-2:]
    s = lax.axis_index("seq")
    half = kept.shape[1]
    for hop, piece in zip(RETURNS, pieces):
        kept[hop] = piece[pl.ds(pl.multiple_of(s * half, 16), half)]
        given[hop] = piece[pl.ds(pl.multiple_of((1 - s) * half, 16), half)]


def gradient_kernel(count, *refs):
    kept, given, same, others, *outs = refs
    e = lax.axis_index("enc")
    features, rows = [], []
    for step in range(count):
        features += [kept[step], given[step]]
        rows += [same[step], others[step]]
    total = jnp.dot(
        jnp.concatenate(features, axis=1),
        jnp.concatenate(rows, axis=0),
        preferred_element_type=jnp.float32,
    )
    width, short = total.shape[1] // count, total.shape[0] // 2
    for target in range(count):
        block = total[:, target * width : (target + 1) * width]
        folded = jnp.concatenate([block[:short], block[short:]], axis=1).astype(jnp.bfloat16)

        for index, out in enumerate(outs):

            @pl.when(e ^ target == SUMS[index])
            def _():
                out[...] = folded


def project_kernel(*refs):
    pieces, (residual, weight, out, attended) = refs[:-4], refs[-4:]
    first = lax.axis_index("dp") ^ lax.axis_index("enc")
    block = pieces[0].shape[0]
    for hop, piece in zip(RETURNS, pieces):
        attended[pl.ds(pl.multiple_of((first ^ hop) * block, 16), block)] = piece[...]
    projected = lax.dot_general(
        attended[...], weight[...], (((0,), (0,)), ((), ())), preferred_element_type=jnp.float32
    )
    out[...] = (residual[...].astype(jnp.float32) + projected).astype(jnp.bfloat16)


def add_kernel(kept, *refs):
    partial, out = refs[:-1], refs[-1]
    stays = lax.axis_index("enc") == 0
    total = jnp.where(stays, kept[...], partial[SUMS.index(0)][...]).astype(jnp.float32)
    for hop, ref in zip(SUMS, partial):
        if hop:
            total = total + ref[...].astype(jnp.float32)
    short, width = total.shape[0], out.shape[1]
    out[:short] = total[:, :width]
    out[short:] = total[:, width:]


def exchange_body(
    sizes, queries, key_vectors, value_vectors, residual, out_weight, cotangent, send_row, image_id
):
    n_dp, n_enc, n_seq = sizes
    rows, width = queries.shape
    block = width // n_enc
    half = block // n_seq
    head_width = width // HEADS
    group = n_enc * rows
    tall = 3 * block + ID_ROWS
    bf16 = functools.partial(jax.ShapeDtypeStruct, dtype=jnp.bfloat16)
    hbm = pltpu.HBM

    def move(data, partner):
        pairs = []
        for d in range(n_dp):
            for e in range(n_enc):
                for s in range(n_seq):
                    to_d, to_e, to_s = partner(d, e, s)
                    source = (d * n_enc + e) * n_seq + s
                    target = (to_d * n_enc + to_e) * n_seq + to_s
                    if source != target:
                        pairs.append((source, target))
        return lax.ppermute(data, AXES, pairs)

    def along_enc(pieces, hops):
        return [
            move(piece, lambda d, e, s, hop=hop: (d, e ^ hop, s)) if hop else piece
            for hop, piece in zip(hops, pieces)
        ]

    def along_seq(data):
        return move(data, lambda d, e, s: (d, e, s ^ 1))

    with jax.named_scope("pack"):
        outs = call(
            functools.partial(pack_kernel, block),
            [bf16((tall, rows))] * n_enc + [bf16((rows, width))],
            image_id.reshape(1, rows),
            queries,
            key_vectors,
            value_vectors,
            cotangent,
            spaces=[hbm] * 5,
            scratch=[
                pltpu.VMEM((width, rows), jnp.bfloat16),
                pltpu.VMEM((3, rows, width), jnp.bfloat16),
                pltpu.VMEM((1, rows), jnp.int32),
                pltpu.SemaphoreType.DMA((5,)),
            ],
            bytes_accessed=8 * rows * width * 2,
        )
        slabs, cotangent = outs[:-1], outs[-1]
    with jax.named_scope("exchange_heads"):
        slabs = along_enc(slabs, SENDS)
    with jax.named_scope("gather_cotangent"):
        same = [cotangent] + [
            move(cotangent, lambda d, e, s, k=k: (d ^ k, e, s)) for k in range(1, n_dp)
        ]
    with jax.named_scope("attention"):
        known = group - rows
        f32 = functools.partial(jax.ShapeDtypeStruct, dtype=jnp.float32)
        state = call(
            functools.partial(attend_first_kernel, block, head_width),
            [f32((block, known)), f32((8, known)), f32((8, known))],
            *slabs[:-1],
            scratch=[pltpu.VMEM((known, known), jnp.float32)],
            flops=55 * known * known * block,
            bytes_accessed=8 * group * block,
        )
        across = call(
            functools.partial(attend_across_kernel, head_width),
            [bf16((block, rows))] * 2,
            *slabs,
            *state,
            scratch=[pltpu.VMEM((rows, rows), jnp.float32), pltpu.VMEM((group, rows), jnp.float32)],
            flops=55 * rows * (rows + group) * block,
            bytes_accessed=8 * group * block,
        )
        rest = call(
            functools.partial(attend_rest_kernel, head_width),
            [bf16((block, rows))] * 2,
            *slabs[1:],
            *state,
            scratch=[pltpu.VMEM((rows, 2 * rows), jnp.float32)],
            flops=55 * rows * 2 * rows * block,
            bytes_accessed=8 * group * block,
        )
        pieces = dict(zip(SENDS, [across[0], *rest, across[1]]))
        pieces = [pieces[hop] for hop in RETURNS]
    with jax.named_scope("send_to_owner"):
        pieces = [
            move(piece, lambda d, e, s, hop=hop: (d ^ hop, e ^ hop, s)) if hop else piece
            for hop, piece in zip(RETURNS, pieces)
        ]
        kept, given = call(
            halve_kernel,
            [bf16((n_dp, half, rows))] * 2,
            *pieces,
            flops=400 * group * group * half,
        )
        given = along_seq(given)
    with jax.named_scope("swap_cotangent"):
        stacked = call(
            functools.partial(stack_kernel, n_dp),
            bf16((n_dp, rows, width)),
            *same,
            spaces=[pltpu.VMEM] * n_dp + [pl.ANY] * 0,
            scratch=[pltpu.SemaphoreType.DMA((n_dp,))],
            bytes_accessed=4 * n_dp * rows * width,
        )
    with jax.named_scope("gradient"):
        partial = call(
            functools.partial(gradient_kernel, n_enc),
            [bf16((half // 2, 2 * block))] * n_enc,
            kept,
            given,
            stacked,
            along_seq(stacked),
            flops=2 * half * width * rows * n_dp * n_seq,
            bytes_accessed=2 * n_dp * n_seq * rows * width,
        )
    with jax.named_scope("sum_gradient"):
        kept = partial[SUMS.index(0)]
        partial = [
            move(part, lambda d, e, s, hop=hop: (d ^ e, e ^ hop, s))
            for hop, part in zip(SUMS, partial)
        ]
    with jax.named_scope("send_home"):
        homes = [
            move(piece, lambda d, e, s, hop=hop: (d ^ hop, e, s)) if hop else piece
            for hop, piece in zip(RETURNS, pieces)
        ]
    with jax.named_scope("project"):
        layer_out = call(
            project_kernel,
            bf16((rows, width)),
            *homes,
            residual,
            out_weight,
            scratch=[pltpu.VMEM((width, rows), jnp.bfloat16)],
            flops=2 * rows * width * width,
            bytes_accessed=2 * width * width,
        )
    with jax.named_scope("add_gradient"):
        grad_weight = call(
            add_kernel,
            jax.ShapeDtypeStruct((half, block), jnp.float32),
            kept,
            *partial,
            bytes_accessed=4 * half * block * 4,
        )
    return (layer_out, grad_weight)


def attend_groups(query_group, key_group, value_group, image_ids):
    items, slot_count, group_width = query_group.shape
    group_heads = HEADS // 2
    head_width = group_width // group_heads
    scale = 1.0 / math.sqrt(head_width)
    position = jnp.arange(slot_count)
    image_ids = jnp.where(image_ids < 0, -1 - position[None, :], image_ids)
    shaped_query = query_group.reshape(items, slot_count, group_heads, head_width)
    shaped_key = key_group.reshape(items, slot_count, group_heads, head_width)
    shaped_value = value_group.reshape(items, slot_count, group_heads, head_width)
    scores = (
        jnp.einsum("gqhd,gkhd->ghqk", shaped_query, shaped_key, preferred_element_type=jnp.float32)
        * scale
    )
    same_image = image_ids[:, None, :, None] == image_ids[:, None, None, :]
    scores = jnp.where(same_image, scores, -1e30)
    highest = jnp.max(scores, axis=-1, keepdims=True)
    weights = jnp.exp(scores - highest)
    probs = (weights / jnp.sum(weights, axis=-1, keepdims=True)).astype(jnp.bfloat16)
    mixed = jnp.einsum("ghqk,gkhd->gqhd", probs, shaped_value, preferred_element_type=jnp.float32)
    return mixed.reshape(items, slot_count, group_width).astype(jnp.bfloat16)


def routed_body(
    queries, key_vectors, value_vectors, residual, out_weight, cotangent, send_row, image_id
):
    row_count, full_width = queries.shape
    half_width = full_width // 2
    is_live = send_row < row_count
    source_row = jnp.minimum(send_row, row_count - 1)

    def arrange(data):
        grouped = data.reshape(row_count, 2, half_width).transpose(1, 0, 2)
        return jnp.where(is_live[None, :, None], grouped[:, source_row], jnp.zeros((), data.dtype))

    send_query = arrange(queries)
    send_key = arrange(key_vectors)
    send_value = arrange(value_vectors)
    send_image = jnp.where(is_live, image_id[source_row], -1)
    send_image = jnp.broadcast_to(send_image[None, :], (2, send_row.shape[0]))
    received = (
        lax.all_to_all(send_query, "enc", split_axis=1, concat_axis=1, tiled=True),
        lax.all_to_all(send_key, "enc", split_axis=1, concat_axis=1, tiled=True),
        lax.all_to_all(send_value, "enc", split_axis=1, concat_axis=1, tiled=True),
        lax.all_to_all(send_image, "enc", split_axis=1, concat_axis=1, tiled=True),
    )
    output = attend_groups(received[0], received[1], received[2], received[3])
    returned = lax.all_to_all(output, "enc", split_axis=1, concat_axis=1, tiled=True)
    holder = jnp.zeros((2, row_count + 1, half_width), jnp.bfloat16).at[:, send_row].set(returned)
    attended = holder[:, :row_count].transpose(1, 0, 2).reshape(row_count, full_width)
    projected = jnp.dot(attended, out_weight, preferred_element_type=jnp.float32)
    layer_out = (residual.astype(jnp.float32) + projected).astype(jnp.bfloat16)
    first_sum = lax.psum_scatter(
        lax.dot_general(
            attended, cotangent, (((0,), (0,)), ((), ())), preferred_element_type=jnp.float32
        ).astype(jnp.bfloat16),
        "dp",
        scatter_dimension=0,
        tiled=True,
    )
    second_sum = lax.psum_scatter(first_sum, "seq", scatter_dimension=0, tiled=True).astype(
        jnp.float32
    )
    grad_weight = lax.psum_scatter(second_sum, "enc", scatter_dimension=1, tiled=True)
    return (layer_out, grad_weight)


def solution(mesh):
    sizes = tuple(mesh.shape[name] for name in AXES)
    n_dp, n_enc, n_seq = sizes
    fits = n_seq == 2 and n_dp == n_enc == 4 and HEADS % (2 * n_enc) == 0
    body = functools.partial(exchange_body, sizes) if fits else routed_body
    placed = (
        P(("dp", "enc", "seq"), None),
        P(("dp", "enc", "seq"), None),
        P(("dp", "enc", "seq"), None),
        P(("dp", "enc", "seq"), None),
        P(),
        P(("dp", "enc", "seq"), None),
        P(("dp", "enc", "seq")),
        P(("dp", "enc", "seq")),
    )
    return jax.shard_map(
        body,
        mesh=mesh,
        in_specs=placed,
        out_specs=(P(("dp", "enc", "seq"), None), P(("dp", "seq"), "enc")),
        check_vma=False,
    )
```

```python
import functools
import math

import jax
import jax.numpy as jnp
from jax import lax
from jax.experimental import pallas as pl
from jax.experimental.pallas import tpu as pltpu
from jax.sharding import PartitionSpec as P

HEADS = 16
AXES = ("dp", "enc", "seq")
ID_ROWS = 16
ID_BASE = 64
SENDS = (3, 0, 1, 2)
RETURNS = (2, 3, 1, 0)
SUMS = (2, 3, 0, 1)


def call(
    kernel,
    out_shape,
    *args,
    spaces=None,
    scratch=(),
    limit=16,
    flops=0,
    bytes_accessed=0,
):
    def placed(space):
        return pl.BlockSpec(memory_space=space)

    many = isinstance(out_shape, (list, tuple))
    spaces = spaces or [pltpu.VMEM] * len(args)
    args = [
        pltpu.with_memory_space_constraint(arg, pltpu.HBM) if space == pltpu.HBM else arg
        for arg, space in zip(args, spaces)
    ]
    return pl.pallas_call(
        kernel,
        out_shape=out_shape,
        in_specs=[placed(space) for space in spaces],
        out_specs=[placed(pltpu.VMEM)] * len(out_shape) if many else placed(pltpu.VMEM),
        scratch_shapes=list(scratch),
        compiler_params=pltpu.CompilerParams(vmem_limit_bytes=limit * 1024 * 1024),
        cost_estimate=pl.CostEstimate(
            flops=flops, bytes_accessed=bytes_accessed, transcendentals=0
        ),
    )(*args)


def pack_kernel(block, *refs):
    sources, outs, (ready, held, arrived, ids_held, sems) = refs[:5], refs[5:-5], refs[-5:]
    targets = [ids_held] + [arrived.at[which] for which in range(3)] + [ready]
    copies = [
        pltpu.make_async_copy(source, target, sems.at[which])
        for which, (source, target) in enumerate(zip(sources, targets))
    ]
    for copy in copies:
        copy.start()
    first = lax.axis_index("dp") ^ lax.axis_index("enc")
    copies[0].wait()
    ids = ids_held[...]
    row = lax.broadcasted_iota(jnp.int32, (ID_ROWS, ids.shape[1]), 0)
    digits = jnp.where(row == 0, ids // ID_BASE, jnp.where(row == 1, ids % ID_BASE, 0))
    digits = digits.astype(jnp.float32).astype(jnp.bfloat16)
    for out in outs:
        out[3 * block :] = digits
    for which in range(3):
        copies[1 + which].wait()
        held[...] = arrived[which].T
        for hop, out in zip(SENDS, outs):
            begin = pl.multiple_of((first ^ hop) * block, 16)
            out[which * block : (which + 1) * block] = held[pl.ds(begin, block)]
    copies[4].wait()


def identifiers(slabs, block):
    numbers = []
    for slab in slabs:
        digits = slab[3 * block : 3 * block + ID_ROWS].astype(jnp.float32)
        numbers.append(digits[0:1] * ID_BASE + digits[1:2])
    return numbers


def set_bias(bias, key_ids, query_ids):
    queries = jnp.concatenate(query_ids, axis=1)
    for index, ids in enumerate(key_ids):
        rows = ids.shape[1]
        column = jnp.broadcast_to(ids, (rows, rows)).T
        column = jnp.concatenate([column] * len(query_ids), axis=1)
        bias[index * rows : (index + 1) * rows] = jnp.where(column == queries, 0.0, -1e30)


def gather(slabs, which, block, head, head_width):
    begin = which * block + head * head_width
    return jnp.concatenate([slab[begin : begin + head_width] for slab in slabs], axis=1)


def weigh(key, query, bias):
    scores = lax.dot_general(
        key, query, (((0,), (0,)), ((), ())), preferred_element_type=jnp.float32
    )
    scores = scores + bias
    return scores, jnp.max(scores, axis=0, keepdims=True)


def attend_first_kernel(block, head_width, *refs):
    slabs, (mixed, highest, total, bias) = refs[:-4], refs[-4:]
    ids = identifiers(slabs, block)
    set_bias(bias, ids, ids)
    factor = math.log2(math.e) / math.sqrt(head_width)
    for head in range(block // head_width):
        query, key, value = (gather(slabs, which, block, head, head_width) for which in range(3))
        scores, top = weigh(key, query, bias[...])
        weights = jnp.exp2((scores - top) * factor)
        highest[head : head + 1] = top
        total[head : head + 1] = jnp.sum(weights, axis=0, keepdims=True)
        mixed[head * head_width : (head + 1) * head_width] = jnp.dot(
            value, weights.astype(jnp.bfloat16), preferred_element_type=jnp.float32
        )


def attend_more(early, late, state, bias, outs, first, head_width):
    mixed, highest, total = state
    block, rows = outs[0].shape
    columns = slice(first, first + len(early) * rows)
    set_bias(bias, identifiers([late], block), identifiers(early, block))
    factor = math.log2(math.e) / math.sqrt(head_width)
    for head in range(block // head_width):
        span = slice(head * head_width, (head + 1) * head_width)
        query = gather(early, 0, block, head, head_width)
        key, value = (gather([late], which, block, head, head_width) for which in (1, 2))
        scores, top = weigh(key, query, bias[...])
        before = highest[head : head + 1, columns]
        top = jnp.maximum(top, before)
        weights = jnp.exp2((scores - top) * factor)
        shrink = jnp.exp2((before - top) * factor)
        sums = total[head : head + 1, columns] * shrink
        sums = sums + jnp.sum(weights, axis=0, keepdims=True)
        result = mixed[span, columns] * shrink + jnp.dot(
            value, weights.astype(jnp.bfloat16), preferred_element_type=jnp.float32
        )
        result = (result / sums).astype(jnp.bfloat16)
        for index, out in enumerate(outs):
            out[span] = result[:, index * rows : (index + 1) * rows]


def attend_across_kernel(head_width, *refs):
    count = len(SENDS)
    slabs, state, (first, last, old_bias, bias) = refs[:count], refs[count:-4], refs[-4:]
    block = last.shape[0]
    ids = identifiers(slabs, block)
    set_bias(bias, ids, ids[-1:])
    factor = math.log2(math.e) / math.sqrt(head_width)
    for head in range(block // head_width):
        span = slice(head * head_width, (head + 1) * head_width)
        query = gather(slabs[-1:], 0, block, head, head_width)
        key, value = (gather(slabs, which, block, head, head_width) for which in (1, 2))
        scores, top = weigh(key, query, bias[...])
        weights = jnp.exp2((scores - top) * factor)
        sums = jnp.sum(weights, axis=0, keepdims=True)
        result = jnp.dot(value, weights.astype(jnp.bfloat16), preferred_element_type=jnp.float32)
        last[span] = (result / sums).astype(jnp.bfloat16)
    attend_more(slabs[:1], slabs[-1], state, old_bias, [first], 0, head_width)


def attend_rest_kernel(head_width, *refs):
    early, late, state, outs, bias = refs[:2], refs[2], refs[3:6], refs[6:8], refs[8]
    attend_more(early, late, state, bias, outs, late.shape[1], head_width)


def stack_kernel(count, *refs):
    sources, out, sems = refs[:count], refs[-2], refs[-1]
    copies = [
        pltpu.make_async_copy(source, out.at[index], sems.at[index])
        for index, source in enumerate(sources)
    ]
    for copy in copies:
        copy.start()
    for copy in copies:
        copy.wait()


def halve_kernel(*refs):
    pieces, (kept, given) = refs[:-2], refs[-2:]
    s = lax.axis_index("seq")
    half = kept.shape[1]
    for hop, piece in zip(RETURNS, pieces):
        kept[hop] = piece[pl.ds(pl.multiple_of(s * half, 16), half)]
        given[hop] = piece[pl.ds(pl.multiple_of((1 - s) * half, 16), half)]


def gradient_kernel(count, *refs):
    kept, given, same, others, *outs = refs
    e = lax.axis_index("enc")
    features, rows = [], []
    for step in range(count):
        features += [kept[step], given[step]]
        rows += [same[step], others[step]]
    total = jnp.dot(
        jnp.concatenate(features, axis=1),
        jnp.concatenate(rows, axis=0),
        preferred_element_type=jnp.float32,
    )
    width, short = total.shape[1] // count, total.shape[0] // 2
    for target in range(count):
        block = total[:, target * width : (target + 1) * width]
        folded = jnp.concatenate([block[:short], block[short:]], axis=1).astype(jnp.bfloat16)

        for index, out in enumerate(outs):

            @pl.when(e ^ target == SUMS[index])
            def _():
                out[...] = folded


def project_kernel(*refs):
    pieces, (residual, weight, out, attended) = refs[:-4], refs[-4:]
    first = lax.axis_index("dp") ^ lax.axis_index("enc")
    block = pieces[0].shape[0]
    for hop, piece in zip(RETURNS, pieces):
        attended[pl.ds(pl.multiple_of((first ^ hop) * block, 16), block)] = piece[...]
    projected = lax.dot_general(
        attended[...], weight[...], (((0,), (0,)), ((), ())), preferred_element_type=jnp.float32
    )
    out[...] = (residual[...].astype(jnp.float32) + projected).astype(jnp.bfloat16)


def add_kernel(kept, *refs):
    partial, out = refs[:-1], refs[-1]
    stays = lax.axis_index("enc") == 0
    total = jnp.where(stays, kept[...], partial[SUMS.index(0)][...]).astype(jnp.float32)
    for hop, ref in zip(SUMS, partial):
        if hop:
            total = total + ref[...].astype(jnp.float32)
    short, width = total.shape[0], out.shape[1]
    out[:short] = total[:, :width]
    out[short:] = total[:, width:]


def exchange_body(
    sizes, queries, key_vectors, value_vectors, residual, out_weight, cotangent, send_row, image_id
):
    n_dp, n_enc, n_seq = sizes
    rows, width = queries.shape
    block = width // n_enc
    half = block // n_seq
    head_width = width // HEADS
    group = n_enc * rows
    tall = 3 * block + ID_ROWS
    bf16 = functools.partial(jax.ShapeDtypeStruct, dtype=jnp.bfloat16)
    hbm = pltpu.HBM

    def move(data, partner):
        pairs = []
        for d in range(n_dp):
            for e in range(n_enc):
                for s in range(n_seq):
                    to_d, to_e, to_s = partner(d, e, s)
                    source = (d * n_enc + e) * n_seq + s
                    target = (to_d * n_enc + to_e) * n_seq + to_s
                    if source != target:
                        pairs.append((source, target))
        return lax.ppermute(data, AXES, pairs)

    def along_enc(pieces, hops):
        return [
            move(piece, lambda d, e, s, hop=hop: (d, e ^ hop, s)) if hop else piece
            for hop, piece in zip(hops, pieces)
        ]

    def along_seq(data):
        return move(data, lambda d, e, s: (d, e, s ^ 1))

    with jax.named_scope("pack"):
        outs = call(
            functools.partial(pack_kernel, block),
            [bf16((tall, rows))] * n_enc + [bf16((rows, width))],
            image_id.reshape(1, rows),
            queries,
            key_vectors,
            value_vectors,
            cotangent,
            spaces=[hbm] * 5,
            scratch=[
                pltpu.VMEM((width, rows), jnp.bfloat16),
                pltpu.VMEM((3, rows, width), jnp.bfloat16),
                pltpu.VMEM((1, rows), jnp.int32),
                pltpu.SemaphoreType.DMA((5,)),
            ],
            bytes_accessed=8 * rows * width * 2,
        )
        slabs, cotangent = outs[:-1], outs[-1]
    with jax.named_scope("exchange_heads"):
        slabs = along_enc(slabs, SENDS)
    with jax.named_scope("gather_cotangent"):
        same = [cotangent] + [
            move(cotangent, lambda d, e, s, k=k: (d ^ k, e, s)) for k in range(1, n_dp)
        ]
    with jax.named_scope("attention"):
        known = group - rows
        f32 = functools.partial(jax.ShapeDtypeStruct, dtype=jnp.float32)
        state = call(
            functools.partial(attend_first_kernel, block, head_width),
            [f32((block, known)), f32((8, known)), f32((8, known))],
            *slabs[:-1],
            scratch=[pltpu.VMEM((known, known), jnp.float32)],
            flops=55 * known * known * block,
            bytes_accessed=8 * group * block,
        )
        across = call(
            functools.partial(attend_across_kernel, head_width),
            [bf16((block, rows))] * 2,
            *slabs,
            *state,
            scratch=[pltpu.VMEM((rows, rows), jnp.float32), pltpu.VMEM((group, rows), jnp.float32)],
            flops=55 * rows * (rows + group) * block,
            bytes_accessed=8 * group * block,
        )
        rest = call(
            functools.partial(attend_rest_kernel, head_width),
            [bf16((block, rows))] * 2,
            *slabs[1:],
            *state,
            scratch=[pltpu.VMEM((rows, 2 * rows), jnp.float32)],
            flops=55 * rows * 2 * rows * block,
            bytes_accessed=8 * group * block,
        )
        pieces = dict(zip(SENDS, [across[0], *rest, across[1]]))
        pieces = [pieces[hop] for hop in RETURNS]
    with jax.named_scope("send_to_owner"):
        pieces = [
            move(piece, lambda d, e, s, hop=hop: (d ^ hop, e ^ hop, s)) if hop else piece
            for hop, piece in zip(RETURNS, pieces)
        ]
        kept, given = call(
            halve_kernel,
            [bf16((n_dp, half, rows))] * 2,
            *pieces,
            flops=400 * group * group * half,
        )
        given = along_seq(given)
    with jax.named_scope("swap_cotangent"):
        stacked = call(
            functools.partial(stack_kernel, n_dp),
            bf16((n_dp, rows, width)),
            *same,
            spaces=[pltpu.VMEM] * n_dp + [pl.ANY] * 0,
            scratch=[pltpu.SemaphoreType.DMA((n_dp,))],
            bytes_accessed=4 * n_dp * rows * width,
        )
    with jax.named_scope("gradient"):
        partial = call(
            functools.partial(gradient_kernel, n_enc),
            [bf16((half // 2, 2 * block))] * n_enc,
            kept,
            given,
            stacked,
            along_seq(stacked),
            flops=2 * half * width * rows * n_dp * n_seq,
            bytes_accessed=2 * n_dp * n_seq * rows * width,
        )
    with jax.named_scope("sum_gradient"):
        kept = partial[SUMS.index(0)]
        partial = [
            move(part, lambda d, e, s, hop=hop: (d ^ e, e ^ hop, s))
            for hop, part in zip(SUMS, partial)
        ]
    with jax.named_scope("send_home"):
        homes = [
            move(piece, lambda d, e, s, hop=hop: (d ^ hop, e, s)) if hop else piece
            for hop, piece in zip(RETURNS, pieces)
        ]
    with jax.named_scope("project"):
        layer_out = call(
            project_kernel,
            bf16((rows, width)),
            *homes,
            residual,
            out_weight,
            scratch=[pltpu.VMEM((width, rows), jnp.bfloat16)],
            flops=2 * rows * width * width,
            bytes_accessed=2 * width * width,
        )
    with jax.named_scope("add_gradient"):
        grad_weight = call(
            add_kernel,
            jax.ShapeDtypeStruct((half, block), jnp.float32),
            kept,
            *partial,
            bytes_accessed=4 * half * block * 4,
        )
    return (layer_out, grad_weight)


def attend_groups(query_group, key_group, value_group, image_ids):
    items, slot_count, group_width = query_group.shape
    group_heads = HEADS // 2
    head_width = group_width // group_heads
    scale = 1.0 / math.sqrt(head_width)
    position = jnp.arange(slot_count)
    image_ids = jnp.where(image_ids < 0, -1 - position[None, :], image_ids)
    shaped_query = query_group.reshape(items, slot_count, group_heads, head_width)
    shaped_key = key_group.reshape(items, slot_count, group_heads, head_width)
    shaped_value = value_group.reshape(items, slot_count, group_heads, head_width)
    scores = (
        jnp.einsum("gqhd,gkhd->ghqk", shaped_query, shaped_key, preferred_element_type=jnp.float32)
        * scale
    )
    same_image = image_ids[:, None, :, None] == image_ids[:, None, None, :]
    scores = jnp.where(same_image, scores, -1e30)
    highest = jnp.max(scores, axis=-1, keepdims=True)
    weights = jnp.exp(scores - highest)
    probs = (weights / jnp.sum(weights, axis=-1, keepdims=True)).astype(jnp.bfloat16)
    mixed = jnp.einsum("ghqk,gkhd->gqhd", probs, shaped_value, preferred_element_type=jnp.float32)
    return mixed.reshape(items, slot_count, group_width).astype(jnp.bfloat16)


def routed_body(
    queries, key_vectors, value_vectors, residual, out_weight, cotangent, send_row, image_id
):
    row_count, full_width = queries.shape
    half_width = full_width // 2
    is_live = send_row < row_count
    source_row = jnp.minimum(send_row, row_count - 1)

    def arrange(data):
        grouped = data.reshape(row_count, 2, half_width).transpose(1, 0, 2)
        return jnp.where(is_live[None, :, None], grouped[:, source_row], jnp.zeros((), data.dtype))

    send_query = arrange(queries)
    send_key = arrange(key_vectors)
    send_value = arrange(value_vectors)
    send_image = jnp.where(is_live, image_id[source_row], -1)
    send_image = jnp.broadcast_to(send_image[None, :], (2, send_row.shape[0]))
    received = (
        lax.all_to_all(send_query, "enc", split_axis=1, concat_axis=1, tiled=True),
        lax.all_to_all(send_key, "enc", split_axis=1, concat_axis=1, tiled=True),
        lax.all_to_all(send_value, "enc", split_axis=1, concat_axis=1, tiled=True),
        lax.all_to_all(send_image, "enc", split_axis=1, concat_axis=1, tiled=True),
    )
    output = attend_groups(received[0], received[1], received[2], received[3])
    returned = lax.all_to_all(output, "enc", split_axis=1, concat_axis=1, tiled=True)
    holder = jnp.zeros((2, row_count + 1, half_width), jnp.bfloat16).at[:, send_row].set(returned)
    attended = holder[:, :row_count].transpose(1, 0, 2).reshape(row_count, full_width)
    projected = jnp.dot(attended, out_weight, preferred_element_type=jnp.float32)
    layer_out = (residual.astype(jnp.float32) + projected).astype(jnp.bfloat16)
    first_sum = lax.psum_scatter(
        lax.dot_general(
            attended, cotangent, (((0,), (0,)), ((), ())), preferred_element_type=jnp.float32
        ).astype(jnp.bfloat16),
        "dp",
        scatter_dimension=0,
        tiled=True,
    )
    second_sum = lax.psum_scatter(first_sum, "seq", scatter_dimension=0, tiled=True).astype(
        jnp.float32
    )
    grad_weight = lax.psum_scatter(second_sum, "enc", scatter_dimension=1, tiled=True)
    return (layer_out, grad_weight)


def solution(mesh):
    sizes = tuple(mesh.shape[name] for name in AXES)
    n_dp, n_enc, n_seq = sizes
    fits = n_seq == 2 and n_dp == n_enc == 4 and HEADS % (2 * n_enc) == 0
    body = functools.partial(exchange_body, sizes) if fits else routed_body
    placed = (
        P(("dp", "enc", "seq"), None),
        P(("dp", "enc", "seq"), None),
        P(("dp", "enc", "seq"), None),
        P(("dp", "enc", "seq"), None),
        P(),
        P(("dp", "enc", "seq"), None),
        P(("dp", "enc", "seq")),
        P(("dp", "enc", "seq")),
    )
    return jax.shard_map(
        body,
        mesh=mesh,
        in_specs=placed,
        out_specs=(P(("dp", "enc", "seq"), None), P(("dp", "seq"), "enc")),
        check_vma=False,
    )
```

```python
import functools
import math

import jax
import jax.numpy as jnp
from jax import lax
from jax.experimental import pallas as pl
from jax.experimental.pallas import tpu as pltpu
from jax.sharding import PartitionSpec as P

HEADS = 16
AXES = ("dp", "enc", "seq")
ID_ROWS = 16
ID_BASE = 64
VMEM_LIMIT = 16 * 1024 * 1024
SENDS = (3, 0, 1, 2)
RETURNS = (2, 3, 1, 0)
SUMS = (2, 3, 1, 0)


def call(
    kernel,
    out_shape,
    *args,
    spaces=None,
    scratch=(),
    flops=0,
    bytes_accessed=0,
):
    def placed(space):
        return pl.BlockSpec(memory_space=space)

    many = isinstance(out_shape, (list, tuple))
    spaces = spaces or [pltpu.VMEM] * len(args)
    args = [
        pltpu.with_memory_space_constraint(arg, pltpu.HBM) if space == pltpu.HBM else arg
        for arg, space in zip(args, spaces)
    ]
    return pl.pallas_call(
        kernel,
        out_shape=out_shape,
        in_specs=[placed(space) for space in spaces],
        out_specs=[placed(pltpu.VMEM)] * len(out_shape) if many else placed(pltpu.VMEM),
        scratch_shapes=list(scratch),
        compiler_params=pltpu.CompilerParams(vmem_limit_bytes=VMEM_LIMIT),
        cost_estimate=pl.CostEstimate(
            flops=flops, bytes_accessed=bytes_accessed, transcendentals=0
        ),
    )(*args)


def pack_kernel(block, *refs):
    sources, outs, (ready, held, arrived, ids_held, sems) = refs[:5], refs[5:-5], refs[-5:]
    targets = [ids_held] + [arrived.at[which] for which in range(3)] + [ready]
    copies = [
        pltpu.make_async_copy(source, target, sems.at[which])
        for which, (source, target) in enumerate(zip(sources, targets))
    ]
    for copy in copies:
        copy.start()
    first = lax.axis_index("dp") ^ lax.axis_index("enc")
    copies[0].wait()
    ids = ids_held[...]
    row = lax.broadcasted_iota(jnp.int32, (ID_ROWS, ids.shape[1]), 0)
    digits = jnp.where(row == 0, ids // ID_BASE, jnp.where(row == 1, ids % ID_BASE, 0))
    digits = digits.astype(jnp.float32).astype(jnp.bfloat16)
    for out in outs:
        out[3 * block :] = digits
    for which in range(3):
        copies[1 + which].wait()
        held[...] = arrived[which].T
        for hop, out in zip(SENDS, outs):
            begin = pl.multiple_of((first ^ hop) * block, 16)
            out[which * block : (which + 1) * block] = held[pl.ds(begin, block)]
    copies[4].wait()


def identifiers(slabs, block):
    numbers = []
    for slab in slabs:
        digits = slab[3 * block : 3 * block + ID_ROWS].astype(jnp.float32)
        numbers.append(digits[0:1] * ID_BASE + digits[1:2])
    return numbers


def set_bias(bias, key_ids, query_ids):
    queries = jnp.concatenate(query_ids, axis=1)
    for index, ids in enumerate(key_ids):
        rows = ids.shape[1]
        column = jnp.broadcast_to(ids, (rows, rows)).T
        column = jnp.concatenate([column] * len(query_ids), axis=1)
        bias[index * rows : (index + 1) * rows] = jnp.where(column == queries, 0.0, -1e30)


def gather(slabs, which, block, head, head_width):
    begin = which * block + head * head_width
    return jnp.concatenate([slab[begin : begin + head_width] for slab in slabs], axis=1)


def weigh(key, query, bias):
    scores = lax.dot_general(
        key, query, (((0,), (0,)), ((), ())), preferred_element_type=jnp.float32
    )
    scores = scores + bias
    return scores, jnp.max(scores, axis=0, keepdims=True)


def attend_first_kernel(block, head_width, *refs):
    slabs, (mixed, highest, total, bias) = refs[:-4], refs[-4:]
    ids = identifiers(slabs, block)
    set_bias(bias, ids, ids)
    factor = math.log2(math.e) / math.sqrt(head_width)
    for head in range(block // head_width):
        query, key, value = (gather(slabs, which, block, head, head_width) for which in range(3))
        scores, top = weigh(key, query, bias[...])
        weights = jnp.exp2((scores - top) * factor)
        highest[head : head + 1] = top
        total[head : head + 1] = jnp.sum(weights, axis=0, keepdims=True)
        mixed[head * head_width : (head + 1) * head_width] = jnp.dot(
            value, weights.astype(jnp.bfloat16), preferred_element_type=jnp.float32
        )


def attend_more(early, late, state, bias, outs, first, head_width):
    mixed, highest, total = state
    block, rows = outs[0].shape
    columns = slice(first, first + len(early) * rows)
    set_bias(bias, identifiers([late], block), identifiers(early, block))
    factor = math.log2(math.e) / math.sqrt(head_width)
    for head in range(block // head_width):
        span = slice(head * head_width, (head + 1) * head_width)
        query = gather(early, 0, block, head, head_width)
        key, value = (gather([late], which, block, head, head_width) for which in (1, 2))
        scores, top = weigh(key, query, bias[...])
        before = highest[head : head + 1, columns]
        top = jnp.maximum(top, before)
        weights = jnp.exp2((scores - top) * factor)
        shrink = jnp.exp2((before - top) * factor)
        sums = total[head : head + 1, columns] * shrink
        sums = sums + jnp.sum(weights, axis=0, keepdims=True)
        result = mixed[span, columns] * shrink + jnp.dot(
            value, weights.astype(jnp.bfloat16), preferred_element_type=jnp.float32
        )
        result = (result / sums).astype(jnp.bfloat16)
        for index, out in enumerate(outs):
            out[span] = result[:, index * rows : (index + 1) * rows]


def attend_across_kernel(head_width, *refs):
    count = len(SENDS)
    slabs, state, (first, last, old_bias, bias) = refs[:count], refs[count:-4], refs[-4:]
    block = last.shape[0]
    ids = identifiers(slabs, block)
    set_bias(bias, ids, ids[-1:])
    factor = math.log2(math.e) / math.sqrt(head_width)
    for head in range(block // head_width):
        span = slice(head * head_width, (head + 1) * head_width)
        query = gather(slabs[-1:], 0, block, head, head_width)
        key, value = (gather(slabs, which, block, head, head_width) for which in (1, 2))
        scores, top = weigh(key, query, bias[...])
        weights = jnp.exp2((scores - top) * factor)
        sums = jnp.sum(weights, axis=0, keepdims=True)
        result = jnp.dot(value, weights.astype(jnp.bfloat16), preferred_element_type=jnp.float32)
        last[span] = (result / sums).astype(jnp.bfloat16)
    attend_more(slabs[:1], slabs[-1], state, old_bias, [first], 0, head_width)


def attend_rest_kernel(head_width, *refs):
    early, late, state, outs, bias = refs[:2], refs[2], refs[3:6], refs[6:8], refs[8]
    attend_more(early, late, state, bias, outs, late.shape[1], head_width)


def stack_kernel(*refs):
    sources, (out, sems) = refs[:-2], refs[-2:]
    copies = [
        pltpu.make_async_copy(source, out.at[index], sems.at[index])
        for index, source in enumerate(sources)
    ]
    for copy in copies:
        copy.start()
    for copy in copies:
        copy.wait()


def halve_kernel(*refs):
    pieces, (kept, given) = refs[:-2], refs[-2:]
    s = lax.axis_index("seq")
    half = kept.shape[1]
    for hop, piece in zip(RETURNS, pieces):
        kept[hop] = piece[pl.ds(pl.multiple_of(s * half, 16), half)]
        given[hop] = piece[pl.ds(pl.multiple_of((1 - s) * half, 16), half)]


def gradient_kernel(count, *refs):
    kept, given, same, others, *outs = refs
    e = lax.axis_index("enc")
    features, rows = [], []
    for step in range(count):
        features += [kept[step], given[step]]
        rows += [same[step], others[step]]
    total = jnp.dot(
        jnp.concatenate(features, axis=1),
        jnp.concatenate(rows, axis=0),
        preferred_element_type=jnp.float32,
    )
    width, short = total.shape[1] // count, total.shape[0] // 2
    for target in range(count):
        block = total[:, target * width : (target + 1) * width]
        folded = jnp.concatenate([block[:short], block[short:]], axis=1).astype(jnp.bfloat16)

        for index, out in enumerate(outs):

            @pl.when(e ^ target == SUMS[index])
            def _():
                out[...] = folded


def project_kernel(*refs):
    pieces, (residual, weight, out, attended) = refs[:-4], refs[-4:]
    first = lax.axis_index("dp") ^ lax.axis_index("enc")
    block = pieces[0].shape[0]
    for hop, piece in zip(RETURNS, pieces):
        attended[pl.ds(pl.multiple_of((first ^ hop) * block, 16), block)] = piece[...]
    projected = lax.dot_general(
        attended[...], weight[...], (((0,), (0,)), ((), ())), preferred_element_type=jnp.float32
    )
    out[...] = (residual[...].astype(jnp.float32) + projected).astype(jnp.bfloat16)


def add_kernel(*refs):
    partial, out = refs[:-1], refs[-1]
    total = partial[0][...].astype(jnp.float32)
    for ref in partial[1:]:
        total = total + ref[...].astype(jnp.float32)
    short, width = total.shape[0], out.shape[1]
    out[:short] = total[:, :width]
    out[short:] = total[:, width:]


def exchange_body(
    sizes, queries, key_vectors, value_vectors, residual, out_weight, cotangent, send_row, image_id
):
    n_dp, n_enc, n_seq = sizes
    rows, width = queries.shape
    block = width // n_enc
    half = block // n_seq
    head_width = width // HEADS
    group = n_enc * rows
    tall = 3 * block + ID_ROWS
    bf16 = functools.partial(jax.ShapeDtypeStruct, dtype=jnp.bfloat16)
    hbm = pltpu.HBM

    def move(data, partner):
        pairs = []
        for d in range(n_dp):
            for e in range(n_enc):
                for s in range(n_seq):
                    to_d, to_e, to_s = partner(d, e, s)
                    pairs.append(
                        ((d * n_enc + e) * n_seq + s, (to_d * n_enc + to_e) * n_seq + to_s)
                    )
        return lax.ppermute(data, AXES, pairs)

    def along_enc(pieces, hops):
        return [
            move(piece, lambda d, e, s, hop=hop: (d, e ^ hop, s)) if hop else piece
            for hop, piece in zip(hops, pieces)
        ]

    def along_seq(data):
        return move(data, lambda d, e, s: (d, e, s ^ 1))

    with jax.named_scope("pack"):
        outs = call(
            functools.partial(pack_kernel, block),
            [bf16((tall, rows))] * n_enc + [bf16((rows, width))],
            image_id.reshape(1, rows),
            queries,
            key_vectors,
            value_vectors,
            cotangent,
            spaces=[hbm] * 5,
            scratch=[
                pltpu.VMEM((width, rows), jnp.bfloat16),
                pltpu.VMEM((3, rows, width), jnp.bfloat16),
                pltpu.VMEM((1, rows), jnp.int32),
                pltpu.SemaphoreType.DMA((5,)),
            ],
            bytes_accessed=8 * rows * width * 2,
        )
        slabs, cotangent = outs[:-1], outs[-1]
    with jax.named_scope("exchange_heads"):
        slabs = along_enc(slabs, SENDS)
    with jax.named_scope("gather_cotangent"):
        same = [cotangent] + [
            move(cotangent, lambda d, e, s, k=k: (d ^ k, e, s)) for k in range(1, n_dp)
        ]
    with jax.named_scope("attention"):
        known = group - rows
        f32 = functools.partial(jax.ShapeDtypeStruct, dtype=jnp.float32)
        state = call(
            functools.partial(attend_first_kernel, block, head_width),
            [f32((block, known)), f32((8, known)), f32((8, known))],
            *slabs[:-1],
            scratch=[pltpu.VMEM((known, known), jnp.float32)],
            flops=55 * known * known * block,
            bytes_accessed=8 * group * block,
        )
        across = call(
            functools.partial(attend_across_kernel, head_width),
            [bf16((block, rows))] * 2,
            *slabs,
            *state,
            scratch=[pltpu.VMEM((rows, rows), jnp.float32), pltpu.VMEM((group, rows), jnp.float32)],
            flops=55 * rows * (rows + group) * block,
            bytes_accessed=8 * group * block,
        )
        rest = call(
            functools.partial(attend_rest_kernel, head_width),
            [bf16((block, rows))] * 2,
            *slabs[1:],
            *state,
            scratch=[pltpu.VMEM((rows, 2 * rows), jnp.float32)],
            flops=55 * rows * 2 * rows * block,
            bytes_accessed=8 * group * block,
        )
        pieces = dict(zip(SENDS, [across[0], *rest, across[1]]))
        pieces = [pieces[hop] for hop in RETURNS]
    with jax.named_scope("send_to_owner"):
        pieces = [
            move(piece, lambda d, e, s, hop=hop: (d ^ hop, e ^ hop, s)) if hop else piece
            for hop, piece in zip(RETURNS, pieces)
        ]
        kept, given = call(
            halve_kernel,
            [bf16((n_dp, half, rows))] * 2,
            *pieces,
            flops=400 * group * group * half,
        )
        given = along_seq(given)
    with jax.named_scope("swap_cotangent"):
        stacked = call(
            stack_kernel,
            bf16((n_dp, rows, width)),
            *same,
            scratch=[pltpu.SemaphoreType.DMA((n_dp,))],
            bytes_accessed=4 * n_dp * rows * width,
        )
    with jax.named_scope("gradient"):
        partial = call(
            functools.partial(gradient_kernel, n_enc),
            [bf16((half // 2, 2 * block))] * n_enc,
            kept,
            given,
            stacked,
            along_seq(stacked),
            flops=2 * half * width * rows * n_dp * n_seq,
            bytes_accessed=2 * n_dp * n_seq * rows * width,
        )
    with jax.named_scope("sum_gradient"):
        partial = [
            move(part, lambda d, e, s, hop=hop: (d ^ e, e ^ hop, s))
            for hop, part in zip(SUMS, partial)
        ]
    with jax.named_scope("send_home"):
        homes = [
            move(piece, lambda d, e, s, hop=hop: (d ^ hop, e, s)) if hop else piece
            for hop, piece in zip(RETURNS, pieces)
        ]
    with jax.named_scope("project"):
        layer_out = call(
            project_kernel,
            bf16((rows, width)),
            *homes,
            residual,
            out_weight,
            scratch=[pltpu.VMEM((width, rows), jnp.bfloat16)],
            flops=2 * rows * width * width,
            bytes_accessed=2 * width * width,
        )
    with jax.named_scope("add_gradient"):
        grad_weight = call(
            add_kernel,
            jax.ShapeDtypeStruct((half, block), jnp.float32),
            *partial,
            bytes_accessed=4 * half * block * 4,
        )
    return (layer_out, grad_weight)


def attend_groups(query_group, key_group, value_group, image_ids):
    items, slot_count, group_width = query_group.shape
    group_heads = HEADS // 2
    head_width = group_width // group_heads
    scale = 1.0 / math.sqrt(head_width)
    position = jnp.arange(slot_count)
    image_ids = jnp.where(image_ids < 0, -1 - position[None, :], image_ids)
    shaped_query = query_group.reshape(items, slot_count, group_heads, head_width)
    shaped_key = key_group.reshape(items, slot_count, group_heads, head_width)
    shaped_value = value_group.reshape(items, slot_count, group_heads, head_width)
    scores = (
        jnp.einsum("gqhd,gkhd->ghqk", shaped_query, shaped_key, preferred_element_type=jnp.float32)
        * scale
    )
    same_image = image_ids[:, None, :, None] == image_ids[:, None, None, :]
    scores = jnp.where(same_image, scores, -1e30)
    highest = jnp.max(scores, axis=-1, keepdims=True)
    weights = jnp.exp(scores - highest)
    probs = (weights / jnp.sum(weights, axis=-1, keepdims=True)).astype(jnp.bfloat16)
    mixed = jnp.einsum("ghqk,gkhd->gqhd", probs, shaped_value, preferred_element_type=jnp.float32)
    return mixed.reshape(items, slot_count, group_width).astype(jnp.bfloat16)


def routed_body(
    queries, key_vectors, value_vectors, residual, out_weight, cotangent, send_row, image_id
):
    row_count, full_width = queries.shape
    half_width = full_width // 2
    is_live = send_row < row_count
    source_row = jnp.minimum(send_row, row_count - 1)

    def arrange(data):
        grouped = data.reshape(row_count, 2, half_width).transpose(1, 0, 2)
        return jnp.where(is_live[None, :, None], grouped[:, source_row], jnp.zeros((), data.dtype))

    send_query = arrange(queries)
    send_key = arrange(key_vectors)
    send_value = arrange(value_vectors)
    send_image = jnp.where(is_live, image_id[source_row], -1)
    send_image = jnp.broadcast_to(send_image[None, :], (2, send_row.shape[0]))
    received = (
        lax.all_to_all(send_query, "enc", split_axis=1, concat_axis=1, tiled=True),
        lax.all_to_all(send_key, "enc", split_axis=1, concat_axis=1, tiled=True),
        lax.all_to_all(send_value, "enc", split_axis=1, concat_axis=1, tiled=True),
        lax.all_to_all(send_image, "enc", split_axis=1, concat_axis=1, tiled=True),
    )
    output = attend_groups(received[0], received[1], received[2], received[3])
    returned = lax.all_to_all(output, "enc", split_axis=1, concat_axis=1, tiled=True)
    holder = jnp.zeros((2, row_count + 1, half_width), jnp.bfloat16).at[:, send_row].set(returned)
    attended = holder[:, :row_count].transpose(1, 0, 2).reshape(row_count, full_width)
    projected = jnp.dot(attended, out_weight, preferred_element_type=jnp.float32)
    layer_out = (residual.astype(jnp.float32) + projected).astype(jnp.bfloat16)
    first_sum = lax.psum_scatter(
        lax.dot_general(
            attended, cotangent, (((0,), (0,)), ((), ())), preferred_element_type=jnp.float32
        ).astype(jnp.bfloat16),
        "dp",
        scatter_dimension=0,
        tiled=True,
    )
    second_sum = lax.psum_scatter(first_sum, "seq", scatter_dimension=0, tiled=True).astype(
        jnp.float32
    )
    grad_weight = lax.psum_scatter(second_sum, "enc", scatter_dimension=1, tiled=True)
    return (layer_out, grad_weight)


def solution(mesh):
    sizes = tuple(mesh.shape[name] for name in AXES)
    n_dp, n_enc, n_seq = sizes
    fits = n_seq == 2 and n_dp == n_enc == 4 and HEADS % (2 * n_enc) == 0
    body = functools.partial(exchange_body, sizes) if fits else routed_body
    placed = (
        P(("dp", "enc", "seq"), None),
        P(("dp", "enc", "seq"), None),
        P(("dp", "enc", "seq"), None),
        P(("dp", "enc", "seq"), None),
        P(),
        P(("dp", "enc", "seq"), None),
        P(("dp", "enc", "seq")),
        P(("dp", "enc", "seq")),
    )
    return jax.shard_map(
        body,
        mesh=mesh,
        in_specs=placed,
        out_specs=(P(("dp", "enc", "seq"), None), P(("dp", "seq"), "enc")),
        check_vma=False,
    )
```

```python
import functools
import math

import jax
import jax.numpy as jnp
from jax import lax
from jax.experimental import pallas as pl
from jax.experimental.pallas import tpu as pltpu
from jax.sharding import PartitionSpec as P

HEADS = 16
AXES = ("dp", "enc", "seq")
ID_ROWS = 16
ID_BASE = 64
SENDS = (3, 0, 1, 2)
RETURNS = (2, 3, 1, 0)
SUMS = (2, 3, 1)


def call(
    kernel,
    out_shape,
    *args,
    spaces=None,
    scratch=(),
    limit=16,
    flops=0,
    bytes_accessed=0,
):
    def placed(space):
        return pl.BlockSpec(memory_space=space)

    many = isinstance(out_shape, (list, tuple))
    spaces = spaces or [pltpu.VMEM] * len(args)
    args = [
        pltpu.with_memory_space_constraint(arg, pltpu.HBM) if space == pltpu.HBM else arg
        for arg, space in zip(args, spaces)
    ]
    return pl.pallas_call(
        kernel,
        out_shape=out_shape,
        in_specs=[placed(space) for space in spaces],
        out_specs=[placed(pltpu.VMEM)] * len(out_shape) if many else placed(pltpu.VMEM),
        scratch_shapes=list(scratch),
        compiler_params=pltpu.CompilerParams(vmem_limit_bytes=limit * 1024 * 1024),
        cost_estimate=pl.CostEstimate(
            flops=flops, bytes_accessed=bytes_accessed, transcendentals=0
        ),
    )(*args)


def pack_kernel(block, *refs):
    sources, outs, (ready, held, arrived, ids_held, sems) = refs[:5], refs[5:-5], refs[-5:]
    targets = [ids_held] + [arrived.at[which] for which in range(3)] + [ready]
    copies = [
        pltpu.make_async_copy(source, target, sems.at[which])
        for which, (source, target) in enumerate(zip(sources, targets))
    ]
    for copy in copies:
        copy.start()
    first = lax.axis_index("dp") ^ lax.axis_index("enc")
    copies[0].wait()
    ids = ids_held[...]
    row = lax.broadcasted_iota(jnp.int32, (ID_ROWS, ids.shape[1]), 0)
    digits = jnp.where(row == 0, ids // ID_BASE, jnp.where(row == 1, ids % ID_BASE, 0))
    digits = digits.astype(jnp.float32).astype(jnp.bfloat16)
    for out in outs:
        out[3 * block :] = digits
    for which in range(3):
        copies[1 + which].wait()
        held[...] = arrived[which].T
        for hop, out in zip(SENDS, outs):
            begin = pl.multiple_of((first ^ hop) * block, 16)
            out[which * block : (which + 1) * block] = held[pl.ds(begin, block)]
    copies[4].wait()


def identifiers(slabs, block):
    numbers = []
    for slab in slabs:
        digits = slab[3 * block : 3 * block + ID_ROWS].astype(jnp.float32)
        numbers.append(digits[0:1] * ID_BASE + digits[1:2])
    return numbers


def set_bias(bias, key_ids, query_ids):
    queries = jnp.concatenate(query_ids, axis=1)
    for index, ids in enumerate(key_ids):
        rows = ids.shape[1]
        column = jnp.broadcast_to(ids, (rows, rows)).T
        column = jnp.concatenate([column] * len(query_ids), axis=1)
        bias[index * rows : (index + 1) * rows] = jnp.where(column == queries, 0.0, -1e30)


def gather(slabs, which, block, head, head_width):
    begin = which * block + head * head_width
    return jnp.concatenate([slab[begin : begin + head_width] for slab in slabs], axis=1)


def weigh(key, query, bias):
    scores = lax.dot_general(
        key, query, (((0,), (0,)), ((), ())), preferred_element_type=jnp.float32
    )
    scores = scores + bias
    return scores, jnp.max(scores, axis=0, keepdims=True)


def attend_first_kernel(block, head_width, *refs):
    slabs, (mixed, highest, total, bias) = refs[:-4], refs[-4:]
    ids = identifiers(slabs, block)
    set_bias(bias, ids, ids)
    factor = math.log2(math.e) / math.sqrt(head_width)
    for head in range(block // head_width):
        query, key, value = (gather(slabs, which, block, head, head_width) for which in range(3))
        scores, top = weigh(key, query, bias[...])
        weights = jnp.exp2((scores - top) * factor)
        highest[head : head + 1] = top
        total[head : head + 1] = jnp.sum(weights, axis=0, keepdims=True)
        mixed[head * head_width : (head + 1) * head_width] = jnp.dot(
            value, weights.astype(jnp.bfloat16), preferred_element_type=jnp.float32
        )


def attend_more(early, late, state, bias, outs, first, head_width):
    mixed, highest, total = state
    block, rows = outs[0].shape
    columns = slice(first, first + len(early) * rows)
    set_bias(bias, identifiers([late], block), identifiers(early, block))
    factor = math.log2(math.e) / math.sqrt(head_width)
    for head in range(block // head_width):
        span = slice(head * head_width, (head + 1) * head_width)
        query = gather(early, 0, block, head, head_width)
        key, value = (gather([late], which, block, head, head_width) for which in (1, 2))
        scores, top = weigh(key, query, bias[...])
        before = highest[head : head + 1, columns]
        top = jnp.maximum(top, before)
        weights = jnp.exp2((scores - top) * factor)
        shrink = jnp.exp2((before - top) * factor)
        sums = total[head : head + 1, columns] * shrink
        sums = sums + jnp.sum(weights, axis=0, keepdims=True)
        result = mixed[span, columns] * shrink + jnp.dot(
            value, weights.astype(jnp.bfloat16), preferred_element_type=jnp.float32
        )
        result = (result / sums).astype(jnp.bfloat16)
        for index, out in enumerate(outs):
            out[span] = result[:, index * rows : (index + 1) * rows]


def attend_across_kernel(head_width, *refs):
    count = len(SENDS)
    slabs, state, (first, last, old_bias, bias) = refs[:count], refs[count:-4], refs[-4:]
    block = last.shape[0]
    ids = identifiers(slabs, block)
    set_bias(bias, ids, ids[-1:])
    factor = math.log2(math.e) / math.sqrt(head_width)
    for head in range(block // head_width):
        span = slice(head * head_width, (head + 1) * head_width)
        query = gather(slabs[-1:], 0, block, head, head_width)
        key, value = (gather(slabs, which, block, head, head_width) for which in (1, 2))
        scores, top = weigh(key, query, bias[...])
        weights = jnp.exp2((scores - top) * factor)
        sums = jnp.sum(weights, axis=0, keepdims=True)
        result = jnp.dot(value, weights.astype(jnp.bfloat16), preferred_element_type=jnp.float32)
        last[span] = (result / sums).astype(jnp.bfloat16)
    attend_more(slabs[:1], slabs[-1], state, old_bias, [first], 0, head_width)


def attend_rest_kernel(head_width, *refs):
    early, late, state, outs, bias = refs[:2], refs[2], refs[3:6], refs[6:8], refs[8]
    attend_more(early, late, state, bias, outs, late.shape[1], head_width)


def stack_kernel(count, *refs):
    sources, out, sems = refs[:count], refs[-2], refs[-1]
    copies = [
        pltpu.make_async_copy(source, out.at[index], sems.at[index])
        for index, source in enumerate(sources)
    ]
    for copy in copies:
        copy.start()
    for copy in copies:
        copy.wait()


def halve_kernel(*refs):
    count = len(RETURNS)
    pieces, homes, (kept, given) = refs[:count], refs[count : 2 * count], refs[2 * count :]
    e, s = lax.axis_index("enc"), lax.axis_index("seq")
    half = kept.shape[1]
    for hop, piece in zip(RETURNS, pieces):
        kept[e ^ hop] = piece[pl.ds(pl.multiple_of(s * half, 16), half)]
        given[e ^ hop] = piece[pl.ds(pl.multiple_of((1 - s) * half, 16), half)]
    for hop, piece in zip(RETURNS, pieces):
        for step, home in enumerate(homes):

            @pl.when(e ^ hop == step)
            def _():
                home[...] = piece[...]


def gradient_kernel(count, *refs):
    kept, given, same, others, own, *outs = refs
    e = lax.axis_index("enc")
    features, rows = [], []
    for step in range(count):
        features += [kept[step], given[step]]
        rows += [same[step], others[step]]
    total = jnp.dot(
        jnp.concatenate(features, axis=1),
        jnp.concatenate(rows, axis=0),
        preferred_element_type=jnp.float32,
    )
    width, short = total.shape[1] // count, total.shape[0] // 2
    for target in range(count):
        block = total[:, target * width : (target + 1) * width]
        folded = jnp.concatenate([block[:short], block[short:]], axis=1).astype(jnp.bfloat16)

        @pl.when(e == target)
        def _():
            own[...] = block

        for index, out in enumerate(outs):

            @pl.when(e ^ target == SUMS[index])
            def _():
                out[...] = folded


def project(pieces, steps, weight, attended):
    d = lax.axis_index("dp")
    block = pieces[0].shape[0]
    rows = []
    for index, (step, piece) in enumerate(zip(steps, pieces)):
        attended[index * block : (index + 1) * block] = piece[...]
        rows.append(weight[pl.ds(pl.multiple_of((d ^ step) * block, 16), block)])
    return lax.dot_general(
        attended[...],
        jnp.concatenate(rows, axis=0),
        (((0,), (0,)), ((), ())),
        preferred_element_type=jnp.float32,
    )


def project_kernel(residual, weight, *refs):
    pieces, (out, attended) = refs[:-2], refs[-2:]
    out[...] = residual[...].astype(jnp.float32) + project(
        pieces, range(len(pieces)), weight, attended
    )


def finish_kernel(count, early, *refs):
    partial, mine, pieces = refs[: count - 1], refs[count - 1], refs[count : 2 * count - early]
    projected, weight, out, grad, attended = refs[2 * count - early :]
    total = partial[0][...].astype(jnp.float32)
    for ref in partial[1:]:
        total = total + ref[...].astype(jnp.float32)
    short, width = total.shape[0], mine.shape[1]
    grad[:short] = mine[:short] + total[:, :width]
    grad[short:] = mine[short:] + total[:, width:]
    projected = projected[...] + project(pieces, range(early, count), weight, attended)
    out[...] = projected.astype(jnp.bfloat16)


def exchange_body(
    sizes, queries, key_vectors, value_vectors, residual, out_weight, cotangent, send_row, image_id
):
    n_dp, n_enc, n_seq = sizes
    rows, width = queries.shape
    block = width // n_enc
    half = block // n_seq
    head_width = width // HEADS
    group = n_enc * rows
    tall = 3 * block + ID_ROWS
    bf16 = functools.partial(jax.ShapeDtypeStruct, dtype=jnp.bfloat16)
    hbm = pltpu.HBM

    def move(data, partner):
        pairs = []
        for d in range(n_dp):
            for e in range(n_enc):
                for s in range(n_seq):
                    to_d, to_e, to_s = partner(d, e, s)
                    pairs.append(
                        ((d * n_enc + e) * n_seq + s, (to_d * n_enc + to_e) * n_seq + to_s)
                    )
        return lax.ppermute(data, AXES, pairs)

    def along_enc(pieces, hops):
        return [
            move(piece, lambda d, e, s, hop=hop: (d, e ^ hop, s)) if hop else piece
            for hop, piece in zip(hops, pieces)
        ]

    def along_seq(data):
        return move(data, lambda d, e, s: (d, e, s ^ 1))

    with jax.named_scope("pack"):
        outs = call(
            functools.partial(pack_kernel, block),
            [bf16((tall, rows))] * n_enc + [bf16((rows, width))],
            image_id.reshape(1, rows),
            queries,
            key_vectors,
            value_vectors,
            cotangent,
            spaces=[hbm] * 5,
            scratch=[
                pltpu.VMEM((width, rows), jnp.bfloat16),
                pltpu.VMEM((3, rows, width), jnp.bfloat16),
                pltpu.VMEM((1, rows), jnp.int32),
                pltpu.SemaphoreType.DMA((5,)),
            ],
            bytes_accessed=8 * rows * width * 2,
        )
        slabs, cotangent = outs[:-1], outs[-1]
    with jax.named_scope("exchange_heads"):
        slabs = along_enc(slabs, SENDS)
    with jax.named_scope("gather_cotangent"):
        same = [cotangent] + [
            move(cotangent, lambda d, e, s, k=k: (d ^ k, e, s)) for k in range(1, n_dp)
        ]
    with jax.named_scope("attention"):
        known = group - rows
        f32 = functools.partial(jax.ShapeDtypeStruct, dtype=jnp.float32)
        state = call(
            functools.partial(attend_first_kernel, block, head_width),
            [f32((block, known)), f32((8, known)), f32((8, known))],
            *slabs[:-1],
            scratch=[pltpu.VMEM((known, known), jnp.float32)],
            flops=55 * known * known * block,
            bytes_accessed=8 * group * block,
        )
        across = call(
            functools.partial(attend_across_kernel, head_width),
            [bf16((block, rows))] * 2,
            *slabs,
            *state,
            scratch=[pltpu.VMEM((rows, rows), jnp.float32), pltpu.VMEM((group, rows), jnp.float32)],
            flops=55 * rows * (rows + group) * block,
            bytes_accessed=8 * group * block,
        )
        rest = call(
            functools.partial(attend_rest_kernel, head_width),
            [bf16((block, rows))] * 2,
            *slabs[1:],
            *state,
            scratch=[pltpu.VMEM((rows, 2 * rows), jnp.float32)],
            flops=55 * rows * 2 * rows * block,
            bytes_accessed=8 * group * block,
        )
        pieces = dict(zip(SENDS, [across[0], *rest, across[1]]))
        pieces = [pieces[hop] for hop in RETURNS]
    with jax.named_scope("send_to_owner"):
        pieces = [
            move(piece, lambda d, e, s, hop=hop: (d ^ e, e ^ hop, s))
            for hop, piece in zip(RETURNS, pieces)
        ]
        *homes, kept, given = call(
            halve_kernel,
            [bf16((block, rows))] * n_dp + [bf16((n_dp, half, rows))] * 2,
            *pieces,
            flops=400 * group * group * half,
        )
        given = along_seq(given)
    with jax.named_scope("swap_cotangent"):
        stacked = call(
            functools.partial(stack_kernel, n_dp),
            bf16((n_dp, rows, width)),
            *same,
            spaces=[pltpu.VMEM] * n_dp + [pl.ANY] * 0,
            scratch=[pltpu.SemaphoreType.DMA((n_dp,))],
            bytes_accessed=4 * n_dp * rows * width,
        )
    with jax.named_scope("gradient"):
        mine, *partial = call(
            functools.partial(gradient_kernel, n_enc),
            [jax.ShapeDtypeStruct((half, block), jnp.float32)]
            + [bf16((half // 2, 2 * block))] * (n_enc - 1),
            kept,
            given,
            stacked,
            along_seq(stacked),
            flops=2 * half * width * rows * n_dp * n_seq,
            bytes_accessed=2 * n_dp * n_seq * rows * width,
        )
    with jax.named_scope("sum_gradient"):
        partial = along_enc(partial, SUMS)
    with jax.named_scope("send_home"):
        homes[1:] = [
            move(homes[k], lambda d, e, s, k=k: (d ^ k, e, s)) for k in range(1, n_dp)
        ]
    early = 2
    with jax.named_scope("project"):
        projected = call(
            project_kernel,
            jax.ShapeDtypeStruct((rows, width), jnp.float32),
            residual,
            out_weight,
            *homes[:early],
            scratch=[pltpu.VMEM((early * block, rows), jnp.bfloat16)],
            flops=2 * rows * early * block * width,
            bytes_accessed=2 * early * block * width,
        )
    with jax.named_scope("finish"):
        layer_out, grad_weight = call(
            functools.partial(finish_kernel, n_dp, early),
            [bf16((rows, width)), jax.ShapeDtypeStruct((half, block), jnp.float32)],
            *partial,
            mine,
            *homes[early:],
            projected,
            out_weight,
            scratch=[pltpu.VMEM(((n_dp - early) * block, rows), jnp.bfloat16)],
            flops=2 * rows * (n_dp - early) * block * width,
            bytes_accessed=2 * (n_dp - early) * block * width,
        )
    return (layer_out, grad_weight)


def attend_groups(query_group, key_group, value_group, image_ids):
    items, slot_count, group_width = query_group.shape
    group_heads = HEADS // 2
    head_width = group_width // group_heads
    scale = 1.0 / math.sqrt(head_width)
    position = jnp.arange(slot_count)
    image_ids = jnp.where(image_ids < 0, -1 - position[None, :], image_ids)
    shaped_query = query_group.reshape(items, slot_count, group_heads, head_width)
    shaped_key = key_group.reshape(items, slot_count, group_heads, head_width)
    shaped_value = value_group.reshape(items, slot_count, group_heads, head_width)
    scores = (
        jnp.einsum("gqhd,gkhd->ghqk", shaped_query, shaped_key, preferred_element_type=jnp.float32)
        * scale
    )
    same_image = image_ids[:, None, :, None] == image_ids[:, None, None, :]
    scores = jnp.where(same_image, scores, -1e30)
    highest = jnp.max(scores, axis=-1, keepdims=True)
    weights = jnp.exp(scores - highest)
    probs = (weights / jnp.sum(weights, axis=-1, keepdims=True)).astype(jnp.bfloat16)
    mixed = jnp.einsum("ghqk,gkhd->gqhd", probs, shaped_value, preferred_element_type=jnp.float32)
    return mixed.reshape(items, slot_count, group_width).astype(jnp.bfloat16)


def routed_body(
    queries, key_vectors, value_vectors, residual, out_weight, cotangent, send_row, image_id
):
    row_count, full_width = queries.shape
    half_width = full_width // 2
    is_live = send_row < row_count
    source_row = jnp.minimum(send_row, row_count - 1)

    def arrange(data):
        grouped = data.reshape(row_count, 2, half_width).transpose(1, 0, 2)
        return jnp.where(is_live[None, :, None], grouped[:, source_row], jnp.zeros((), data.dtype))

    send_query = arrange(queries)
    send_key = arrange(key_vectors)
    send_value = arrange(value_vectors)
    send_image = jnp.where(is_live, image_id[source_row], -1)
    send_image = jnp.broadcast_to(send_image[None, :], (2, send_row.shape[0]))
    received = (
        lax.all_to_all(send_query, "enc", split_axis=1, concat_axis=1, tiled=True),
        lax.all_to_all(send_key, "enc", split_axis=1, concat_axis=1, tiled=True),
        lax.all_to_all(send_value, "enc", split_axis=1, concat_axis=1, tiled=True),
        lax.all_to_all(send_image, "enc", split_axis=1, concat_axis=1, tiled=True),
    )
    output = attend_groups(received[0], received[1], received[2], received[3])
    returned = lax.all_to_all(output, "enc", split_axis=1, concat_axis=1, tiled=True)
    holder = jnp.zeros((2, row_count + 1, half_width), jnp.bfloat16).at[:, send_row].set(returned)
    attended = holder[:, :row_count].transpose(1, 0, 2).reshape(row_count, full_width)
    projected = jnp.dot(attended, out_weight, preferred_element_type=jnp.float32)
    layer_out = (residual.astype(jnp.float32) + projected).astype(jnp.bfloat16)
    first_sum = lax.psum_scatter(
        lax.dot_general(
            attended, cotangent, (((0,), (0,)), ((), ())), preferred_element_type=jnp.float32
        ).astype(jnp.bfloat16),
        "dp",
        scatter_dimension=0,
        tiled=True,
    )
    second_sum = lax.psum_scatter(first_sum, "seq", scatter_dimension=0, tiled=True).astype(
        jnp.float32
    )
    grad_weight = lax.psum_scatter(second_sum, "enc", scatter_dimension=1, tiled=True)
    return (layer_out, grad_weight)


def solution(mesh):
    sizes = tuple(mesh.shape[name] for name in AXES)
    n_dp, n_enc, n_seq = sizes
    fits = n_seq == 2 and n_dp == n_enc == 4 and HEADS % (2 * n_enc) == 0
    body = functools.partial(exchange_body, sizes) if fits else routed_body
    placed = (
        P(("dp", "enc", "seq"), None),
        P(("dp", "enc", "seq"), None),
        P(("dp", "enc", "seq"), None),
        P(("dp", "enc", "seq"), None),
        P(),
        P(("dp", "enc", "seq"), None),
        P(("dp", "enc", "seq")),
        P(("dp", "enc", "seq")),
    )
    return jax.shard_map(
        body,
        mesh=mesh,
        in_specs=placed,
        out_specs=(P(("dp", "enc", "seq"), None), P(("dp", "seq"), "enc")),
        check_vma=False,
    )
```

```python
import functools
import math

import jax
import jax.numpy as jnp
from jax import lax
from jax.experimental import pallas as pl
from jax.experimental.pallas import tpu as pltpu
from jax.sharding import PartitionSpec as P

HEADS = 16
AXES = ("dp", "enc", "seq")
ID_ROWS = 16
ID_BASE = 64
SENDS = (3, 0, 1, 2)
RETURNS = (2, 3, 1, 0)
SUMS = (2, 3, 1)


def call(
    kernel,
    out_shape,
    *args,
    spaces=None,
    scratch=(),
    limit=16,
    flops=0,
    bytes_accessed=0,
):
    def placed(space):
        return pl.BlockSpec(memory_space=space)

    many = isinstance(out_shape, (list, tuple))
    spaces = spaces or [pltpu.VMEM] * len(args)
    args = [
        pltpu.with_memory_space_constraint(arg, pltpu.HBM) if space == pltpu.HBM else arg
        for arg, space in zip(args, spaces)
    ]
    return pl.pallas_call(
        kernel,
        out_shape=out_shape,
        in_specs=[placed(space) for space in spaces],
        out_specs=[placed(pltpu.VMEM)] * len(out_shape) if many else placed(pltpu.VMEM),
        scratch_shapes=list(scratch),
        compiler_params=pltpu.CompilerParams(vmem_limit_bytes=limit * 1024 * 1024),
        cost_estimate=pl.CostEstimate(
            flops=flops, bytes_accessed=bytes_accessed, transcendentals=0
        ),
    )(*args)


def pack_kernel(block, *refs):
    sources, outs, (ready, held, arrived, ids_held, sems) = refs[:5], refs[5:-5], refs[-5:]
    targets = [ids_held] + [arrived.at[which] for which in range(3)] + [ready]
    copies = [
        pltpu.make_async_copy(source, target, sems.at[which])
        for which, (source, target) in enumerate(zip(sources, targets))
    ]
    for copy in copies:
        copy.start()
    first = lax.axis_index("dp") ^ lax.axis_index("enc")
    copies[0].wait()
    ids = ids_held[...]
    row = lax.broadcasted_iota(jnp.int32, (ID_ROWS, ids.shape[1]), 0)
    digits = jnp.where(row == 0, ids // ID_BASE, jnp.where(row == 1, ids % ID_BASE, 0))
    digits = digits.astype(jnp.float32).astype(jnp.bfloat16)
    for out in outs:
        out[3 * block :] = digits
    for which in range(3):
        copies[1 + which].wait()
        held[...] = arrived[which].T
        for hop, out in zip(SENDS, outs):
            begin = pl.multiple_of((first ^ hop) * block, 16)
            out[which * block : (which + 1) * block] = held[pl.ds(begin, block)]
    copies[4].wait()


def identifiers(slabs, block):
    numbers = []
    for slab in slabs:
        digits = slab[3 * block : 3 * block + ID_ROWS].astype(jnp.float32)
        numbers.append(digits[0:1] * ID_BASE + digits[1:2])
    return numbers


def set_bias(bias, key_ids, query_ids):
    queries = jnp.concatenate(query_ids, axis=1)
    for index, ids in enumerate(key_ids):
        rows = ids.shape[1]
        column = jnp.broadcast_to(ids, (rows, rows)).T
        column = jnp.concatenate([column] * len(query_ids), axis=1)
        bias[index * rows : (index + 1) * rows] = jnp.where(column == queries, 0.0, -1e30)


def gather(slabs, which, block, head, head_width):
    begin = which * block + head * head_width
    return jnp.concatenate([slab[begin : begin + head_width] for slab in slabs], axis=1)


def weigh(key, query, bias):
    scores = lax.dot_general(
        key, query, (((0,), (0,)), ((), ())), preferred_element_type=jnp.float32
    )
    scores = scores + bias
    return scores, jnp.max(scores, axis=0, keepdims=True)


def attend_first_kernel(block, head_width, *refs):
    slabs, (mixed, highest, total, bias) = refs[:-4], refs[-4:]
    ids = identifiers(slabs, block)
    set_bias(bias, ids, ids)
    factor = math.log2(math.e) / math.sqrt(head_width)
    for head in range(block // head_width):
        query, key, value = (gather(slabs, which, block, head, head_width) for which in range(3))
        scores, top = weigh(key, query, bias[...])
        weights = jnp.exp2((scores - top) * factor)
        highest[head : head + 1] = top
        total[head : head + 1] = jnp.sum(weights, axis=0, keepdims=True)
        mixed[head * head_width : (head + 1) * head_width] = jnp.dot(
            value, weights.astype(jnp.bfloat16), preferred_element_type=jnp.float32
        )


def attend_more(early, late, state, bias, outs, first, head_width):
    mixed, highest, total = state
    block, rows = outs[0].shape
    columns = slice(first, first + len(early) * rows)
    set_bias(bias, identifiers([late], block), identifiers(early, block))
    factor = math.log2(math.e) / math.sqrt(head_width)
    for head in range(block // head_width):
        span = slice(head * head_width, (head + 1) * head_width)
        query = gather(early, 0, block, head, head_width)
        key, value = (gather([late], which, block, head, head_width) for which in (1, 2))
        scores, top = weigh(key, query, bias[...])
        before = highest[head : head + 1, columns]
        top = jnp.maximum(top, before)
        weights = jnp.exp2((scores - top) * factor)
        shrink = jnp.exp2((before - top) * factor)
        sums = total[head : head + 1, columns] * shrink
        sums = sums + jnp.sum(weights, axis=0, keepdims=True)
        result = mixed[span, columns] * shrink + jnp.dot(
            value, weights.astype(jnp.bfloat16), preferred_element_type=jnp.float32
        )
        result = (result / sums).astype(jnp.bfloat16)
        for index, out in enumerate(outs):
            out[span] = result[:, index * rows : (index + 1) * rows]


def attend_across_kernel(head_width, *refs):
    count = len(SENDS)
    slabs, state, (first, last, old_bias, bias) = refs[:count], refs[count:-4], refs[-4:]
    block = last.shape[0]
    ids = identifiers(slabs, block)
    set_bias(bias, ids, ids[-1:])
    factor = math.log2(math.e) / math.sqrt(head_width)
    for head in range(block // head_width):
        span = slice(head * head_width, (head + 1) * head_width)
        query = gather(slabs[-1:], 0, block, head, head_width)
        key, value = (gather(slabs, which, block, head, head_width) for which in (1, 2))
        scores, top = weigh(key, query, bias[...])
        weights = jnp.exp2((scores - top) * factor)
        sums = jnp.sum(weights, axis=0, keepdims=True)
        result = jnp.dot(value, weights.astype(jnp.bfloat16), preferred_element_type=jnp.float32)
        last[span] = (result / sums).astype(jnp.bfloat16)
    attend_more(slabs[:1], slabs[-1], state, old_bias, [first], 0, head_width)


def attend_rest_kernel(head_width, *refs):
    early, late, state, outs, bias = refs[:2], refs[2], refs[3:6], refs[6:8], refs[8]
    attend_more(early, late, state, bias, outs, late.shape[1], head_width)


def stack_kernel(count, *refs):
    sources, out, sems = refs[:count], refs[-2], refs[-1]
    copies = [
        pltpu.make_async_copy(source, out.at[index], sems.at[index])
        for index, source in enumerate(sources)
    ]
    for copy in copies:
        copy.start()
    for copy in copies:
        copy.wait()


def halve_kernel(*refs):
    count = len(RETURNS)
    pieces, homes, (kept, given) = refs[:count], refs[count : 2 * count], refs[2 * count :]
    e, s = lax.axis_index("enc"), lax.axis_index("seq")
    half = kept.shape[1]
    for hop, piece in zip(RETURNS, pieces):
        kept[e ^ hop] = piece[pl.ds(pl.multiple_of(s * half, 16), half)]
        given[e ^ hop] = piece[pl.ds(pl.multiple_of((1 - s) * half, 16), half)]
    for hop, piece in zip(RETURNS, pieces):
        for step, home in enumerate(homes):

            @pl.when(e ^ hop == step)
            def _():
                home[...] = piece[...]


def gradient_kernel(count, *refs):
    kept, given, same, others, own, *outs = refs
    e = lax.axis_index("enc")
    features, rows = [], []
    for step in range(count):
        features += [kept[step], given[step]]
        rows += [same[step], others[step]]
    total = jnp.dot(
        jnp.concatenate(features, axis=1),
        jnp.concatenate(rows, axis=0),
        preferred_element_type=jnp.float32,
    )
    width, short = total.shape[1] // count, total.shape[0] // 2
    for target in range(count):
        block = total[:, target * width : (target + 1) * width]
        folded = jnp.concatenate([block[:short], block[short:]], axis=1).astype(jnp.bfloat16)

        @pl.when(e == target)
        def _():
            own[...] = block

        for index, out in enumerate(outs):

            @pl.when(e ^ target == SUMS[index])
            def _():
                out[...] = folded


def project(pieces, steps, weight, attended):
    d = lax.axis_index("dp")
    block = pieces[0].shape[0]
    rows = []
    for index, (step, piece) in enumerate(zip(steps, pieces)):
        attended[index * block : (index + 1) * block] = piece[...]
        rows.append(weight[pl.ds(pl.multiple_of((d ^ step) * block, 16), block)])
    return lax.dot_general(
        attended[...],
        jnp.concatenate(rows, axis=0),
        (((0,), (0,)), ((), ())),
        preferred_element_type=jnp.float32,
    )


def project_kernel(residual, weight, *refs):
    pieces, (out, attended) = refs[:-2], refs[-2:]
    out[...] = residual[...].astype(jnp.float32) + project(
        pieces, range(len(pieces)), weight, attended
    )


def finish_kernel(count, early, *refs):
    partial, mine, pieces = refs[: count - 1], refs[count - 1], refs[count : 2 * count - early]
    projected, weight, out, grad, attended = refs[2 * count - early :]
    total = partial[0][...].astype(jnp.float32)
    for ref in partial[1:]:
        total = total + ref[...].astype(jnp.float32)
    short, width = total.shape[0], mine.shape[1]
    grad[:short] = mine[:short] + total[:, :width]
    grad[short:] = mine[short:] + total[:, width:]
    projected = projected[...] + project(pieces, range(early, count), weight, attended)
    out[...] = projected.astype(jnp.bfloat16)


def exchange_body(
    sizes, queries, key_vectors, value_vectors, residual, out_weight, cotangent, send_row, image_id
):
    n_dp, n_enc, n_seq = sizes
    rows, width = queries.shape
    block = width // n_enc
    half = block // n_seq
    head_width = width // HEADS
    group = n_enc * rows
    tall = 3 * block + ID_ROWS
    bf16 = functools.partial(jax.ShapeDtypeStruct, dtype=jnp.bfloat16)
    hbm = pltpu.HBM

    def move(data, partner):
        pairs = []
        for d in range(n_dp):
            for e in range(n_enc):
                for s in range(n_seq):
                    to_d, to_e, to_s = partner(d, e, s)
                    pairs.append(
                        ((d * n_enc + e) * n_seq + s, (to_d * n_enc + to_e) * n_seq + to_s)
                    )
        return lax.ppermute(data, AXES, pairs)

    def along_enc(pieces, hops):
        return [
            move(piece, lambda d, e, s, hop=hop: (d, e ^ hop, s)) if hop else piece
            for hop, piece in zip(hops, pieces)
        ]

    def along_seq(data):
        return move(data, lambda d, e, s: (d, e, s ^ 1))

    with jax.named_scope("pack"):
        outs = call(
            functools.partial(pack_kernel, block),
            [bf16((tall, rows))] * n_enc + [bf16((rows, width))],
            image_id.reshape(1, rows),
            queries,
            key_vectors,
            value_vectors,
            cotangent,
            spaces=[hbm] * 5,
            scratch=[
                pltpu.VMEM((width, rows), jnp.bfloat16),
                pltpu.VMEM((3, rows, width), jnp.bfloat16),
                pltpu.VMEM((1, rows), jnp.int32),
                pltpu.SemaphoreType.DMA((5,)),
            ],
            bytes_accessed=8 * rows * width * 2,
        )
        slabs, cotangent = outs[:-1], outs[-1]
    with jax.named_scope("exchange_heads"):
        slabs = along_enc(slabs, SENDS)
    with jax.named_scope("gather_cotangent"):
        same = [cotangent] + [
            move(cotangent, lambda d, e, s, k=k: (d ^ k, e, s)) for k in range(1, n_dp)
        ]
    with jax.named_scope("attention"):
        known = group - rows
        f32 = functools.partial(jax.ShapeDtypeStruct, dtype=jnp.float32)
        state = call(
            functools.partial(attend_first_kernel, block, head_width),
            [f32((block, known)), f32((8, known)), f32((8, known))],
            *slabs[:-1],
            scratch=[pltpu.VMEM((known, known), jnp.float32)],
            flops=55 * known * known * block,
            bytes_accessed=8 * group * block,
        )
        across = call(
            functools.partial(attend_across_kernel, head_width),
            [bf16((block, rows))] * 2,
            *slabs,
            *state,
            scratch=[pltpu.VMEM((rows, rows), jnp.float32), pltpu.VMEM((group, rows), jnp.float32)],
            flops=55 * rows * (rows + group) * block,
            bytes_accessed=8 * group * block,
        )
        rest = call(
            functools.partial(attend_rest_kernel, head_width),
            [bf16((block, rows))] * 2,
            *slabs[1:],
            *state,
            scratch=[pltpu.VMEM((rows, 2 * rows), jnp.float32)],
            flops=55 * rows * 2 * rows * block,
            bytes_accessed=8 * group * block,
        )
        pieces = dict(zip(SENDS, [across[0], *rest, across[1]]))
        pieces = [pieces[hop] for hop in RETURNS]
    with jax.named_scope("send_to_owner"):
        pieces = [
            move(piece, lambda d, e, s, hop=hop: (d ^ e, e ^ hop, s))
            for hop, piece in zip(RETURNS, pieces)
        ]
        *homes, kept, given = call(
            halve_kernel,
            [bf16((block, rows))] * n_dp + [bf16((n_dp, half, rows))] * 2,
            *pieces,
            flops=400 * group * group * half,
        )
        given = along_seq(given)
    with jax.named_scope("swap_cotangent"):
        stacked = call(
            functools.partial(stack_kernel, n_dp),
            bf16((n_dp, rows, width)),
            *same,
            spaces=[pltpu.VMEM] * n_dp + [pl.ANY] * 0,
            scratch=[pltpu.SemaphoreType.DMA((n_dp,))],
            bytes_accessed=4 * n_dp * rows * width,
        )
    with jax.named_scope("gradient"):
        mine, *partial = call(
            functools.partial(gradient_kernel, n_enc),
            [jax.ShapeDtypeStruct((half, block), jnp.float32)]
            + [bf16((half // 2, 2 * block))] * (n_enc - 1),
            kept,
            given,
            stacked,
            along_seq(stacked),
            flops=2 * half * width * rows * n_dp * n_seq,
            bytes_accessed=2 * n_dp * n_seq * rows * width,
        )
    with jax.named_scope("sum_gradient"):
        partial = along_enc(partial, SUMS)
    with jax.named_scope("send_home"):
        homes[1:] = [
            move(homes[k], lambda d, e, s, k=k: (d ^ k, e, s)) for k in range(1, n_dp)
        ]
    early = 3
    with jax.named_scope("project"):
        projected = call(
            project_kernel,
            jax.ShapeDtypeStruct((rows, width), jnp.float32),
            residual,
            out_weight,
            *homes[:early],
            scratch=[pltpu.VMEM((early * block, rows), jnp.bfloat16)],
            flops=2 * rows * early * block * width,
            bytes_accessed=2 * early * block * width,
        )
    with jax.named_scope("finish"):
        layer_out, grad_weight = call(
            functools.partial(finish_kernel, n_dp, early),
            [bf16((rows, width)), jax.ShapeDtypeStruct((half, block), jnp.float32)],
            *partial,
            mine,
            *homes[early:],
            projected,
            out_weight,
            scratch=[pltpu.VMEM(((n_dp - early) * block, rows), jnp.bfloat16)],
            flops=2 * rows * (n_dp - early) * block * width,
            bytes_accessed=2 * (n_dp - early) * block * width,
        )
    return (layer_out, grad_weight)


def attend_groups(query_group, key_group, value_group, image_ids):
    items, slot_count, group_width = query_group.shape
    group_heads = HEADS // 2
    head_width = group_width // group_heads
    scale = 1.0 / math.sqrt(head_width)
    position = jnp.arange(slot_count)
    image_ids = jnp.where(image_ids < 0, -1 - position[None, :], image_ids)
    shaped_query = query_group.reshape(items, slot_count, group_heads, head_width)
    shaped_key = key_group.reshape(items, slot_count, group_heads, head_width)
    shaped_value = value_group.reshape(items, slot_count, group_heads, head_width)
    scores = (
        jnp.einsum("gqhd,gkhd->ghqk", shaped_query, shaped_key, preferred_element_type=jnp.float32)
        * scale
    )
    same_image = image_ids[:, None, :, None] == image_ids[:, None, None, :]
    scores = jnp.where(same_image, scores, -1e30)
    highest = jnp.max(scores, axis=-1, keepdims=True)
    weights = jnp.exp(scores - highest)
    probs = (weights / jnp.sum(weights, axis=-1, keepdims=True)).astype(jnp.bfloat16)
    mixed = jnp.einsum("ghqk,gkhd->gqhd", probs, shaped_value, preferred_element_type=jnp.float32)
    return mixed.reshape(items, slot_count, group_width).astype(jnp.bfloat16)


def routed_body(
    queries, key_vectors, value_vectors, residual, out_weight, cotangent, send_row, image_id
):
    row_count, full_width = queries.shape
    half_width = full_width // 2
    is_live = send_row < row_count
    source_row = jnp.minimum(send_row, row_count - 1)

    def arrange(data):
        grouped = data.reshape(row_count, 2, half_width).transpose(1, 0, 2)
        return jnp.where(is_live[None, :, None], grouped[:, source_row], jnp.zeros((), data.dtype))

    send_query = arrange(queries)
    send_key = arrange(key_vectors)
    send_value = arrange(value_vectors)
    send_image = jnp.where(is_live, image_id[source_row], -1)
    send_image = jnp.broadcast_to(send_image[None, :], (2, send_row.shape[0]))
    received = (
        lax.all_to_all(send_query, "enc", split_axis=1, concat_axis=1, tiled=True),
        lax.all_to_all(send_key, "enc", split_axis=1, concat_axis=1, tiled=True),
        lax.all_to_all(send_value, "enc", split_axis=1, concat_axis=1, tiled=True),
        lax.all_to_all(send_image, "enc", split_axis=1, concat_axis=1, tiled=True),
    )
    output = attend_groups(received[0], received[1], received[2], received[3])
    returned = lax.all_to_all(output, "enc", split_axis=1, concat_axis=1, tiled=True)
    holder = jnp.zeros((2, row_count + 1, half_width), jnp.bfloat16).at[:, send_row].set(returned)
    attended = holder[:, :row_count].transpose(1, 0, 2).reshape(row_count, full_width)
    projected = jnp.dot(attended, out_weight, preferred_element_type=jnp.float32)
    layer_out = (residual.astype(jnp.float32) + projected).astype(jnp.bfloat16)
    first_sum = lax.psum_scatter(
        lax.dot_general(
            attended, cotangent, (((0,), (0,)), ((), ())), preferred_element_type=jnp.float32
        ).astype(jnp.bfloat16),
        "dp",
        scatter_dimension=0,
        tiled=True,
    )
    second_sum = lax.psum_scatter(first_sum, "seq", scatter_dimension=0, tiled=True).astype(
        jnp.float32
    )
    grad_weight = lax.psum_scatter(second_sum, "enc", scatter_dimension=1, tiled=True)
    return (layer_out, grad_weight)


def solution(mesh):
    sizes = tuple(mesh.shape[name] for name in AXES)
    n_dp, n_enc, n_seq = sizes
    fits = n_seq == 2 and n_dp == n_enc == 4 and HEADS % (2 * n_enc) == 0
    body = functools.partial(exchange_body, sizes) if fits else routed_body
    placed = (
        P(("dp", "enc", "seq"), None),
        P(("dp", "enc", "seq"), None),
        P(("dp", "enc", "seq"), None),
        P(("dp", "enc", "seq"), None),
        P(),
        P(("dp", "enc", "seq"), None),
        P(("dp", "enc", "seq")),
        P(("dp", "enc", "seq")),
    )
    return jax.shard_map(
        body,
        mesh=mesh,
        in_specs=placed,
        out_specs=(P(("dp", "enc", "seq"), None), P(("dp", "seq"), "enc")),
        check_vma=False,
    )
```
